32 devices in a mesh: section: 2 (over y), tp: 4 (over z), rep: 4 (over x, core).
Axes of the slice: x: 2, y: 2, z: 4, core: 2. Of those that a mesh axis runs over, the one named last changes fastest.
Arguments:
- prompt: bfloat16 [768, 2560], P('rep', 'tp'), parts along dimension 0, may hold values from -6 to 6
- block_sizes: int32 [32], P('rep'), parts along dimension 0, may hold values from 1 to 48, 192 in all
- w_query_down: bfloat16 [2, 2560, 768], P('section', None, 'tp'), may hold values from -0.125 to 0.125
- w_query: bfloat16 [2, 768, 2560], P('section', None, 'tp'), may hold values from -0.21875 to 0.21875
- w_latent: bfloat16 [2, 2560, 544], P('section', None, 'tp'), may hold values from -0.125 to 0.125
- w_keys: bfloat16 [2, 512, 2048], P('section', None, 'tp'), may hold values from -0.25 to 0.25
- w_values: bfloat16 [2, 512, 2048], P('section', None, 'tp'), may hold values from -0.25 to 0.25
- w_out: bfloat16 [2, 2048, 2560], P('section', 'tp'), may hold values from -1.5 to 1.5
Outputs:
- latent_cache: bfloat16 [2, 768, 544], P('section', ('rep', 'tp')), parts along dimension 1
- layer_ends: bfloat16 [2, 32, 2560], P('section', 'rep', 'tp'), parts along dimension 1
The draws below stay inside these ranges and needn't reach their ends.
There are 4 independent parts, one for each index of `rep`. The reference program is written for one: setup_inputs(seed, part) draws one part's arguments, and reference() takes and returns one part's arrays. A program takes and returns all parts, laid end to end along the dimension named above; an argument that names none is the same for every part. Nothing has to cross between parts.
Inputs may be any that keep to these rules, and one draw needn't show every extreme that they name: `block_sizes`: the block sizes sum to 192, and the largest is exactly 48.
All inputs are finite; a program needn't handle non-finite values.
Results may differ from the reference program's by a relative error of at most 0.017.
Values may be sent and summed in bfloat16 or wider, within the bound.
No kernel may reach another device: no remote copies, remote signals or barrier semaphores. Data moves between devices by JAX's collectives and lax.ppermute only.
A program may use at most 64 MiB of HBM per device.

```python
import math
import jax
import jax.numpy as jnp
import numpy as np
from jax import lax

TOKENS = 192
BLOCKS = 8
BLOCK_MOST = 48
HEADS_DEV = 4
HEADS = 16
MODEL = 2560
QUERY_RANK = 768
NOPE_DIM = 128
ROPE_DIM = 32
VALUE_DIM = 128
LATENT = 512
LAYERS = 2
N_TP = 4


def block_scale(own_key, dims, pieces, least, high):
    loudness = 1.0
    for position, blocks in pieces:
        draws = jax.random.uniform(jax.random.fold_in(jax.random.fold_in(own_key, 6), position), (blocks,), jnp.float32, least / len(pieces), high / len(pieces))
        loudness = loudness * jnp.repeat(jnp.exp(draws), dims[position] // blocks).reshape((-1,) + (1,) * (len(dims) - 1 - position))
    return loudness


def split_up(number_of, total, reach, lean):
    weights = [(1 << 20) // math.isqrt(standing ** lean) + 1 for standing in range(2, number_of + 1)]
    surplus, counts = total - reach - (number_of - 1), [1] * (number_of - 1)
    while surplus > 0:
        movable = [i for i in range(number_of - 1) if counts[i] < reach]
        pool, budget = sum([weights[i] for i in movable]), surplus
        for i in movable:
            more = min(reach - counts[i], max(1, budget * weights[i] // pool), surplus)
            counts[i] = counts[i] + more
            surplus = surplus - more
    return np.array([reach] + counts)


def uneven_parts(own_key, count, total, most, slope):
    if count == 2:
        one = jax.random.randint(own_key, (), max(1, total - most), min(most, total - 1) + 1)
        return jnp.stack([one, total - one])
    lengths = jnp.asarray(split_up(count, total, most, slope), jnp.int32)
    twos = (count - 1) // 2
    giver, sink = lengths[1:1 + 2 * twos:2], lengths[2:2 + 2 * twos:2]
    margin = jnp.minimum(giver - 1, most - sink)
    moved = jax.random.randint(jax.random.fold_in(own_key, 1), (twos,), 0, 1 << 20) % (margin + 1)
    lengths = lengths.at[1:1 + 2 * twos:2].set(giver - moved).at[2:2 + 2 * twos:2].set(sink + moved)
    return lengths[jax.random.permutation(jax.random.fold_in(own_key, 2), count)]


def normal_values(key, extent, deviation, bound, pieces=(), held_as=jnp.bfloat16):
    factor_of = block_scale(key, extent, pieces, -0.22, 0.18) if pieces else 1.0
    array = jax.random.normal(key, extent, jnp.float32) * deviation * factor_of
    return jnp.minimum(jnp.maximum(array, -bound), bound).astype(held_as)


def setup_inputs(seed: int = 0, part: int = 0) -> dict:
    seeds = jax.random.split(jax.random.key(seed), 9)
    part_splits = jax.random.split(jax.random.fold_in(seeds[8], part), 9)
    return {
        "prompt": normal_values(part_splits[0], (TOKENS, MODEL), 1.0, 6.0, ((1, 4),)),
        "block_sizes": uneven_parts(part_splits[1], BLOCKS, TOKENS, BLOCK_MOST, 1).astype(jnp.int32),
        "w_query_down": normal_values(seeds[2], (LAYERS, MODEL, QUERY_RANK), MODEL ** -0.5, 0.125, ((0, 2), (2, 4))),
        "w_query": normal_values(seeds[3], (LAYERS, QUERY_RANK, HEADS * (NOPE_DIM + ROPE_DIM)), QUERY_RANK ** -0.5, 0.21875, ((0, 2), (2, 4))),
        "w_latent": normal_values(seeds[4], (LAYERS, MODEL, LATENT + ROPE_DIM), MODEL ** -0.5, 0.125, ((0, 2), (2, 4))),
        "w_keys": normal_values(seeds[5], (LAYERS, LATENT, HEADS * NOPE_DIM), LATENT ** -0.5, 0.25, ((0, 2), (2, 4))),
        "w_values": normal_values(seeds[6], (LAYERS, LATENT, HEADS * VALUE_DIM), LATENT ** -0.5, 0.25, ((0, 2), (2, 4))),
        "w_out": normal_values(seeds[7], (LAYERS, HEADS * VALUE_DIM, MODEL), HEADS ** -0.5, 1.5, ((0, 2), (1, 4))),
    }


EPSILON = 1e-06

def rms_rows(values):
    return values * lax.rsqrt(lax.optimization_barrier(jnp.mean(values * values, axis=-1, keepdims=True)) + EPSILON)

def rotate(values, positions):
    half_width = values.shape[-1] // 2
    frequency = 10000.0 ** (-2.0 * jnp.arange(half_width, dtype=jnp.float32) / values.shape[-1])
    angles = positions.astype(jnp.float32)[:, None] * frequency[None, :]
    if values.ndim == 3:
        angles = angles[:, None, :]
    cosine = jnp.cos(angles)
    sine_part = jnp.sin(angles)
    first_half = values[..., :half_width]
    second = values[..., half_width:]
    return jnp.concatenate([first_half * cosine - second * sine_part, first_half * sine_part + second * cosine], axis=-1)

def one_layer(hidden, down_weight, query_weight, latent_weight, key_weight, value_weight, out_weight):
    row_count = hidden.shape[0]
    positions = jnp.arange(row_count, dtype=jnp.int32)
    normed = rms_rows(hidden.astype(jnp.float32)).astype(jnp.bfloat16)
    compressed = rms_rows(jnp.dot(normed, down_weight, preferred_element_type=jnp.float32)).astype(jnp.bfloat16)
    queries = jnp.dot(compressed, query_weight, preferred_element_type=jnp.float32).reshape(row_count, HEADS, NOPE_DIM + ROPE_DIM)
    queries = jnp.concatenate([queries[..., :NOPE_DIM], rotate(queries[..., NOPE_DIM:], positions)], axis=-1).astype(jnp.bfloat16)
    latent = jnp.dot(normed, latent_weight, preferred_element_type=jnp.float32)
    cache_rows = jnp.concatenate([rms_rows(latent[:, :LATENT]), rotate(latent[:, LATENT:], positions)], axis=-1).astype(jnp.bfloat16)
    key_nope = jnp.dot(cache_rows[:, :LATENT], key_weight, preferred_element_type=jnp.float32).astype(jnp.bfloat16).reshape(row_count, HEADS, NOPE_DIM)
    value_rows = jnp.dot(cache_rows[:, :LATENT], value_weight, preferred_element_type=jnp.float32).astype(jnp.bfloat16).reshape(row_count, HEADS, VALUE_DIM)
    visible = positions[:, None] >= positions[None, :]
    scale_factor = (NOPE_DIM + ROPE_DIM) ** (-0.5)
    rope_keys = cache_rows[:, LATENT:].astype(jnp.float32)

    def head_group(group_index):
        first_head = (group_index * HEADS_DEV).astype(jnp.int32)
        group_queries = lax.dynamic_slice_in_dim(queries, first_head, HEADS_DEV, 1).astype(jnp.float32)
        group_keys = lax.dynamic_slice_in_dim(key_nope, first_head, HEADS_DEV, 1).astype(jnp.float32)
        group_values = lax.dynamic_slice_in_dim(value_rows, first_head, HEADS_DEV, 1).astype(jnp.float32)
        scores = jnp.einsum('ihd,jhd->hij', group_queries[..., :NOPE_DIM], group_keys)
        scores = scores + jnp.einsum('ihr,jr->hij', group_queries[..., NOPE_DIM:], rope_keys)
        powered = jnp.where(visible[None], jnp.exp(scores * scale_factor), 0.0)
        attention = (powered / lax.optimization_barrier(jnp.sum(powered, axis=-1, keepdims=True))).astype(jnp.bfloat16)
        mixed_rows = jnp.einsum('hij,jhv->ihv', attention.astype(jnp.float32), group_values).astype(jnp.bfloat16)
        out_rows = lax.dynamic_slice_in_dim(out_weight, (first_head * VALUE_DIM).astype(jnp.int32), HEADS_DEV * VALUE_DIM, 0)
        return jnp.dot(mixed_rows.reshape(row_count, HEADS_DEV * VALUE_DIM), out_rows, preferred_element_type=jnp.float32).astype(jnp.bfloat16)
    partials = lax.map(head_group, jnp.arange(N_TP, dtype=jnp.int32))
    summed = lax.optimization_barrier(jnp.sum(partials.astype(jnp.float32), axis=0))
    return ((hidden.astype(jnp.float32) + summed).astype(jnp.bfloat16), cache_rows)

def reference(prompt, block_sizes, w_query_down, w_query, w_latent, w_keys, w_values, w_out):
    end_rows = (jnp.cumsum(block_sizes) - 1).astype(jnp.int32)
    hidden = prompt
    caches = []
    finals = []
    for layer_index in range(LAYERS):
        hidden, cache_rows = one_layer(hidden, w_query_down[layer_index], w_query[layer_index], w_latent[layer_index], w_keys[layer_index], w_values[layer_index], w_out[layer_index])
        caches.append(cache_rows)
        finals.append(jnp.take(hidden, end_rows, axis=0))
    return (jnp.stack(caches), jnp.stack(finals))
```

```python
import jax
import jax.numpy as jnp
from jax import lax
from jax.sharding import PartitionSpec as P

NOPE_DIM = 128
ROPE_DIM = 32
VALUE_DIM = 128
LATENT = 512
EPSILON = 1e-06
F32 = jnp.float32
BF16 = jnp.bfloat16


def rms_rows(values):
    return values * lax.rsqrt(jnp.mean(values * values, axis=-1, keepdims=True) + EPSILON)


def rotate(values, positions):
    half_width = values.shape[-1] // 2
    frequency = 10000.0 ** (-2.0 * jnp.arange(half_width, dtype=F32) / values.shape[-1])
    angles = positions.astype(F32)[:, None] * frequency[None, :]
    if values.ndim == 3:
        angles = angles[:, None, :]
    cosine = jnp.cos(angles)
    sine_part = jnp.sin(angles)
    first_half = values[..., :half_width]
    second = values[..., half_width:]
    return jnp.concatenate(
        [first_half * cosine - second * sine_part, first_half * sine_part + second * cosine],
        axis=-1,
    )


def dot(a, b):
    return jnp.dot(a, b, preferred_element_type=F32)


def local(prompt, block_sizes, w_query_down, w_query, w_latent, w_keys, w_values, w_out):
    sections = lax.axis_size("section")
    section_id = lax.axis_index("section")
    tp_id = lax.axis_index("tp")
    tp_count = lax.axis_size("tp")
    tokens, share_cols = prompt.shape
    share_rows = tokens // tp_count
    down_weight, query_weight, latent_weight = w_query_down[0], w_query[0], w_latent[0]
    key_weight, value_weight, out_weight = w_keys[0], w_values[0], w_out[0]
    down_cols, latent_cols = down_weight.shape[1], latent_weight.shape[1]
    head_count = query_weight.shape[1] // (NOPE_DIM + ROPE_DIM)
    scale_factor = (NOPE_DIM + ROPE_DIM) ** (-0.5)
    all_positions = jnp.arange(tokens, dtype=jnp.int32)
    end_rows = jnp.cumsum(block_sizes) - 1

    def shift(array, distance, routes):
        pairs = [
            (a * tp_count + i, b * tp_count + (i + distance) % tp_count)
            for a, b in routes
            for i in range(tp_count)
        ]
        return lax.ppermute(array, ("section", "tp"), pairs)

    def gather(array, where, axis):
        routes = [(s, s) for s in where]
        width = array.shape[axis]
        shape = list(array.shape)
        shape[axis] = width * tp_count
        whole = jnp.zeros(shape, array.dtype)
        for k in range(tp_count):
            piece = array if k == 0 else shift(array, k, routes)
            whole = lax.dynamic_update_slice_in_dim(
                whole, piece, lax.rem(tp_id - k + tp_count, tp_count) * width, axis
            )
        return whole

    def keys_and_values(cache):
        plain = cache[:, :LATENT]
        keys = dot(plain, key_weight).astype(BF16).reshape(tokens, head_count, NOPE_DIM)
        values = dot(plain, value_weight).astype(BF16).reshape(tokens, head_count, VALUE_DIM)
        return keys, values

    def attend(compressed, positions, cache):
        keys, values = keys_and_values(cache)
        rows = compressed.shape[0]
        queries = dot(compressed, query_weight).reshape(rows, head_count, NOPE_DIM + ROPE_DIM)
        queries = jnp.concatenate(
            [queries[..., :NOPE_DIM], rotate(queries[..., NOPE_DIM:], positions)], axis=-1
        ).astype(BF16)
        scores = jnp.einsum("ihd,jhd->hij", queries[..., :NOPE_DIM], keys, preferred_element_type=F32)
        scores = scores + jnp.einsum(
            "ihr,jr->hij", queries[..., NOPE_DIM:], cache[:, LATENT:], preferred_element_type=F32
        )
        visible = all_positions[None, :] <= positions[:, None]
        powered = jnp.where(visible[None], jnp.exp(scores * scale_factor), 0.0)
        attention = (powered / jnp.sum(powered, axis=-1, keepdims=True)).astype(BF16)
        mixed = jnp.einsum("hij,jhv->ihv", attention, values, preferred_element_type=F32)
        return dot(mixed.astype(BF16).reshape(rows, head_count * VALUE_DIM), out_weight)

    def layer(hidden, own_share, tick):
        normed = rms_rows(hidden.astype(F32)).astype(BF16)
        parts = jnp.concatenate(
            [dot(normed, down_weight).astype(BF16), dot(normed, latent_weight).astype(BF16)], axis=1
        )
        whole = gather(parts[None], [tick], 0).astype(F32)
        down = jnp.concatenate([whole[m, :, :down_cols] for m in range(tp_count)], axis=1)
        latent = jnp.concatenate([whole[m, :, down_cols:] for m in range(tp_count)], axis=1)
        compressed = rms_rows(down).astype(BF16)
        cache = jnp.concatenate(
            [rms_rows(latent[:, :LATENT]), rotate(latent[:, LATENT:], all_positions)], axis=-1
        ).astype(BF16)
        partial = attend(compressed, all_positions, cache)
        start = tp_id * share_cols
        mine = lax.dynamic_slice_in_dim(partial, start, share_cols, 1) + own_share.astype(F32)
        partial = lax.dynamic_update_slice_in_dim(partial, mine, start, 1).astype(BF16)
        return partial, cache

    def pass_on(partial, tick):
        ends = jnp.take(partial, end_rows, axis=0)
        total = 0.0
        for k in range(tp_count):
            first = lax.rem(tp_id + k, tp_count) * share_rows
            block = lax.dynamic_slice_in_dim(partial, first, share_rows, 0)
            block = jnp.concatenate([block, ends], axis=0)
            total = total + shift(block, k, [(tick, tick + 1)]).astype(F32)
        total = total.astype(BF16)
        return total[:share_rows], total[share_rows:]

    own_cache = jnp.zeros((share_rows, LATENT + ROPE_DIM), BF16)
    own_ends = jnp.zeros((block_sizes.shape[0], share_cols), BF16)
    last = sections - 1
    latent_whole = gather(latent_weight, range(1, sections), 1) if last else latent_weight
    hidden, own_share = gather(prompt, [0], 1), prompt
    for tick in range(last):
        partial, cache = layer(hidden, own_share, tick)
        mine = lax.dynamic_slice_in_dim(cache, tp_id * share_rows, share_rows, 0)
        own_cache = jnp.where(section_id == tick, mine, own_cache)
        rows, ends = pass_on(partial, tick)
        ends_share = lax.dynamic_slice_in_dim(ends, tp_id * share_cols, share_cols, 1)
        own_ends = jnp.where(section_id == tick, shift(ends_share, 0, [(tick + 1, tick)]), own_ends)
        if tick + 1 < last:
            hidden = gather(rows, [tick + 1], 0)
            own_share = lax.dynamic_slice_in_dim(hidden, tp_id * share_cols, share_cols, 1)

    row_positions = tp_id * share_rows + jnp.arange(share_rows, dtype=jnp.int32)
    latent = dot(rms_rows(rows.astype(F32)).astype(BF16), latent_whole)
    fresh = jnp.concatenate(
        [rms_rows(latent[:, :LATENT]), rotate(latent[:, LATENT:], row_positions)], axis=-1
    ).astype(BF16)
    own_cache = jnp.where(section_id == last, fresh, own_cache)
    down = dot(rms_rows(ends.astype(F32)).astype(BF16), down_weight).astype(BF16)
    down = jnp.pad(down, ((0, 0), (0, fresh.shape[1] - down_cols)))
    whole = gather(jnp.concatenate([fresh, down], axis=0)[None], [last], 0)
    cache = whole[:, :share_rows].reshape(tokens, LATENT + ROPE_DIM)
    down = jnp.concatenate([whole[m, share_rows:, :down_cols] for m in range(tp_count)], axis=1)
    compressed = rms_rows(down.astype(F32)).astype(BF16)
    partial = attend(compressed, end_rows, cache).astype(BF16)
    total = ends_share.astype(F32)
    for k in range(tp_count):
        start = lax.rem(tp_id + k, tp_count) * share_cols
        block = lax.dynamic_slice_in_dim(partial, start, share_cols, 1)
        total = total + (shift(block, k, [(last, last)]) if k else block).astype(F32)
    own_ends = jnp.where(section_id == last, total.astype(BF16), own_ends)
    return (own_cache[None], own_ends[None])


def solution(mesh):
    in_specs = (
        P("rep", "tp"),
        P("rep"),
        P("section", None, "tp"),
        P("section", None, "tp"),
        P("section", None, "tp"),
        P("section", None, "tp"),
        P("section", None, "tp"),
        P("section", "tp", None),
    )
    out_specs = (P("section", ("rep", "tp"), None), P("section", "rep", "tp"))
    return jax.shard_map(local, mesh=mesh, in_specs=in_specs, out_specs=out_specs, check_vma=False)
```

```python
import jax
import jax.numpy as jnp
from jax import lax
from jax.experimental import pallas as pl
from jax.experimental.pallas import tpu as pltpu
from jax.sharding import PartitionSpec as P

NOPE_DIM = 128
ROPE_DIM = 32
VALUE_DIM = 128
LATENT = 512
EPSILON = 1e-06
F32 = jnp.float32
BF16 = jnp.bfloat16


def rms_rows(values):
    return values * lax.rsqrt(jnp.mean(values * values, axis=-1, keepdims=True) + EPSILON)


def rotate(values, positions):
    half_width = values.shape[-1] // 2
    frequency = 10000.0 ** (-2.0 * jnp.arange(half_width, dtype=F32) / values.shape[-1])
    angles = positions.astype(F32)[:, None] * frequency[None, :]
    if values.ndim == 3:
        angles = angles[:, None, :]
    cosine = jnp.cos(angles)
    sine_part = jnp.sin(angles)
    first_half = values[..., :half_width]
    second = values[..., half_width:]
    return jnp.concatenate(
        [first_half * cosine - second * sine_part, first_half * sine_part + second * cosine],
        axis=-1,
    )


def dot(a, b):
    return jnp.dot(a, b, preferred_element_type=F32)


def local(prompt, block_sizes, w_query_down, w_query, w_latent, w_keys, w_values, w_out):
    sections = lax.axis_size("section")
    section_id = lax.axis_index("section")
    tp_id = lax.axis_index("tp")
    tp_count = lax.axis_size("tp")
    tokens, share_cols = prompt.shape
    share_rows = tokens // tp_count
    down_weight, query_weight, latent_weight = w_query_down[0], w_query[0], w_latent[0]
    key_weight, value_weight, out_weight = w_keys[0], w_values[0], w_out[0]
    down_cols, latent_cols = down_weight.shape[1], latent_weight.shape[1]
    head_count = query_weight.shape[1] // (NOPE_DIM + ROPE_DIM)
    scale_factor = (NOPE_DIM + ROPE_DIM) ** (-0.5)
    all_positions = jnp.arange(tokens, dtype=jnp.int32)
    end_rows = jnp.cumsum(block_sizes) - 1

    def shift(array, distance, routes):
        pairs = [
            (a * tp_count + i, b * tp_count + (i + distance) % tp_count)
            for a, b in routes
            for i in range(tp_count)
        ]
        return lax.ppermute(array, ("section", "tp"), pairs)

    def gather(array, where, axis):
        routes = [(s, s) for s in where]
        width = array.shape[axis]
        shape = list(array.shape)
        shape[axis] = width * tp_count
        whole = jnp.zeros(shape, array.dtype)
        for k in range(tp_count):
            piece = array if k == 0 else shift(array, k, routes)
            whole = lax.dynamic_update_slice_in_dim(
                whole, piece, lax.rem(tp_id - k + tp_count, tp_count) * width, axis
            )
        return whole

    def keys_and_values(cache):
        plain = cache[:, :LATENT]
        keys = dot(plain, key_weight).astype(BF16).reshape(tokens, head_count, NOPE_DIM)
        values = dot(plain, value_weight).astype(BF16).reshape(tokens, head_count, VALUE_DIM)
        return keys, values

    def attend(compressed, positions, cache):
        keys, values = keys_and_values(cache)
        rows = compressed.shape[0]
        queries = dot(compressed, query_weight).reshape(rows, head_count, NOPE_DIM + ROPE_DIM)
        queries = jnp.concatenate(
            [queries[..., :NOPE_DIM], rotate(queries[..., NOPE_DIM:], positions)], axis=-1
        ).astype(BF16)
        scores = jnp.einsum("ihd,jhd->hij", queries[..., :NOPE_DIM], keys, preferred_element_type=F32)
        scores = scores + jnp.einsum(
            "ihr,jr->hij", queries[..., NOPE_DIM:], cache[:, LATENT:], preferred_element_type=F32
        )
        visible = all_positions[None, :] <= positions[:, None]
        powered = jnp.where(visible[None], jnp.exp(scores * scale_factor), 0.0)
        attention = (powered / jnp.sum(powered, axis=-1, keepdims=True)).astype(BF16)
        mixed = jnp.einsum("hij,jhv->ihv", attention, values, preferred_element_type=F32)
        return dot(mixed.astype(BF16).reshape(rows, head_count * VALUE_DIM), out_weight)

    def layer(hidden, own_share, tick):
        normed = rms_rows(hidden.astype(F32)).astype(BF16)
        parts = jnp.concatenate(
            [dot(normed, down_weight).astype(BF16), dot(normed, latent_weight).astype(BF16)], axis=1
        )
        whole = gather(parts[None], [tick], 0).astype(F32)
        down = jnp.concatenate([whole[m, :, :down_cols] for m in range(tp_count)], axis=1)
        latent = jnp.concatenate([whole[m, :, down_cols:] for m in range(tp_count)], axis=1)
        compressed = rms_rows(down).astype(BF16)
        cache = jnp.concatenate(
            [rms_rows(latent[:, :LATENT]), rotate(latent[:, LATENT:], all_positions)], axis=-1
        ).astype(BF16)
        partial = attend(compressed, all_positions, cache)
        start = tp_id * share_cols
        mine = lax.dynamic_slice_in_dim(partial, start, share_cols, 1) + own_share.astype(F32)
        partial = lax.dynamic_update_slice_in_dim(partial, mine, start, 1).astype(BF16)
        return partial, cache

    def pass_on(partial, tick):
        ends = jnp.take(partial, end_rows, axis=0)
        total = 0.0
        for k in range(tp_count):
            first = lax.rem(tp_id + k, tp_count) * share_rows
            block = lax.dynamic_slice_in_dim(partial, first, share_rows, 0)
            block = jnp.concatenate([block, ends], axis=0)
            total = total + shift(block, k, [(tick, tick + 1)]).astype(F32)
        total = total.astype(BF16)
        return total[:share_rows], total[share_rows:]

    own_cache = jnp.zeros((share_rows, LATENT + ROPE_DIM), BF16)
    own_ends = jnp.zeros((block_sizes.shape[0], share_cols), BF16)
    last = sections - 1
    latent_whole = gather(latent_weight, range(1, sections), 1) if last else latent_weight
    hidden, own_share = gather(prompt, [0], 1), prompt
    for tick in range(last):
        partial, cache = layer(hidden, own_share, tick)
        mine = lax.dynamic_slice_in_dim(cache, tp_id * share_rows, share_rows, 0)
        own_cache = jnp.where(section_id == tick, mine, own_cache)
        rows, ends = pass_on(partial, tick)
        ends_share = lax.dynamic_slice_in_dim(ends, tp_id * share_cols, share_cols, 1)
        own_ends = jnp.where(section_id == tick, shift(ends_share, 0, [(tick + 1, tick)]), own_ends)
        if tick + 1 < last:
            hidden = gather(rows, [tick + 1], 0)
            own_share = lax.dynamic_slice_in_dim(hidden, tp_id * share_cols, share_cols, 1)

    row_positions = tp_id * share_rows + jnp.arange(share_rows, dtype=jnp.int32)
    latent = dot(rms_rows(rows.astype(F32)).astype(BF16), latent_whole)
    fresh = jnp.concatenate(
        [rms_rows(latent[:, :LATENT]), rotate(latent[:, LATENT:], row_positions)], axis=-1
    ).astype(BF16)
    own_cache = jnp.where(section_id == last, fresh, own_cache)
    down = dot(rms_rows(ends.astype(F32)).astype(BF16), down_weight).astype(BF16)
    down = jnp.pad(down, ((0, 0), (0, fresh.shape[1] - down_cols)))
    whole = gather(jnp.concatenate([fresh, down], axis=0)[None], [last], 0)
    cache = whole[:, :share_rows].reshape(tokens, LATENT + ROPE_DIM)
    down = jnp.concatenate([whole[m, share_rows:, :down_cols] for m in range(tp_count)], axis=1)
    compressed = rms_rows(down.astype(F32)).astype(BF16)
    partial = attend(compressed, end_rows, cache).astype(BF16)
    total = ends_share.astype(F32)
    for k in range(tp_count):
        start = lax.rem(tp_id + k, tp_count) * share_cols
        block = lax.dynamic_slice_in_dim(partial, start, share_cols, 1)
        total = total + (shift(block, k, [(last, last)]) if k else block).astype(F32)
    own_ends = jnp.where(section_id == last, total.astype(BF16), own_ends)
    return (own_cache[None], own_ends[None])


ROW_WIDTH = LATENT + ROPE_DIM
HEAD_WIDTH = NOPE_DIM + ROPE_DIM
SMEM = pl.BlockSpec(memory_space=pltpu.SMEM)
VMEM = pl.BlockSpec(memory_space=pltpu.VMEM)


def call(kernel, out_shape, args, scratch=(), flops=0):
    many = isinstance(out_shape, list)
    moved = sum(a.size * a.dtype.itemsize for a in args)
    return pl.pallas_call(
        kernel,
        out_shape=out_shape,
        in_specs=[SMEM] + [VMEM] * (len(args) - 1),
        out_specs=[VMEM] * len(out_shape) if many else VMEM,
        scratch_shapes=list(scratch),
        compiler_params=pltpu.CompilerParams(vmem_limit_bytes=40 * 2**20),
        cost_estimate=pl.CostEstimate(flops=flops, bytes_accessed=moved, transcendentals=0),
    )(*args)


def dot_t(a, b):
    return lax.dot_general(a, b, (((1,), (1,)), ((), ())), preferred_element_type=F32)


def unit(values):
    return lax.rsqrt(jnp.mean(values * values, axis=-1, keepdims=True) + EPSILON)


def turn(pair, cosine, sine):
    half = pair.shape[1] // 2
    a, b = pair[:, :half], pair[:, half:]
    return jnp.concatenate([a * cosine - b * sine, a * sine + b * cosine], axis=1)


def down_kernel(ids, own, one, two, three, w_down, w_latent, out):
    tp = ids[1]
    share = own.shape[1]
    squares, down, latent = 0.0, 0.0, 0.0
    for k, ref in enumerate((own, one, two, three)):
        rows = pl.ds(pl.multiple_of((tp ^ k) * share, share), share)
        piece = ref[...]
        wide = piece.astype(F32)
        squares = squares + jnp.sum(wide * wide, axis=1, keepdims=True)
        down = down + dot(piece, w_down[rows, :])
        latent = latent + dot(piece, w_latent[rows, :])
    scale = lax.rsqrt(squares / (4 * share) + EPSILON)
    out[...] = jnp.concatenate([down * scale, latent * scale], axis=1).astype(BF16)


def attend_rows(compressed, cache, seen, cosine, sine, w_query, w_keys, w_values):
    queries = dot(compressed, w_query[...])
    plain, turned = cache[:, :LATENT], cache[:, LATENT:]
    keys = dot(plain, w_keys[...]).astype(BF16)
    values = dot(plain, w_values[...]).astype(BF16)
    mixed = []
    for head in range(queries.shape[1] // HEAD_WIDTH):
        query = queries[:, head * HEAD_WIDTH : (head + 1) * HEAD_WIDTH]
        query = jnp.concatenate(
            [query[:, :NOPE_DIM], turn(query[:, NOPE_DIM:], cosine, sine)], axis=1
        ).astype(BF16)
        key = jnp.concatenate([keys[:, head * NOPE_DIM : (head + 1) * NOPE_DIM], turned], axis=1)
        scores = dot_t(query, key) * HEAD_WIDTH**-0.5
        powered = jnp.where(seen, jnp.exp(scores), 0.0)
        attention = (powered / jnp.sum(powered, axis=1, keepdims=True)).astype(BF16)
        mixed.append(dot(attention, values[:, head * VALUE_DIM : (head + 1) * VALUE_DIM]))
    return jnp.concatenate(mixed, axis=1).astype(BF16)


def layer_kernel(
    ids, ends, own, one, two, three, share, cosine, sine, w_query, w_keys, w_values, w_out,
    out0, out1, out2, out3, own_cache, stack, total, cached,
):
    tp = ids[1]
    tokens, width = share.shape
    block = tokens // 4
    down_cols = w_query.shape[0] // 4
    for k, ref in enumerate((own, one, two, three)):
        stack[k] = ref[...]
    pieces = [stack[tp ^ m].astype(F32) for m in range(4)]
    down = jnp.concatenate([p[:, :down_cols] for p in pieces], axis=1)
    latent = jnp.concatenate([p[:, down_cols:] for p in pieces], axis=1)
    compressed = (down * unit(down)).astype(BF16)
    plain = latent[:, :LATENT]
    cache = jnp.concatenate(
        [plain * unit(plain), turn(latent[:, LATENT:], cosine[...], sine[...])], axis=1
    ).astype(BF16)
    cached[...] = cache
    own_cache[...] = cached[pl.ds(pl.multiple_of(tp * block, block), block), :]
    seen = lax.broadcasted_iota(jnp.int32, (tokens, tokens), 0) >= lax.broadcasted_iota(
        jnp.int32, (tokens, tokens), 1
    )
    mixed = attend_rows(
        compressed, cache, seen, cosine[...], sine[...], w_query, w_keys, w_values
    )
    chosen = (
        lax.broadcasted_iota(jnp.int32, (ends.shape[0], tokens), 1) == ends[...]
    ).astype(BF16)
    rows = jnp.concatenate([mixed, dot(chosen, mixed).astype(BF16)], axis=0)
    total[...] = dot(rows, w_out[...])
    mine = pl.ds(pl.multiple_of(tp * width, 128), width)
    added = jnp.concatenate([share[...].astype(F32), dot(chosen, share[...])], axis=0)
    total[:, mine] += added
    last = total[tokens:, :]
    for k, out in enumerate((out0, out1, out2, out3)):
        part = total[pl.ds(pl.multiple_of((tp ^ k) * block, block), block), :]
        out[...] = jnp.concatenate([part, last], axis=0).astype(BF16)


def latent_kernel(
    ids, one, two, three, four, cosine, sine, quarter0, quarter1, quarter2, quarter3, w_down,
    out, own_ends, hidden,
):
    tp, rep = ids[1], ids[2]
    block = cosine.shape[0]
    width = own_ends.shape[1]
    rows = one[...].astype(F32) + two[...].astype(F32) + three[...].astype(F32) + four[...].astype(F32)
    narrow = rows.astype(BF16)
    rows = narrow.astype(F32)
    hidden[...] = rows
    scale = unit(rows)
    count = w_down.shape[1]
    parts = []
    for source in range(4):
        total = 0.0
        for step, quarter in enumerate((quarter0, quarter1, quarter2, quarter3)):
            columns = pl.ds(pl.multiple_of((rep ^ step) * width, 128), width)
            piece = hidden[0:block, columns].astype(BF16)
            total = total + dot_t(piece, quarter[source])
        parts.append(total)
    latent = jnp.concatenate(parts, axis=1) * scale[:block]
    plain = latent[:, :LATENT]
    fresh = jnp.concatenate(
        [plain * unit(plain), turn(latent[:, LATENT:], cosine[...], sine[...])], axis=1
    )
    down = dot(narrow[block:, :], w_down[...]) * scale[block:]
    down = jnp.concatenate([down, jnp.zeros((down.shape[0], ROW_WIDTH - count), F32)], axis=1)
    out[...] = jnp.concatenate([fresh, down], axis=0).astype(BF16)
    mine = pl.ds(pl.multiple_of(tp * width, 128), width)
    own_ends[...] = hidden[block:, mine].astype(BF16)


def ends_kernel(
    ids, ends, own, one, two, three, cosine, sine, w_query, w_keys, w_values, w_out,
    out0, out1, out2, out3, stack, total,
):
    tp = ids[1]
    count = ends.shape[0]
    block = own.shape[0] - count
    down_cols = w_query.shape[0] // 4
    width = out0.shape[1]
    for k, ref in enumerate((own, one, two, three)):
        stack[k] = ref[...].astype(F32)
    pieces = [stack[tp ^ m] for m in range(4)]
    cache = jnp.concatenate([p[:block] for p in pieces], axis=0).astype(BF16)
    down = jnp.concatenate([p[block:, :down_cols] for p in pieces], axis=1)
    compressed = (down * unit(down)).astype(BF16)
    seen = lax.broadcasted_iota(jnp.int32, (count, 4 * block), 1) <= ends[...]
    mixed = attend_rows(
        compressed, cache, seen, cosine[...], sine[...], w_query, w_keys, w_values
    )
    total[...] = dot(mixed, w_out[...])
    for k, out in enumerate((out0, out1, out2, out3)):
        columns = pl.ds(pl.multiple_of((tp ^ k) * width, 128), width)
        out[...] = total[:, columns].astype(BF16)


def local_two(prompt, block_sizes, w_query_down, w_query, w_latent, w_keys, w_values, w_out):
    section, tp, rep = (lax.axis_index(a) for a in ("section", "tp", "rep"))
    ids = jnp.stack([section, tp, rep]).astype(jnp.int32)
    tokens, share = prompt.shape
    block = tokens // 4
    count = block_sizes.shape[0]
    w_down, w_up, w_lat = w_query_down[0], w_query[0], w_latent[0]
    w_key, w_value, w_final = w_keys[0], w_values[0], w_out[0]
    down_cols, latent_cols = w_down.shape[1], w_lat.shape[1]
    model = 4 * share
    ends = (jnp.cumsum(block_sizes) - 1).astype(jnp.int32)[:, None]
    frequency = 10000.0 ** (-2.0 * jnp.arange(ROPE_DIM // 2, dtype=F32) / ROPE_DIM)

    def tables(positions):
        angles = positions.astype(F32) * frequency[None, :]
        return jnp.cos(angles), jnp.sin(angles)

    cosine, sine = tables(jnp.arange(tokens)[:, None])
    own_cosine, own_sine = tables(tp * block + jnp.arange(block)[:, None])
    end_cosine, end_sine = tables(ends)

    def within(array, k):
        pairs = [(s * 4 + i, s * 4 + (i ^ k)) for s in range(2) for i in range(4)]
        return lax.ppermute(array, ("section", "tp"), pairs)

    def onward(array, k):
        pairs = [(i, 4 + (i ^ k)) for i in range(4)] + [(4 + i, i) for i in range(4)]
        return lax.ppermute(array, ("section", "tp"), pairs)

    def over_rep(array, k):
        return lax.ppermute(array, "rep", [(i, i ^ k) for i in range(4)])

    quarter = lax.dynamic_slice_in_dim(w_lat, rep * share, share, 0).T
    quarter = jnp.pad(quarter, ((0, tokens - latent_cols), (0, 0)))
    sent = jnp.where(section == 0, prompt, quarter)
    shares = [sent] + [within(sent, k) for k in (1, 2, 3)]
    parts = call(
        down_kernel,
        jax.ShapeDtypeStruct((tokens, down_cols + latent_cols), BF16),
        [ids, *shares, w_down, w_lat],
        flops=2 * tokens * model * (down_cols + latent_cols),
    )
    pieces = [parts] + [within(parts, k) for k in (1, 2, 3)]

    ordered = jnp.stack([p[:latent_cols] for p in shares])
    ordered = jnp.stack([lax.dynamic_index_in_dim(ordered, tp ^ m, 0, False) for m in range(4)])
    across = over_rep(ordered, 2)
    both = jnp.stack([ordered, across])

    message = jax.ShapeDtypeStruct((block + count, model), BF16)
    *blocks, first_cache = call(
        layer_kernel,
        [message] * 4 + [jax.ShapeDtypeStruct((block, ROW_WIDTH), BF16)],
        [ids, ends, *pieces, prompt, cosine, sine, w_up, w_key, w_value, w_final],
        [
            pltpu.VMEM((4, tokens, down_cols + latent_cols), BF16),
            pltpu.VMEM((tokens + count, model), F32),
            pltpu.VMEM((tokens, ROW_WIDTH), BF16),
        ],
        flops=2 * tokens * (w_up.size + w_key.size + w_value.size + w_final.size),
    )
    arrived = [onward(blocks[k], k) for k in (3, 2, 1, 0)]
    near = over_rep(both, 1)
    quarters = [both[0], near[0], both[1], near[1]]
    fresh, ends_share = call(
        latent_kernel,
        [
            jax.ShapeDtypeStruct((block + count, ROW_WIDTH), BF16),
            jax.ShapeDtypeStruct((count, share), BF16),
        ],
        [ids, *arrived, own_cosine, own_sine, *quarters, w_down],
        [pltpu.VMEM((block + count, model), F32)],
        flops=2 * block * model * ROW_WIDTH,
    )
    pieces = [fresh] + [within(fresh, k) for k in (1, 2, 3)]
    first_ends = onward(ends_share, 0)
    outs = call(
        ends_kernel,
        [jax.ShapeDtypeStruct((count, share), BF16)] * 4,
        [ids, ends, *pieces, end_cosine, end_sine, w_up, w_key, w_value, w_final],
        [
            pltpu.VMEM((4, block + count, ROW_WIDTH), F32),
            pltpu.VMEM((count, model), F32),
        ],
        flops=2 * tokens * (w_key.size + w_value.size),
    )
    total = ends_share.astype(F32) + outs[0].astype(F32)
    for k in (1, 2, 3):
        total = total + within(outs[k], k).astype(F32)
    own_ends = jnp.where(section == 0, first_ends, total.astype(BF16))
    own_cache = jnp.where(section == 0, first_cache, fresh[:block])
    return (own_cache[None], own_ends[None])


def solution(mesh):
    sizes = [mesh.shape[a] for a in ("section", "tp", "rep")]
    body = local_two if sizes == [2, 4, 4] else local
    in_specs = (
        P("rep", "tp"),
        P("rep"),
        P("section", None, "tp"),
        P("section", None, "tp"),
        P("section", None, "tp"),
        P("section", None, "tp"),
        P("section", None, "tp"),
        P("section", "tp", None),
    )
    out_specs = (P("section", ("rep", "tp"), None), P("section", "rep", "tp"))
    return jax.shard_map(body, mesh=mesh, in_specs=in_specs, out_specs=out_specs, check_vma=False)
```

```python
import jax
import jax.numpy as jnp
import numpy as np
from jax import lax
from jax.experimental import pallas as pl
from jax.experimental.pallas import tpu as pltpu
from jax.sharding import PartitionSpec as P

NOPE_DIM = 128
ROPE_DIM = 32
VALUE_DIM = 128
LATENT = 512
EPSILON = 1e-06
F32 = jnp.float32
BF16 = jnp.bfloat16


def rms_rows(values):
    return values * lax.rsqrt(jnp.mean(values * values, axis=-1, keepdims=True) + EPSILON)


def rotate(values, positions):
    half_width = values.shape[-1] // 2
    frequency = 10000.0 ** (-2.0 * jnp.arange(half_width, dtype=F32) / values.shape[-1])
    angles = positions.astype(F32)[:, None] * frequency[None, :]
    if values.ndim == 3:
        angles = angles[:, None, :]
    cosine = jnp.cos(angles)
    sine_part = jnp.sin(angles)
    first_half = values[..., :half_width]
    second = values[..., half_width:]
    return jnp.concatenate(
        [first_half * cosine - second * sine_part, first_half * sine_part + second * cosine],
        axis=-1,
    )


def dot(a, b):
    return jnp.dot(a, b, preferred_element_type=F32)


def local(prompt, block_sizes, w_query_down, w_query, w_latent, w_keys, w_values, w_out):
    sections = lax.axis_size("section")
    section_id = lax.axis_index("section")
    tp_id = lax.axis_index("tp")
    tp_count = lax.axis_size("tp")
    tokens, share_cols = prompt.shape
    share_rows = tokens // tp_count
    down_weight, query_weight, latent_weight = w_query_down[0], w_query[0], w_latent[0]
    key_weight, value_weight, out_weight = w_keys[0], w_values[0], w_out[0]
    down_cols, latent_cols = down_weight.shape[1], latent_weight.shape[1]
    head_count = query_weight.shape[1] // (NOPE_DIM + ROPE_DIM)
    scale_factor = (NOPE_DIM + ROPE_DIM) ** (-0.5)
    all_positions = jnp.arange(tokens, dtype=jnp.int32)
    end_rows = jnp.cumsum(block_sizes) - 1

    def shift(array, distance, routes):
        pairs = [
            (a * tp_count + i, b * tp_count + (i + distance) % tp_count)
            for a, b in routes
            for i in range(tp_count)
        ]
        return lax.ppermute(array, ("section", "tp"), pairs)

    def gather(array, where, axis):
        routes = [(s, s) for s in where]
        width = array.shape[axis]
        shape = list(array.shape)
        shape[axis] = width * tp_count
        whole = jnp.zeros(shape, array.dtype)
        for k in range(tp_count):
            piece = array if k == 0 else shift(array, k, routes)
            whole = lax.dynamic_update_slice_in_dim(
                whole, piece, lax.rem(tp_id - k + tp_count, tp_count) * width, axis
            )
        return whole

    def keys_and_values(cache):
        plain = cache[:, :LATENT]
        keys = dot(plain, key_weight).astype(BF16).reshape(tokens, head_count, NOPE_DIM)
        values = dot(plain, value_weight).astype(BF16).reshape(tokens, head_count, VALUE_DIM)
        return keys, values

    def attend(compressed, positions, cache):
        keys, values = keys_and_values(cache)
        rows = compressed.shape[0]
        queries = dot(compressed, query_weight).reshape(rows, head_count, NOPE_DIM + ROPE_DIM)
        queries = jnp.concatenate(
            [queries[..., :NOPE_DIM], rotate(queries[..., NOPE_DIM:], positions)], axis=-1
        ).astype(BF16)
        scores = jnp.einsum("ihd,jhd->hij", queries[..., :NOPE_DIM], keys, preferred_element_type=F32)
        scores = scores + jnp.einsum(
            "ihr,jr->hij", queries[..., NOPE_DIM:], cache[:, LATENT:], preferred_element_type=F32
        )
        visible = all_positions[None, :] <= positions[:, None]
        powered = jnp.where(visible[None], jnp.exp(scores * scale_factor), 0.0)
        attention = (powered / jnp.sum(powered, axis=-1, keepdims=True)).astype(BF16)
        mixed = jnp.einsum("hij,jhv->ihv", attention, values, preferred_element_type=F32)
        return dot(mixed.astype(BF16).reshape(rows, head_count * VALUE_DIM), out_weight)

    def layer(hidden, own_share, tick):
        normed = rms_rows(hidden.astype(F32)).astype(BF16)
        parts = jnp.concatenate(
            [dot(normed, down_weight).astype(BF16), dot(normed, latent_weight).astype(BF16)], axis=1
        )
        whole = gather(parts[None], [tick], 0).astype(F32)
        down = jnp.concatenate([whole[m, :, :down_cols] for m in range(tp_count)], axis=1)
        latent = jnp.concatenate([whole[m, :, down_cols:] for m in range(tp_count)], axis=1)
        compressed = rms_rows(down).astype(BF16)
        cache = jnp.concatenate(
            [rms_rows(latent[:, :LATENT]), rotate(latent[:, LATENT:], all_positions)], axis=-1
        ).astype(BF16)
        partial = attend(compressed, all_positions, cache)
        start = tp_id * share_cols
        mine = lax.dynamic_slice_in_dim(partial, start, share_cols, 1) + own_share.astype(F32)
        partial = lax.dynamic_update_slice_in_dim(partial, mine, start, 1).astype(BF16)
        return partial, cache

    def pass_on(partial, tick):
        ends = jnp.take(partial, end_rows, axis=0)
        total = 0.0
        for k in range(tp_count):
            first = lax.rem(tp_id + k, tp_count) * share_rows
            block = lax.dynamic_slice_in_dim(partial, first, share_rows, 0)
            block = jnp.concatenate([block, ends], axis=0)
            total = total + shift(block, k, [(tick, tick + 1)]).astype(F32)
        total = total.astype(BF16)
        return total[:share_rows], total[share_rows:]

    own_cache = jnp.zeros((share_rows, LATENT + ROPE_DIM), BF16)
    own_ends = jnp.zeros((block_sizes.shape[0], share_cols), BF16)
    last = sections - 1
    latent_whole = gather(latent_weight, range(1, sections), 1) if last else latent_weight
    hidden, own_share = gather(prompt, [0], 1), prompt
    for tick in range(last):
        partial, cache = layer(hidden, own_share, tick)
        mine = lax.dynamic_slice_in_dim(cache, tp_id * share_rows, share_rows, 0)
        own_cache = jnp.where(section_id == tick, mine, own_cache)
        rows, ends = pass_on(partial, tick)
        ends_share = lax.dynamic_slice_in_dim(ends, tp_id * share_cols, share_cols, 1)
        own_ends = jnp.where(section_id == tick, shift(ends_share, 0, [(tick + 1, tick)]), own_ends)
        if tick + 1 < last:
            hidden = gather(rows, [tick + 1], 0)
            own_share = lax.dynamic_slice_in_dim(hidden, tp_id * share_cols, share_cols, 1)

    row_positions = tp_id * share_rows + jnp.arange(share_rows, dtype=jnp.int32)
    latent = dot(rms_rows(rows.astype(F32)).astype(BF16), latent_whole)
    fresh = jnp.concatenate(
        [rms_rows(latent[:, :LATENT]), rotate(latent[:, LATENT:], row_positions)], axis=-1
    ).astype(BF16)
    own_cache = jnp.where(section_id == last, fresh, own_cache)
    down = dot(rms_rows(ends.astype(F32)).astype(BF16), down_weight).astype(BF16)
    down = jnp.pad(down, ((0, 0), (0, fresh.shape[1] - down_cols)))
    whole = gather(jnp.concatenate([fresh, down], axis=0)[None], [last], 0)
    cache = whole[:, :share_rows].reshape(tokens, LATENT + ROPE_DIM)
    down = jnp.concatenate([whole[m, share_rows:, :down_cols] for m in range(tp_count)], axis=1)
    compressed = rms_rows(down.astype(F32)).astype(BF16)
    partial = attend(compressed, end_rows, cache).astype(BF16)
    total = ends_share.astype(F32)
    for k in range(tp_count):
        start = lax.rem(tp_id + k, tp_count) * share_cols
        block = lax.dynamic_slice_in_dim(partial, start, share_cols, 1)
        total = total + (shift(block, k, [(last, last)]) if k else block).astype(F32)
    own_ends = jnp.where(section_id == last, total.astype(BF16), own_ends)
    return (own_cache[None], own_ends[None])


ROW_WIDTH = LATENT + ROPE_DIM
HEAD_WIDTH = NOPE_DIM + ROPE_DIM
HALF = ROPE_DIM // 2
SMEM = pl.BlockSpec(memory_space=pltpu.SMEM)
VMEM = pl.BlockSpec(memory_space=pltpu.VMEM)


def call(kernel, out_shape, args, scratch=(), flops=0, scalars=0):
    many = isinstance(out_shape, list)
    moved = sum(a.size * a.dtype.itemsize for a in args)
    return pl.pallas_call(
        kernel,
        out_shape=out_shape,
        in_specs=[SMEM] * scalars + [VMEM] * (len(args) - scalars),
        out_specs=[VMEM] * len(out_shape) if many else VMEM,
        scratch_shapes=list(scratch),
        compiler_params=pltpu.CompilerParams(vmem_limit_bytes=20 * 2**20),
        cost_estimate=pl.CostEstimate(flops=flops, bytes_accessed=moved, transcendentals=0),
    )(*args)


def dot_t(a, b):
    return lax.dot_general(a, b, (((1,), (1,)), ((), ())), preferred_element_type=F32)


def unit(values):
    return lax.rsqrt(jnp.mean(values * values, axis=-1, keepdims=True) + EPSILON)


def turn(pair, angles):
    cosine, sine = angles[:, :HALF], angles[:, HALF:]
    a, b = pair[:, :HALF], pair[:, HALF:]
    return jnp.concatenate([a * cosine - b * sine, a * sine + b * cosine], axis=1)


def end_rows(sizes):
    ends = [sizes[0] - 1]
    for i in range(1, sizes.shape[0]):
        ends.append(ends[-1] + sizes[i])
    return ends


def column(scalars):
    rows = lax.broadcasted_iota(jnp.int32, (len(scalars), 1), 0)
    out = jnp.zeros((len(scalars), 1), jnp.int32)
    for i, value in enumerate(scalars):
        out = jnp.where(rows == i, value, out)
    return out


def send_kernel(prompt, w_latent, out):
    section, rep = lax.axis_index("section"), lax.axis_index("rep")
    rows, width = prompt.shape
    latent_cols = w_latent.shape[0]

    @pl.when(section == 0)
    def _():
        out[...] = prompt[...]

    @pl.when(section != 0)
    def _():
        quarter = w_latent[:, pl.ds(pl.multiple_of(rep * width, 128), width)]
        rest = jnp.zeros((rows - latent_cols, width), BF16)
        out[...] = jnp.concatenate([quarter, rest], axis=0)


def down_kernel(own, one, two, three, w_down, w_latent, out, weights):
    tp = lax.axis_index("tp")
    share = own.shape[1]
    latent_cols = w_latent.shape[0]
    squares, down, latent = 0.0, 0.0, 0.0
    for k, ref in enumerate((own, one, two, three)):
        columns = pl.ds(pl.multiple_of((tp ^ k) * share, 128), share)
        piece = ref[...]
        wide = piece.astype(F32)
        squares = squares + jnp.sum(wide * wide, axis=1, keepdims=True)
        down = down + dot_t(piece, w_down[:, columns])
        latent = latent + dot_t(piece, w_latent[:, columns])
        weights[tp ^ k] = piece[:latent_cols]
    scale = lax.rsqrt(squares / (4 * share) + EPSILON)
    out[...] = jnp.concatenate([down * scale, latent * scale], axis=1).astype(BF16)


def attend_rows(compressed, cache, seen, angles, w_query, w_keys, w_values):
    queries = dot(compressed, w_query[...])
    plain, turned = cache[:, :LATENT], cache[:, LATENT:]
    keys = dot(plain, w_keys[...]).astype(BF16)
    values = dot(plain, w_values[...]).astype(BF16)
    mixed = []
    for head in range(queries.shape[1] // HEAD_WIDTH):
        query = queries[:, head * HEAD_WIDTH : (head + 1) * HEAD_WIDTH]
        query = jnp.concatenate(
            [query[:, :NOPE_DIM], turn(query[:, NOPE_DIM:], angles)], axis=1
        ).astype(BF16)
        key = jnp.concatenate([keys[:, head * NOPE_DIM : (head + 1) * NOPE_DIM], turned], axis=1)
        scores = dot_t(query, key) * HEAD_WIDTH**-0.5
        powered = jnp.where(seen, jnp.exp(scores), 0.0)
        attention = (powered / jnp.sum(powered, axis=1, keepdims=True)).astype(BF16)
        mixed.append(dot(attention, values[:, head * VALUE_DIM : (head + 1) * VALUE_DIM]))
    return jnp.concatenate(mixed, axis=1).astype(BF16)


def layer_kernel(
    sizes, own, one, two, three, share, angles, w_query, w_keys, w_values, w_out,
    out0, out1, out2, out3, own_cache, stack, total, cached,
):
    tp = lax.axis_index("tp")
    tokens, width = share.shape
    block = tokens // 4
    down_cols = w_query.shape[0] // 4
    ends = column(end_rows(sizes))
    for k, ref in enumerate((own, one, two, three)):
        stack[tp ^ k] = ref[...]
    pieces = [stack[m].astype(F32) for m in range(4)]
    down = jnp.concatenate([p[:, :down_cols] for p in pieces], axis=1)
    latent = jnp.concatenate([p[:, down_cols:] for p in pieces], axis=1)
    compressed = (down * unit(down)).astype(BF16)
    plain = latent[:, :LATENT]
    cache = jnp.concatenate(
        [plain * unit(plain), turn(latent[:, LATENT:], angles[...])], axis=1
    ).astype(BF16)
    cached[...] = cache
    own_cache[...] = cached[pl.ds(pl.multiple_of(tp * block, block), block), :]
    seen = lax.broadcasted_iota(jnp.int32, (tokens, tokens), 0) >= lax.broadcasted_iota(
        jnp.int32, (tokens, tokens), 1
    )
    mixed = attend_rows(compressed, cache, seen, angles[...], w_query, w_keys, w_values)
    chosen = lax.broadcasted_iota(jnp.int32, (ends.shape[0], tokens), 1) == ends
    chosen = chosen.astype(BF16)
    rows = jnp.concatenate([mixed, dot(chosen, mixed).astype(BF16)], axis=0)
    total[...] = dot(rows, w_out[...])
    mine = pl.ds(pl.multiple_of(tp * width, 128), width)
    added = jnp.concatenate([share[...].astype(F32), dot(chosen, share[...])], axis=0)
    total[:, mine] += added
    last = total[tokens:, :]
    for k, out in enumerate((out0, out1, out2, out3)):
        part = total[pl.ds(pl.multiple_of((tp ^ k) * block, block), block), :]
        out[...] = jnp.concatenate([part, last], axis=0).astype(BF16)


def latent_kernel(
    one, two, three, four, angles, quarter, near, far, w_down,
    out, own_ends, hidden,
):
    tp, rep = lax.axis_index("tp"), lax.axis_index("rep")
    block = angles.shape[0] // 4
    width = own_ends.shape[1]
    rows = one[...].astype(F32) + two[...].astype(F32) + three[...].astype(F32) + four[...].astype(F32)
    narrow = rows.astype(BF16)
    rows = narrow.astype(F32)
    hidden[...] = rows
    scale = unit(rows)
    count = w_down.shape[0]
    totals = [0.0] * 4
    for step, weights in enumerate((quarter, near, far.at[0], far.at[1])):
        columns = pl.ds(pl.multiple_of((rep ^ step) * width, 128), width)
        piece = hidden[0:block, columns].astype(BF16)
        totals = [total + dot_t(piece, weights[m]) for m, total in enumerate(totals)]
    latent = jnp.concatenate(totals, axis=1) * scale[:block]
    plain = latent[:, :LATENT]
    own_angles = angles[pl.ds(pl.multiple_of(tp * block, block), block), :]
    fresh = jnp.concatenate(
        [plain * unit(plain), turn(latent[:, LATENT:], own_angles)], axis=1
    )
    down = dot_t(narrow[block:, :], w_down[...]) * scale[block:]
    down = jnp.concatenate([down, jnp.zeros((down.shape[0], ROW_WIDTH - count), F32)], axis=1)
    out[...] = jnp.concatenate([fresh, down], axis=0).astype(BF16)
    mine = pl.ds(pl.multiple_of(tp * width, 128), width)
    own_ends[...] = hidden[block:, mine].astype(BF16)


def ends_kernel(
    sizes, own, one, two, three, angles, w_query, w_keys, w_values, w_out,
    out0, out1, out2, out3, stack, total,
):
    tp = lax.axis_index("tp")
    ends = end_rows(sizes)
    count = len(ends)
    block = own.shape[0] - count
    down_cols = w_query.shape[0] // 4
    width = out0.shape[1]
    for k, ref in enumerate((own, one, two, three)):
        stack[tp ^ k] = ref[...].astype(F32)
    pieces = [stack[m] for m in range(4)]
    cache = jnp.concatenate([p[:block] for p in pieces], axis=0).astype(BF16)
    down = jnp.concatenate([p[block:, :down_cols] for p in pieces], axis=1)
    compressed = (down * unit(down)).astype(BF16)
    end_angles = jnp.concatenate([angles[pl.ds(e, 1), :] for e in ends], axis=0)
    seen = lax.broadcasted_iota(jnp.int32, (count, 4 * block), 1) <= column(ends)
    mixed = attend_rows(compressed, cache, seen, end_angles, w_query, w_keys, w_values)
    total[...] = dot(mixed, w_out[...])
    for k, out in enumerate((out0, out1, out2, out3)):
        columns = pl.ds(pl.multiple_of((tp ^ k) * width, 128), width)
        out[...] = total[:, columns].astype(BF16)


def local_two(prompt, block_sizes, w_query_down, w_query, w_latent, w_keys, w_values, w_out):
    section = lax.axis_index("section")
    tokens, share = prompt.shape
    block = tokens // 4
    count = block_sizes.shape[0]
    w_down, w_up, w_lat = w_query_down[0].T, w_query[0], w_latent[0].T
    w_key, w_value, w_final = w_keys[0], w_values[0], w_out[0]
    down_cols, latent_cols = w_down.shape[0], w_lat.shape[0]
    model = 4 * share
    frequency = 10000.0 ** (-2.0 * np.arange(HALF, dtype=np.float32) / ROPE_DIM)
    angles = np.arange(tokens, dtype=np.float32)[:, None] * frequency.astype(np.float32)[None, :]
    angles = jnp.asarray(np.concatenate([np.cos(angles), np.sin(angles)], axis=1), F32)

    def within(array, k):
        pairs = [(s * 4 + i, s * 4 + (i ^ k)) for s in range(2) for i in range(4)]
        return lax.ppermute(array, ("section", "tp"), pairs)

    def onward(array, k):
        pairs = [(i, 4 + (i ^ k)) for i in range(4)] + [(4 + i, i) for i in range(4)]
        return lax.ppermute(array, ("section", "tp"), pairs)

    def over_rep(array, k):
        return lax.ppermute(array, "rep", [(i, i ^ k) for i in range(4)])

    sent = call(send_kernel, jax.ShapeDtypeStruct((tokens, share), BF16), [prompt, w_lat])
    shares = [sent] + [within(sent, k) for k in (1, 2, 3)]
    parts, quarter = call(
        down_kernel,
        [
            jax.ShapeDtypeStruct((tokens, down_cols + latent_cols), BF16),
            jax.ShapeDtypeStruct((4, latent_cols, share), BF16),
        ],
        [*shares, w_down, w_lat],
        flops=2 * tokens * model * (down_cols + latent_cols),
    )
    pieces = [parts] + [within(parts, k) for k in (1, 2, 3)]
    near = over_rep(quarter, 1)
    quarters = [quarter, near, over_rep(jnp.stack([quarter, near]), 2)]

    message = jax.ShapeDtypeStruct((block + count, model), BF16)
    *blocks, first_cache = call(
        layer_kernel,
        [message] * 4 + [jax.ShapeDtypeStruct((block, ROW_WIDTH), BF16)],
        [block_sizes, *pieces, prompt, angles, w_up, w_key, w_value, w_final],
        [
            pltpu.VMEM((4, tokens, down_cols + latent_cols), BF16),
            pltpu.VMEM((tokens + count, model), F32),
            pltpu.VMEM((tokens, ROW_WIDTH), BF16),
        ],
        flops=2 * tokens * (w_up.size + w_key.size + w_value.size + w_final.size),
        scalars=1,
    )
    arrived = [onward(blocks[k], k) for k in (0, 3, 2, 1)]
    fresh, ends_share = call(
        latent_kernel,
        [
            jax.ShapeDtypeStruct((block + count, ROW_WIDTH), BF16),
            jax.ShapeDtypeStruct((count, share), BF16),
        ],
        [*arrived, angles, *quarters, w_down],
        [pltpu.VMEM((block + count, model), F32)],
        flops=2 * block * model * ROW_WIDTH,
    )
    pieces = [fresh] + [within(fresh, k) for k in (1, 2, 3)]
    first_ends = onward(ends_share, 0)
    outs = call(
        ends_kernel,
        [jax.ShapeDtypeStruct((count, share), BF16)] * 4,
        [block_sizes, *pieces, angles, w_up, w_key, w_value, w_final],
        [
            pltpu.VMEM((4, block + count, ROW_WIDTH), F32),
            pltpu.VMEM((count, model), F32),
        ],
        flops=2 * tokens * (w_key.size + w_value.size),
        scalars=1,
    )
    total = ends_share.astype(F32) + outs[0].astype(F32)
    for k in (1, 2, 3):
        total = total + within(outs[k], k).astype(F32)
    own_ends = jnp.where(section == 0, first_ends, total.astype(BF16))
    own_cache = jnp.where(section == 0, first_cache, fresh[:block])
    return (own_cache[None], own_ends[None])


def solution(mesh):
    sizes = [mesh.shape[a] for a in ("section", "tp", "rep")]
    body = local_two if sizes == [2, 4, 4] else local
    in_specs = (
        P("rep", "tp"),
        P("rep"),
        P("section", None, "tp"),
        P("section", None, "tp"),
        P("section", None, "tp"),
        P("section", None, "tp"),
        P("section", None, "tp"),
        P("section", "tp", None),
    )
    out_specs = (P("section", ("rep", "tp"), None), P("section", "rep", "tp"))
    return jax.shard_map(body, mesh=mesh, in_specs=in_specs, out_specs=out_specs, check_vma=False)
```

```python
import jax
import jax.numpy as jnp
import numpy as np
from jax import lax
from jax.experimental import pallas as pl
from jax.experimental.pallas import tpu as pltpu
from jax.sharding import PartitionSpec as P

NOPE_DIM = 128
ROPE_DIM = 32
VALUE_DIM = 128
LATENT = 512
EPSILON = 1e-06
F32 = jnp.float32
BF16 = jnp.bfloat16


def rms_rows(values):
    return values * lax.rsqrt(jnp.mean(values * values, axis=-1, keepdims=True) + EPSILON)


def rotate(values, positions):
    half_width = values.shape[-1] // 2
    frequency = 10000.0 ** (-2.0 * jnp.arange(half_width, dtype=F32) / values.shape[-1])
    angles = positions.astype(F32)[:, None] * frequency[None, :]
    if values.ndim == 3:
        angles = angles[:, None, :]
    cosine = jnp.cos(angles)
    sine_part = jnp.sin(angles)
    first_half = values[..., :half_width]
    second = values[..., half_width:]
    return jnp.concatenate(
        [first_half * cosine - second * sine_part, first_half * sine_part + second * cosine],
        axis=-1,
    )


def dot(a, b):
    return jnp.dot(a, b, preferred_element_type=F32)


def local(prompt, block_sizes, w_query_down, w_query, w_latent, w_keys, w_values, w_out):
    sections = lax.axis_size("section")
    section_id = lax.axis_index("section")
    tp_id = lax.axis_index("tp")
    tp_count = lax.axis_size("tp")
    tokens, share_cols = prompt.shape
    share_rows = tokens // tp_count
    down_weight, query_weight, latent_weight = w_query_down[0], w_query[0], w_latent[0]
    key_weight, value_weight, out_weight = w_keys[0], w_values[0], w_out[0]
    down_cols, latent_cols = down_weight.shape[1], latent_weight.shape[1]
    head_count = query_weight.shape[1] // (NOPE_DIM + ROPE_DIM)
    scale_factor = (NOPE_DIM + ROPE_DIM) ** (-0.5)
    all_positions = jnp.arange(tokens, dtype=jnp.int32)
    end_rows = jnp.cumsum(block_sizes) - 1

    def shift(array, distance, routes):
        pairs = [
            (a * tp_count + i, b * tp_count + (i + distance) % tp_count)
            for a, b in routes
            for i in range(tp_count)
        ]
        return lax.ppermute(array, ("section", "tp"), pairs)

    def gather(array, where, axis):
        routes = [(s, s) for s in where]
        width = array.shape[axis]
        shape = list(array.shape)
        shape[axis] = width * tp_count
        whole = jnp.zeros(shape, array.dtype)
        for k in range(tp_count):
            piece = array if k == 0 else shift(array, k, routes)
            whole = lax.dynamic_update_slice_in_dim(
                whole, piece, lax.rem(tp_id - k + tp_count, tp_count) * width, axis
            )
        return whole

    def keys_and_values(cache):
        plain = cache[:, :LATENT]
        keys = dot(plain, key_weight).astype(BF16).reshape(tokens, head_count, NOPE_DIM)
        values = dot(plain, value_weight).astype(BF16).reshape(tokens, head_count, VALUE_DIM)
        return keys, values

    def attend(compressed, positions, cache):
        keys, values = keys_and_values(cache)
        rows = compressed.shape[0]
        queries = dot(compressed, query_weight).reshape(rows, head_count, NOPE_DIM + ROPE_DIM)
        queries = jnp.concatenate(
            [queries[..., :NOPE_DIM], rotate(queries[..., NOPE_DIM:], positions)], axis=-1
        ).astype(BF16)
        scores = jnp.einsum("ihd,jhd->hij", queries[..., :NOPE_DIM], keys, preferred_element_type=F32)
        scores = scores + jnp.einsum(
            "ihr,jr->hij", queries[..., NOPE_DIM:], cache[:, LATENT:], preferred_element_type=F32
        )
        visible = all_positions[None, :] <= positions[:, None]
        powered = jnp.where(visible[None], jnp.exp(scores * scale_factor), 0.0)
        attention = (powered / jnp.sum(powered, axis=-1, keepdims=True)).astype(BF16)
        mixed = jnp.einsum("hij,jhv->ihv", attention, values, preferred_element_type=F32)
        return dot(mixed.astype(BF16).reshape(rows, head_count * VALUE_DIM), out_weight)

    def layer(hidden, own_share, tick):
        normed = rms_rows(hidden.astype(F32)).astype(BF16)
        parts = jnp.concatenate(
            [dot(normed, down_weight).astype(BF16), dot(normed, latent_weight).astype(BF16)], axis=1
        )
        whole = gather(parts[None], [tick], 0).astype(F32)
        down = jnp.concatenate([whole[m, :, :down_cols] for m in range(tp_count)], axis=1)
        latent = jnp.concatenate([whole[m, :, down_cols:] for m in range(tp_count)], axis=1)
        compressed = rms_rows(down).astype(BF16)
        cache = jnp.concatenate(
            [rms_rows(latent[:, :LATENT]), rotate(latent[:, LATENT:], all_positions)], axis=-1
        ).astype(BF16)
        partial = attend(compressed, all_positions, cache)
        start = tp_id * share_cols
        mine = lax.dynamic_slice_in_dim(partial, start, share_cols, 1) + own_share.astype(F32)
        partial = lax.dynamic_update_slice_in_dim(partial, mine, start, 1).astype(BF16)
        return partial, cache

    def pass_on(partial, tick):
        ends = jnp.take(partial, end_rows, axis=0)
        total = 0.0
        for k in range(tp_count):
            first = lax.rem(tp_id + k, tp_count) * share_rows
            block = lax.dynamic_slice_in_dim(partial, first, share_rows, 0)
            block = jnp.concatenate([block, ends], axis=0)
            total = total + shift(block, k, [(tick, tick + 1)]).astype(F32)
        total = total.astype(BF16)
        return total[:share_rows], total[share_rows:]

    own_cache = jnp.zeros((share_rows, LATENT + ROPE_DIM), BF16)
    own_ends = jnp.zeros((block_sizes.shape[0], share_cols), BF16)
    last = sections - 1
    latent_whole = gather(latent_weight, range(1, sections), 1) if last else latent_weight
    hidden, own_share = gather(prompt, [0], 1), prompt
    for tick in range(last):
        partial, cache = layer(hidden, own_share, tick)
        mine = lax.dynamic_slice_in_dim(cache, tp_id * share_rows, share_rows, 0)
        own_cache = jnp.where(section_id == tick, mine, own_cache)
        rows, ends = pass_on(partial, tick)
        ends_share = lax.dynamic_slice_in_dim(ends, tp_id * share_cols, share_cols, 1)
        own_ends = jnp.where(section_id == tick, shift(ends_share, 0, [(tick + 1, tick)]), own_ends)
        if tick + 1 < last:
            hidden = gather(rows, [tick + 1], 0)
            own_share = lax.dynamic_slice_in_dim(hidden, tp_id * share_cols, share_cols, 1)

    row_positions = tp_id * share_rows + jnp.arange(share_rows, dtype=jnp.int32)
    latent = dot(rms_rows(rows.astype(F32)).astype(BF16), latent_whole)
    fresh = jnp.concatenate(
        [rms_rows(latent[:, :LATENT]), rotate(latent[:, LATENT:], row_positions)], axis=-1
    ).astype(BF16)
    own_cache = jnp.where(section_id == last, fresh, own_cache)
    down = dot(rms_rows(ends.astype(F32)).astype(BF16), down_weight).astype(BF16)
    down = jnp.pad(down, ((0, 0), (0, fresh.shape[1] - down_cols)))
    whole = gather(jnp.concatenate([fresh, down], axis=0)[None], [last], 0)
    cache = whole[:, :share_rows].reshape(tokens, LATENT + ROPE_DIM)
    down = jnp.concatenate([whole[m, share_rows:, :down_cols] for m in range(tp_count)], axis=1)
    compressed = rms_rows(down.astype(F32)).astype(BF16)
    partial = attend(compressed, end_rows, cache).astype(BF16)
    total = ends_share.astype(F32)
    for k in range(tp_count):
        start = lax.rem(tp_id + k, tp_count) * share_cols
        block = lax.dynamic_slice_in_dim(partial, start, share_cols, 1)
        total = total + (shift(block, k, [(last, last)]) if k else block).astype(F32)
    own_ends = jnp.where(section_id == last, total.astype(BF16), own_ends)
    return (own_cache[None], own_ends[None])


ROW_WIDTH = LATENT + ROPE_DIM
HEAD_WIDTH = NOPE_DIM + ROPE_DIM
HALF = ROPE_DIM // 2
SMEM = pl.BlockSpec(memory_space=pltpu.SMEM)
VMEM = pl.BlockSpec(memory_space=pltpu.VMEM)
HBM = pl.BlockSpec(memory_space=pltpu.HBM)


def call(kernel, out_shape, args, scratch=(), flops=0, scalars=0, left=0, space=VMEM, grant=8):
    many = isinstance(out_shape, list)
    moved = sum(a.size * a.dtype.itemsize for a in args)
    return pl.pallas_call(
        kernel,
        out_shape=out_shape,
        in_specs=[SMEM] * scalars + [VMEM] * (len(args) - scalars - left) + [HBM] * left,
        out_specs=[space] * len(out_shape) if many else space,
        scratch_shapes=list(scratch),
        compiler_params=pltpu.CompilerParams(vmem_limit_bytes=grant * 2**20),
        cost_estimate=pl.CostEstimate(flops=flops, bytes_accessed=moved, transcendentals=0),
    )(*args)


def dot_t(a, b):
    return lax.dot_general(a, b, (((1,), (1,)), ((), ())), preferred_element_type=F32)


def unit(values):
    return lax.rsqrt(jnp.mean(values * values, axis=-1, keepdims=True) + EPSILON)


def turn(pair, angles):
    cosine, sine = angles[:, :HALF], angles[:, HALF:]
    a, b = pair[:, :HALF], pair[:, HALF:]
    return jnp.concatenate([a * cosine - b * sine, a * sine + b * cosine], axis=1)


def end_rows(sizes):
    ends = [sizes[0] - 1]
    for i in range(1, sizes.shape[0]):
        ends.append(ends[-1] + sizes[i])
    return ends


def column(scalars):
    rows = lax.broadcasted_iota(jnp.int32, (len(scalars), 1), 0)
    out = jnp.zeros((len(scalars), 1), jnp.int32)
    for i, value in enumerate(scalars):
        out = jnp.where(rows == i, value, out)
    return out


def send_kernel(prompt, w_latent, out, half, packed, sem):
    section, rep = lax.axis_index("section"), lax.axis_index("rep")
    width = out.shape[1]
    cols = half.shape[0]

    @pl.when(section == 0)
    def _():
        copy = pltpu.make_async_copy(prompt, packed, sem)
        copy.start()
        copy.wait()
        copy = pltpu.make_async_copy(packed, out, sem)
        copy.start()
        copy.wait()

    @pl.when(section != 0)
    def _():
        columns = pl.ds(pl.multiple_of((rep & 1) * half.shape[1], 128), half.shape[1])
        copy = pltpu.make_async_copy(w_latent.at[:, columns], half, sem)
        copy.start()
        copy.wait()
        extra = half[:, width : width + 256].astype(F32)
        rows = out.shape[0] - cols
        left = cols - 2 * rows
        tail = [extra[2 * rows :, :128], extra[2 * rows :, 128:], jnp.zeros((rows - 2 * left, 128), F32)]
        extra = jnp.concatenate(
            [extra[:rows], extra[rows : 2 * rows], jnp.concatenate(tail, axis=0)], axis=1
        )
        whole = jnp.concatenate([half[:, :width].astype(F32), extra], axis=0)
        packed[...] = whole.astype(BF16)
        copy = pltpu.make_async_copy(packed, out, sem)
        copy.start()
        copy.wait()


def unpack_share(share, cols):
    share = share.astype(F32)
    rows = share.shape[0] - cols
    left = cols - 2 * rows
    extra, tail = share[cols:, :512], share[cols:, 512:]
    tail = jnp.concatenate([tail[:left], tail[left : 2 * left]], axis=1)
    extra = jnp.concatenate([extra[:, :256], extra[:, 256:], tail], axis=0)
    return jnp.concatenate([share[:cols], extra], axis=1).astype(BF16)


def down_kernel(own, one, two, three, w_down, w_latent, out):
    section, tp, rep = (lax.axis_index(a) for a in ("section", "tp", "rep"))
    tokens, share = own.shape
    cols, model = w_latent.shape
    third = tokens // 3

    @pl.when(section == 0)
    def _():
        squares, down, latent = 0.0, 0.0, 0.0
        for k, ref in enumerate((own, one, two, three)):
            columns = pl.ds(pl.multiple_of((tp ^ k) * share, 128), share)
            piece = ref[...]
            wide = piece.astype(F32)
            squares = squares + jnp.sum(wide * wide, axis=1, keepdims=True)
            down = down + dot_t(piece, w_down[:, columns])
            latent = latent + dot_t(piece, w_latent[:, columns])
        scale = lax.rsqrt(squares / model + EPSILON)
        parts = jnp.concatenate([down * scale, latent * scale], axis=1)
        rest = parts[:, 256:]
        rest = [rest[i * third : (i + 1) * third] for i in range(3)]
        rest.append(jnp.zeros((third, 256 - 3 * rest[0].shape[1]), F32))
        out[...] = jnp.concatenate([parts[:, :256], jnp.concatenate(rest, axis=1)], axis=0).astype(BF16)

    @pl.when(section != 0)
    def _():
        first = (rep & 1) * (model // 2) + share + 256
        mine = w_latent[:, pl.ds(pl.multiple_of(first, 128), 384)].astype(F32)
        rest = mine[:, 256:]
        high = cols // 2 + 4
        lower = jnp.concatenate([rest[high:], jnp.zeros((2 * high - cols, 128), F32)], axis=0)
        rest = jnp.concatenate([rest[:high], lower], axis=1)
        blank = jnp.zeros((out.shape[0] - cols - high, 256), F32)
        out[...] = jnp.concatenate([mine[:, :256], rest, blank], axis=0).astype(BF16)


def unpack_rest(piece, cols):
    piece = piece.astype(F32)
    high = cols // 2 + 4
    rest = piece[cols : cols + high]
    rest = jnp.concatenate([rest[:, :128], rest[: cols - high, 128:]], axis=0)
    return jnp.concatenate([piece[:cols], rest], axis=1).astype(BF16)


def unpack_parts(piece, tokens, width):
    piece = piece.astype(F32)
    rest, size = piece[tokens:], width - 256
    rest = jnp.concatenate([rest[:, i * size : (i + 1) * size] for i in range(3)], axis=0)
    return jnp.concatenate([piece[:tokens], rest], axis=1)


def attend_rows(compressed, cache, seen, angles, w_query, w_keys, w_values):
    plain, turned = cache[:, :LATENT], cache[:, LATENT:]
    keys = dot(plain, w_keys[...]).astype(BF16)
    values = dot(plain, w_values[...]).astype(BF16)
    queries = dot(compressed, w_query[...])
    mixed = []
    for head in range(queries.shape[1] // HEAD_WIDTH):
        query = queries[:, head * HEAD_WIDTH : (head + 1) * HEAD_WIDTH]
        query = jnp.concatenate(
            [query[:, :NOPE_DIM], turn(query[:, NOPE_DIM:], angles)], axis=1
        ).astype(BF16)
        key = jnp.concatenate([keys[:, head * NOPE_DIM : (head + 1) * NOPE_DIM], turned], axis=1)
        scores = dot_t(query, key) * HEAD_WIDTH**-0.5
        powered = jnp.where(seen, jnp.exp(scores), 0.0)
        attention = (powered / jnp.sum(powered, axis=1, keepdims=True)).astype(BF16)
        mixed.append(dot(attention, values[:, head * VALUE_DIM : (head + 1) * VALUE_DIM]))
    return jnp.concatenate(mixed, axis=1).astype(BF16)


def layer_kernel(
    sizes, own, one, two, three, share1, share2, share3, w_latent, prompt, angles,
    w_query, w_keys, w_values, w_out, out0, out1, out2, out3, own_cache, half, stack, total, cached,
):
    section, tp, rep = (lax.axis_index(a) for a in ("section", "tp", "rep"))
    tokens, width = prompt.shape
    block = tokens // 4
    cols, long = half.shape[1:]
    down_cols = w_query.shape[0] // 4

    @pl.when(section != 0)
    def _():
        half[tp] = w_latent[:, pl.ds(pl.multiple_of((rep & 1) * long, 128), long)]
        for k, weights, rest in ((1, share1, one), (2, share2, two), (3, share3, three)):
            half[tp ^ k, :, : width + 256] = unpack_share(weights[...], cols)
            half[tp ^ k, :, width + 256 :] = unpack_rest(rest[...], cols)

    @pl.when(section == 0)
    def _():
        ends = column(end_rows(sizes))
        for k, ref in enumerate((own, one, two, three)):
            stack[tp ^ k] = ref[...]
        pieces = [unpack_parts(stack[m], tokens, down_cols + cols) for m in range(4)]
        down = jnp.concatenate([p[:, :down_cols] for p in pieces], axis=1)
        latent = jnp.concatenate([p[:, down_cols:] for p in pieces], axis=1)
        compressed = (down * unit(down)).astype(BF16)
        plain = latent[:, :LATENT]
        cache = jnp.concatenate(
            [plain * unit(plain), turn(latent[:, LATENT:], angles[...])], axis=1
        ).astype(BF16)
        cached[...] = cache
        own_cache[...] = cached[pl.ds(pl.multiple_of(tp * block, block), block), :]
        seen = lax.broadcasted_iota(jnp.int32, (tokens, tokens), 0) >= lax.broadcasted_iota(
            jnp.int32, (tokens, tokens), 1
        )
        mixed = attend_rows(compressed, cache, seen, angles[...], w_query, w_keys, w_values)
        chosen = lax.broadcasted_iota(jnp.int32, (ends.shape[0], tokens), 1) == ends
        chosen = chosen.astype(BF16)
        rows = jnp.concatenate([mixed, dot(chosen, mixed).astype(BF16)], axis=0)
        total[...] = dot(rows, w_out[...])
        mine = pl.ds(pl.multiple_of(tp * width, 128), width)
        added = jnp.concatenate([prompt[...].astype(F32), dot(chosen, prompt[...])], axis=0)
        total[:, mine] += added
        last = total[tokens:, :]
        for k, out in enumerate((out0, out1, out2, out3)):
            part = total[pl.ds(pl.multiple_of((tp ^ k) * block, block), block), :]
            out[...] = jnp.concatenate([part, last], axis=0).astype(BF16)


def latent_kernel(
    one, two, three, four, angles, half, near, w_down, out, own_cache, own_ends, hidden
):
    tp, rep = lax.axis_index("tp"), lax.axis_index("rep")
    block = angles.shape[0] // 4
    width = own_ends.shape[1]
    rows = one[...].astype(F32) + two[...].astype(F32) + three[...].astype(F32) + four[...].astype(F32)
    narrow = rows.astype(BF16)
    rows = narrow.astype(F32)
    hidden[...] = rows
    scale = unit(rows)
    totals = [0.0] * 4
    for step, weights in enumerate((half, near)):
        long = weights.shape[2]
        columns = pl.ds(pl.multiple_of(((rep & 1) ^ step) * long, 128), long)
        piece = hidden[0:block, columns].astype(BF16)
        totals = [total + dot_t(piece, weights[m]) for m, total in enumerate(totals)]
    latent = jnp.concatenate(totals, axis=1) * scale[:block]
    plain = latent[:, :LATENT]
    plain = plain * unit(plain)
    own_angles = angles[pl.ds(pl.multiple_of(tp * block, block), block), :]
    turned = turn(latent[:, LATENT:], own_angles)
    own_cache[...] = jnp.concatenate([plain, turned], axis=1).astype(BF16)
    down = dot_t(narrow[block:, :], w_down[...]) * scale[block:]
    count = down.shape[0]
    turned = [turned[i * count : (i + 1) * count] for i in range(block // count)]
    last = jnp.concatenate([*turned, down], axis=1)
    last = jnp.concatenate([last, jnp.zeros((count, LATENT - last.shape[1]), F32)], axis=1)
    out[...] = jnp.concatenate([plain, last], axis=0).astype(BF16)
    mine = pl.ds(pl.multiple_of(tp * width, 128), width)
    own_ends[...] = hidden[block:, mine].astype(BF16)


def ends_kernel(
    sizes, own, one, two, three, angles, w_query, w_keys, w_values, w_out,
    out0, out1, out2, out3, stack, total,
):
    tp = lax.axis_index("tp")
    ends = end_rows(sizes)
    count = len(ends)
    block = own.shape[0] - count
    steps = block // count
    down_cols = w_query.shape[0] // 4
    width = out0.shape[1]
    for k, ref in enumerate((own, one, two, three)):
        stack[tp ^ k] = ref[...].astype(F32)
    pieces = [stack[m] for m in range(4)]
    plain = jnp.concatenate([p[:block] for p in pieces], axis=0)
    last = [p[block:] for p in pieces]
    turned = jnp.concatenate(
        [p[:, i * ROPE_DIM : (i + 1) * ROPE_DIM] for p in last for i in range(steps)], axis=0
    )
    cache = jnp.concatenate([plain, turned], axis=1).astype(BF16)
    first = steps * ROPE_DIM
    down = jnp.concatenate([p[:, first : first + down_cols] for p in last], axis=1)
    compressed = (down * unit(down)).astype(BF16)
    end_angles = jnp.concatenate([angles[pl.ds(e, 1), :] for e in ends], axis=0)
    seen = lax.broadcasted_iota(jnp.int32, (count, 4 * block), 1) <= column(ends)
    mixed = attend_rows(compressed, cache, seen, end_angles, w_query, w_keys, w_values)
    total[...] = dot(mixed, w_out[...])
    for k, out in enumerate((out0, out1, out2, out3)):
        columns = pl.ds(pl.multiple_of((tp ^ k) * width, 128), width)
        out[...] = total[:, columns].astype(BF16)


def local_two(prompt, block_sizes, w_query_down, w_query, w_latent, w_keys, w_values, w_out):
    section = lax.axis_index("section")
    tokens, share = prompt.shape
    block = tokens // 4
    count = block_sizes.shape[0]
    w_down, w_up, w_lat = w_query_down[0].T, w_query[0], w_latent[0].T
    w_key, w_value, w_final = w_keys[0], w_values[0], w_out[0]
    down_cols, latent_cols = w_down.shape[0], w_lat.shape[0]
    model = 4 * share
    frequency = 10000.0 ** (-2.0 * np.arange(HALF, dtype=np.float32) / ROPE_DIM)
    angles = np.arange(tokens, dtype=np.float32)[:, None] * frequency.astype(np.float32)[None, :]
    angles = jnp.asarray(np.concatenate([np.cos(angles), np.sin(angles)], axis=1), F32)

    def within(array, k):
        pairs = [(s * 4 + i, s * 4 + (i ^ k)) for s in range(2) for i in range(4)]
        return lax.ppermute(array, ("section", "tp"), pairs)

    def onward(array, k):
        pairs = [(i, 4 + (i ^ k)) for i in range(4)] + [(4 + i, i) for i in range(4)]
        return lax.ppermute(array, ("section", "tp"), pairs)

    def over_rep(array, k):
        return lax.ppermute(array, "rep", [(i, i ^ k) for i in range(4)])

    sent = call(
        send_kernel,
        jax.ShapeDtypeStruct((tokens, share), BF16),
        [prompt, w_lat],
        [
            pltpu.VMEM((latent_cols, model // 2), BF16),
            pltpu.VMEM((tokens, share), BF16),
            pltpu.SemaphoreType.DMA,
        ],
        left=2,
        space=HBM,
        grant=57,
        flops=2 * 10**10,
    )
    shares = [within(sent, k) for k in (1, 2, 3)]
    parts = call(
        down_kernel,
        jax.ShapeDtypeStruct((tokens + tokens // 3, 256), BF16),
        [prompt, *shares, w_down, w_lat],
        flops=2 * 10**10,
    )
    pieces = [parts] + [within(parts, k) for k in (1, 2, 3)]

    message = jax.ShapeDtypeStruct((block + count, model), BF16)
    *blocks, first_cache, half = call(
        layer_kernel,
        [message] * 4
        + [
            jax.ShapeDtypeStruct((block, ROW_WIDTH), BF16),
            jax.ShapeDtypeStruct((4, latent_cols, model // 2), BF16),
        ],
        [block_sizes, *pieces, *shares, w_lat, prompt, angles, w_up, w_key, w_value, w_final],
        [
            pltpu.VMEM((4, *parts.shape), BF16),
            pltpu.VMEM((tokens + count, model), F32),
            pltpu.VMEM((tokens, ROW_WIDTH), BF16),
        ],
        flops=2 * tokens * (w_up.size + w_key.size + w_value.size + w_final.size),
        scalars=1,
        grant=16,
    )
    arrived = [onward(blocks[k], k) for k in (3, 2, 1, 0)]
    near = over_rep(half, 1)
    fresh, last_cache, ends_share = call(
        latent_kernel,
        [
            jax.ShapeDtypeStruct((block + count, LATENT), BF16),
            jax.ShapeDtypeStruct((block, ROW_WIDTH), BF16),
            jax.ShapeDtypeStruct((count, share), BF16),
        ],
        [*arrived, angles, half, near, w_down],
        [pltpu.VMEM((block + count, model), F32)],
        flops=2 * 10**11,
    )
    pieces = [fresh] + [within(fresh, k) for k in (1, 2, 3)]
    first_ends = onward(ends_share, 0)
    outs = call(
        ends_kernel,
        [jax.ShapeDtypeStruct((count, share), BF16)] * 4,
        [block_sizes, *pieces, angles, w_up, w_key, w_value, w_final],
        [
            pltpu.VMEM((4, block + count, LATENT), F32),
            pltpu.VMEM((count, model), F32),
        ],
        flops=2 * tokens * (w_key.size + w_value.size),
        scalars=1,
    )
    total = ends_share.astype(F32) + outs[0].astype(F32)
    for k in (1, 2, 3):
        total = total + within(outs[k], k).astype(F32)
    own_ends = jnp.where(section == 0, first_ends, total.astype(BF16))
    own_cache = jnp.where(section == 0, first_cache, last_cache)
    return (own_cache[None], own_ends[None])


def solution(mesh):
    sizes = [mesh.shape[a] for a in ("section", "tp", "rep")]
    body = local_two if sizes == [2, 4, 4] else local
    in_specs = (
        P("rep", "tp"),
        P("rep"),
        P("section", None, "tp"),
        P("section", None, "tp"),
        P("section", None, "tp"),
        P("section", None, "tp"),
        P("section", None, "tp"),
        P("section", "tp", None),
    )
    out_specs = (P("section", ("rep", "tp"), None), P("section", "rep", "tp"))
    return jax.shard_map(body, mesh=mesh, in_specs=in_specs, out_specs=out_specs, check_vma=False)
```

```python
import jax
import jax.numpy as jnp
import numpy as np
from jax import lax
from jax.experimental import pallas as pl
from jax.experimental.pallas import tpu as pltpu
from jax.sharding import PartitionSpec as P

NOPE_DIM = 128
ROPE_DIM = 32
VALUE_DIM = 128
LATENT = 512
EPSILON = 1e-06
F32 = jnp.float32
BF16 = jnp.bfloat16


def rms_rows(values):
    return values * lax.rsqrt(jnp.mean(values * values, axis=-1, keepdims=True) + EPSILON)


def rotate(values, positions):
    half_width = values.shape[-1] // 2
    frequency = 10000.0 ** (-2.0 * jnp.arange(half_width, dtype=F32) / values.shape[-1])
    angles = positions.astype(F32)[:, None] * frequency[None, :]
    if values.ndim == 3:
        angles = angles[:, None, :]
    cosine = jnp.cos(angles)
    sine_part = jnp.sin(angles)
    first_half = values[..., :half_width]
    second = values[..., half_width:]
    return jnp.concatenate(
        [first_half * cosine - second * sine_part, first_half * sine_part + second * cosine],
        axis=-1,
    )


def dot(a, b):
    return jnp.dot(a, b, preferred_element_type=F32)


def local(prompt, block_sizes, w_query_down, w_query, w_latent, w_keys, w_values, w_out):
    sections = lax.axis_size("section")
    section_id = lax.axis_index("section")
    tp_id = lax.axis_index("tp")
    tp_count = lax.axis_size("tp")
    tokens, share_cols = prompt.shape
    share_rows = tokens // tp_count
    down_weight, query_weight, latent_weight = w_query_down[0], w_query[0], w_latent[0]
    key_weight, value_weight, out_weight = w_keys[0], w_values[0], w_out[0]
    down_cols, latent_cols = down_weight.shape[1], latent_weight.shape[1]
    head_count = query_weight.shape[1] // (NOPE_DIM + ROPE_DIM)
    scale_factor = (NOPE_DIM + ROPE_DIM) ** (-0.5)
    all_positions = jnp.arange(tokens, dtype=jnp.int32)
    end_rows = jnp.cumsum(block_sizes) - 1

    def shift(array, distance, routes):
        pairs = [
            (a * tp_count + i, b * tp_count + (i + distance) % tp_count)
            for a, b in routes
            for i in range(tp_count)
        ]
        return lax.ppermute(array, ("section", "tp"), pairs)

    def gather(array, where, axis):
        routes = [(s, s) for s in where]
        width = array.shape[axis]
        shape = list(array.shape)
        shape[axis] = width * tp_count
        whole = jnp.zeros(shape, array.dtype)
        for k in range(tp_count):
            piece = array if k == 0 else shift(array, k, routes)
            whole = lax.dynamic_update_slice_in_dim(
                whole, piece, lax.rem(tp_id - k + tp_count, tp_count) * width, axis
            )
        return whole

    def keys_and_values(cache):
        plain = cache[:, :LATENT]
        keys = dot(plain, key_weight).astype(BF16).reshape(tokens, head_count, NOPE_DIM)
        values = dot(plain, value_weight).astype(BF16).reshape(tokens, head_count, VALUE_DIM)
        return keys, values

    def attend(compressed, positions, cache):
        keys, values = keys_and_values(cache)
        rows = compressed.shape[0]
        queries = dot(compressed, query_weight).reshape(rows, head_count, NOPE_DIM + ROPE_DIM)
        queries = jnp.concatenate(
            [queries[..., :NOPE_DIM], rotate(queries[..., NOPE_DIM:], positions)], axis=-1
        ).astype(BF16)
        scores = jnp.einsum("ihd,jhd->hij", queries[..., :NOPE_DIM], keys, preferred_element_type=F32)
        scores = scores + jnp.einsum(
            "ihr,jr->hij", queries[..., NOPE_DIM:], cache[:, LATENT:], preferred_element_type=F32
        )
        visible = all_positions[None, :] <= positions[:, None]
        powered = jnp.where(visible[None], jnp.exp(scores * scale_factor), 0.0)
        attention = (powered / jnp.sum(powered, axis=-1, keepdims=True)).astype(BF16)
        mixed = jnp.einsum("hij,jhv->ihv", attention, values, preferred_element_type=F32)
        return dot(mixed.astype(BF16).reshape(rows, head_count * VALUE_DIM), out_weight)

    def layer(hidden, own_share, tick):
        normed = rms_rows(hidden.astype(F32)).astype(BF16)
        parts = jnp.concatenate(
            [dot(normed, down_weight).astype(BF16), dot(normed, latent_weight).astype(BF16)], axis=1
        )
        whole = gather(parts[None], [tick], 0).astype(F32)
        down = jnp.concatenate([whole[m, :, :down_cols] for m in range(tp_count)], axis=1)
        latent = jnp.concatenate([whole[m, :, down_cols:] for m in range(tp_count)], axis=1)
        compressed = rms_rows(down).astype(BF16)
        cache = jnp.concatenate(
            [rms_rows(latent[:, :LATENT]), rotate(latent[:, LATENT:], all_positions)], axis=-1
        ).astype(BF16)
        partial = attend(compressed, all_positions, cache)
        start = tp_id * share_cols
        mine = lax.dynamic_slice_in_dim(partial, start, share_cols, 1) + own_share.astype(F32)
        partial = lax.dynamic_update_slice_in_dim(partial, mine, start, 1).astype(BF16)
        return partial, cache

    def pass_on(partial, tick):
        ends = jnp.take(partial, end_rows, axis=0)
        total = 0.0
        for k in range(tp_count):
            first = lax.rem(tp_id + k, tp_count) * share_rows
            block = lax.dynamic_slice_in_dim(partial, first, share_rows, 0)
            block = jnp.concatenate([block, ends], axis=0)
            total = total + shift(block, k, [(tick, tick + 1)]).astype(F32)
        total = total.astype(BF16)
        return total[:share_rows], total[share_rows:]

    own_cache = jnp.zeros((share_rows, LATENT + ROPE_DIM), BF16)
    own_ends = jnp.zeros((block_sizes.shape[0], share_cols), BF16)
    last = sections - 1
    latent_whole = gather(latent_weight, range(1, sections), 1) if last else latent_weight
    hidden, own_share = gather(prompt, [0], 1), prompt
    for tick in range(last):
        partial, cache = layer(hidden, own_share, tick)
        mine = lax.dynamic_slice_in_dim(cache, tp_id * share_rows, share_rows, 0)
        own_cache = jnp.where(section_id == tick, mine, own_cache)
        rows, ends = pass_on(partial, tick)
        ends_share = lax.dynamic_slice_in_dim(ends, tp_id * share_cols, share_cols, 1)
        own_ends = jnp.where(section_id == tick, shift(ends_share, 0, [(tick + 1, tick)]), own_ends)
        if tick + 1 < last:
            hidden = gather(rows, [tick + 1], 0)
            own_share = lax.dynamic_slice_in_dim(hidden, tp_id * share_cols, share_cols, 1)

    row_positions = tp_id * share_rows + jnp.arange(share_rows, dtype=jnp.int32)
    latent = dot(rms_rows(rows.astype(F32)).astype(BF16), latent_whole)
    fresh = jnp.concatenate(
        [rms_rows(latent[:, :LATENT]), rotate(latent[:, LATENT:], row_positions)], axis=-1
    ).astype(BF16)
    own_cache = jnp.where(section_id == last, fresh, own_cache)
    down = dot(rms_rows(ends.astype(F32)).astype(BF16), down_weight).astype(BF16)
    down = jnp.pad(down, ((0, 0), (0, fresh.shape[1] - down_cols)))
    whole = gather(jnp.concatenate([fresh, down], axis=0)[None], [last], 0)
    cache = whole[:, :share_rows].reshape(tokens, LATENT + ROPE_DIM)
    down = jnp.concatenate([whole[m, share_rows:, :down_cols] for m in range(tp_count)], axis=1)
    compressed = rms_rows(down.astype(F32)).astype(BF16)
    partial = attend(compressed, end_rows, cache).astype(BF16)
    total = ends_share.astype(F32)
    for k in range(tp_count):
        start = lax.rem(tp_id + k, tp_count) * share_cols
        block = lax.dynamic_slice_in_dim(partial, start, share_cols, 1)
        total = total + (shift(block, k, [(last, last)]) if k else block).astype(F32)
    own_ends = jnp.where(section_id == last, total.astype(BF16), own_ends)
    return (own_cache[None], own_ends[None])


ROW_WIDTH = LATENT + ROPE_DIM
HEAD_WIDTH = NOPE_DIM + ROPE_DIM
HALF = ROPE_DIM // 2
SMEM = pl.BlockSpec(memory_space=pltpu.SMEM)
VMEM = pl.BlockSpec(memory_space=pltpu.VMEM)
HBM = pl.BlockSpec(memory_space=pltpu.HBM)


def call(kernel, out_shape, args, scratch=(), flops=0, scalars=0, left=0, space=VMEM, grant=8):
    many = isinstance(out_shape, list)
    moved = sum(a.size * a.dtype.itemsize for a in args)
    return pl.pallas_call(
        kernel,
        out_shape=out_shape,
        in_specs=[SMEM] * scalars + [VMEM] * (len(args) - scalars - left) + [HBM] * left,
        out_specs=[space] * len(out_shape) if many else space,
        scratch_shapes=list(scratch),
        compiler_params=pltpu.CompilerParams(vmem_limit_bytes=grant * 2**20),
        cost_estimate=pl.CostEstimate(flops=flops, bytes_accessed=moved, transcendentals=0),
    )(*args)


def dot_t(a, b):
    return lax.dot_general(a, b, (((1,), (1,)), ((), ())), preferred_element_type=F32)


def unit(values):
    return lax.rsqrt(jnp.mean(values * values, axis=-1, keepdims=True) + EPSILON)


def turn(pair, angles):
    cosine, sine = angles[:, :HALF], angles[:, HALF:]
    a, b = pair[:, :HALF], pair[:, HALF:]
    return jnp.concatenate([a * cosine - b * sine, a * sine + b * cosine], axis=1)


def end_rows(sizes):
    ends = [sizes[0] - 1]
    for i in range(1, sizes.shape[0]):
        ends.append(ends[-1] + sizes[i])
    return ends


def column(scalars):
    rows = lax.broadcasted_iota(jnp.int32, (len(scalars), 1), 0)
    out = jnp.zeros((len(scalars), 1), jnp.int32)
    for i, value in enumerate(scalars):
        out = jnp.where(rows == i, value, out)
    return out


def send_kernel(prompt, w_latent, out, other, half, packed, sems):
    section, rep = lax.axis_index("section"), lax.axis_index("rep")
    rows, width = out.shape
    cols, long = half.shape

    @pl.when(section == 0)
    def _():
        copy = pltpu.make_async_copy(prompt, packed.at[0], sems.at[0])
        copy.start()
        copy.wait()
        packed[1] = packed[0]

    @pl.when(section != 0)
    def _():
        columns = pl.ds(pl.multiple_of((rep & 1) * long, 128), long)
        copy = pltpu.make_async_copy(w_latent.at[:, columns], half, sems.at[0])
        copy.start()
        copy.wait()
        rest = jnp.zeros((rows - cols, width), F32)
        for i in range(2):
            piece = half[:, i * width : (i + 1) * width].astype(F32)
            packed[i] = jnp.concatenate([piece, rest], axis=0).astype(BF16)

    copies = [
        pltpu.make_async_copy(packed.at[i], ref, sems.at[i]) for i, ref in enumerate((out, other))
    ]
    for copy in copies:
        copy.start()
    for copy in copies:
        copy.wait()


def down_kernel(own, two, three, one, w_down, w_latent, out):
    section, tp, rep = (lax.axis_index(a) for a in ("section", "tp", "rep"))
    tokens, share = own.shape
    cols, model = w_latent.shape
    third = tokens // 3

    @pl.when(section == 0)
    def _():
        squares, down, latent = 0.0, 0.0, 0.0
        for k, ref in enumerate((own, one, two, three)):
            columns = pl.ds(pl.multiple_of((tp ^ k) * share, 128), share)
            piece = ref[...]
            wide = piece.astype(F32)
            squares = squares + jnp.sum(wide * wide, axis=1, keepdims=True)
            down = down + dot_t(piece, w_down[:, columns])
            latent = latent + dot_t(piece, w_latent[:, columns])
        scale = lax.rsqrt(squares / model + EPSILON)
        parts = jnp.concatenate([down * scale, latent * scale], axis=1)
        rest = parts[:, 256:]
        rest = [rest[i * third : (i + 1) * third] for i in range(3)]
        rest.append(jnp.zeros((third, 256 - 3 * rest[0].shape[1]), F32))
        out[...] = jnp.concatenate([parts[:, :256], jnp.concatenate(rest, axis=1)], axis=0).astype(BF16)

    @pl.when(section != 0)
    def _():
        first = ((rep & 1) + 1) * (model // 2) - 384
        mine = w_latent[:, pl.ds(pl.multiple_of(first, 128), 384)].astype(F32)
        rest = mine[:, 256:]
        high = cols // 2 + 4
        lower = jnp.concatenate([rest[high:], jnp.zeros((2 * high - cols, 128), F32)], axis=0)
        rest = jnp.concatenate([rest[:high], lower], axis=1)
        blank = jnp.zeros((out.shape[0] - cols - high, 256), F32)
        out[...] = jnp.concatenate([mine[:, :256], rest, blank], axis=0).astype(BF16)


def unpack_rest(piece, cols):
    piece = piece.astype(F32)
    high = cols // 2 + 4
    rest = piece[cols : cols + high]
    rest = jnp.concatenate([rest[:, :128], rest[: cols - high, 128:]], axis=0)
    return jnp.concatenate([piece[:cols], rest], axis=1).astype(BF16)


def unpack_parts(piece, tokens, width):
    piece = piece.astype(F32)
    rest, size = piece[tokens:], width - 256
    rest = jnp.concatenate([rest[:, i * size : (i + 1) * size] for i in range(3)], axis=0)
    return jnp.concatenate([piece[:tokens], rest], axis=1)


def attend_rows(compressed, cache, seen, angles, w_query, w_keys, w_values):
    plain, turned = cache[:, :LATENT], cache[:, LATENT:]
    keys = dot(plain, w_keys[...]).astype(BF16)
    values = dot(plain, w_values[...]).astype(BF16)
    queries = dot(compressed, w_query[...])
    mixed = []
    for head in range(queries.shape[1] // HEAD_WIDTH):
        query = queries[:, head * HEAD_WIDTH : (head + 1) * HEAD_WIDTH]
        query = jnp.concatenate(
            [query[:, :NOPE_DIM], turn(query[:, NOPE_DIM:], angles)], axis=1
        ).astype(BF16)
        key = jnp.concatenate([keys[:, head * NOPE_DIM : (head + 1) * NOPE_DIM], turned], axis=1)
        scores = dot_t(query, key) * HEAD_WIDTH**-0.5
        powered = jnp.where(seen, jnp.exp(scores), 0.0)
        attention = (powered / jnp.sum(powered, axis=1, keepdims=True)).astype(BF16)
        mixed.append(dot(attention, values[:, head * VALUE_DIM : (head + 1) * VALUE_DIM]))
    return jnp.concatenate(mixed, axis=1).astype(BF16)


def layer_kernel(
    sizes, own, one, two, three, share1, share3, w_latent, prompt, angles,
    w_query, w_keys, w_values, w_out, out0, out1, out2, out3, own_cache, passed, rest, stack, total, cached,
):
    section, tp, rep = (lax.axis_index(a) for a in ("section", "tp", "rep"))
    tokens, width = prompt.shape
    block = tokens // 4
    cols, early = passed.shape[1:]
    down_cols = w_query.shape[0] // 4

    @pl.when(section != 0)
    def _():
        first = (rep & 1) * (early + rest.shape[2])
        passed[0] = w_latent[:, pl.ds(pl.multiple_of(first, 128), early)]
        passed[1, :, :width] = share3[:cols, :]
        passed[1, :, width:] = share1[:cols, : early - width]
        rest[0] = unpack_rest(two[...], cols)
        rest[1] = unpack_rest(three[...], cols)

    @pl.when(section == 0)
    def _():
        ends = column(end_rows(sizes))
        for k, ref in enumerate((own, one, two, three)):
            stack[tp ^ k] = ref[...]
        pieces = [unpack_parts(stack[m], tokens, down_cols + cols) for m in range(4)]
        down = jnp.concatenate([p[:, :down_cols] for p in pieces], axis=1)
        latent = jnp.concatenate([p[:, down_cols:] for p in pieces], axis=1)
        compressed = (down * unit(down)).astype(BF16)
        plain = latent[:, :LATENT]
        cache = jnp.concatenate(
            [plain * unit(plain), turn(latent[:, LATENT:], angles[...])], axis=1
        ).astype(BF16)
        cached[...] = cache
        own_cache[...] = cached[pl.ds(pl.multiple_of(tp * block, block), block), :]
        seen = lax.broadcasted_iota(jnp.int32, (tokens, tokens), 0) >= lax.broadcasted_iota(
            jnp.int32, (tokens, tokens), 1
        )
        mixed = attend_rows(compressed, cache, seen, angles[...], w_query, w_keys, w_values)
        chosen = lax.broadcasted_iota(jnp.int32, (ends.shape[0], tokens), 1) == ends
        chosen = chosen.astype(BF16)
        rows = jnp.concatenate([mixed, dot(chosen, mixed).astype(BF16)], axis=0)
        total[...] = dot(rows, w_out[...])
        mine = pl.ds(pl.multiple_of(tp * width, 128), width)
        added = jnp.concatenate([prompt[...].astype(F32), dot(chosen, prompt[...])], axis=0)
        total[:, mine] += added
        last = total[tokens:, :]
        for k, out in enumerate((out0, out1, out2, out3)):
            part = total[pl.ds(pl.multiple_of((tp ^ k) * block, block), block), :]
            out[...] = jnp.concatenate([part, last], axis=0).astype(BF16)


def latent_kernel(
    one, two, three, four, angles, w_latent, share3, share1, near3, near1, passed, near_two, near_three,
    rest, near_rest, w_down, out, own_cache, own_ends, hidden, parts,
):
    tp, rep = lax.axis_index("tp"), lax.axis_index("rep")
    block = angles.shape[0] // 4
    width = own_ends.shape[1]
    cols, model = w_latent.shape
    early = passed.shape[2]
    rows = one[...].astype(F32) + two[...].astype(F32) + three[...].astype(F32) + four[...].astype(F32)
    narrow = rows.astype(BF16)
    rows = narrow.astype(F32)
    hidden[...] = rows
    scale = unit(rows)
    parts[tp] = dot_t(narrow[:block], w_latent[...])
    sums = [0.0, 0.0, 0.0]
    for core, (lower, upper, from_two, from_three, late) in enumerate(
        ((share3, share1, passed.at[0], passed.at[1], rest), (near3, near1, near_two, near_three, near_rest))
    ):
        first = ((rep & 1) ^ core) * (model // 2)

        def piece(start, size):
            columns = pl.ds(pl.multiple_of(first + start, 128), size)
            return hidden[0:block, columns].astype(BF16)

        sums[0] += dot_t(piece(0, width), lower[:cols, :]) + dot_t(piece(width, width), upper[:cols, :])
        head, tail = piece(0, early), piece(early, model // 2 - early)
        sums[1] += dot_t(head, from_two[...]) + dot_t(tail, late[0])
        sums[2] += dot_t(head, from_three[...]) + dot_t(tail, late[1])
    for k, value in enumerate(sums):
        parts[tp ^ (k + 1)] = value
    latent = jnp.concatenate([parts[m] for m in range(4)], axis=1) * scale[:block]
    plain = latent[:, :LATENT]
    plain = plain * unit(plain)
    own_angles = angles[pl.ds(pl.multiple_of(tp * block, block), block), :]
    turned = turn(latent[:, LATENT:], own_angles)
    own_cache[...] = jnp.concatenate([plain, turned], axis=1).astype(BF16)
    down = dot_t(narrow[block:, :], w_down[...]) * scale[block:]
    count = down.shape[0]
    turned = [turned[i * count : (i + 1) * count] for i in range(block // count)]
    last = jnp.concatenate([*turned, down], axis=1)
    last = jnp.concatenate([last, jnp.zeros((count, LATENT - last.shape[1]), F32)], axis=1)
    out[...] = jnp.concatenate([plain, last], axis=0).astype(BF16)
    mine = pl.ds(pl.multiple_of(tp * width, 128), width)
    own_ends[...] = hidden[block:, mine].astype(BF16)


def ends_kernel(
    sizes, own, one, two, three, angles, w_query, w_keys, w_values, w_out,
    out0, out1, out2, out3, stack, total,
):
    tp = lax.axis_index("tp")
    ends = end_rows(sizes)
    count = len(ends)
    block = own.shape[0] - count
    steps = block // count
    down_cols = w_query.shape[0] // 4
    width = out0.shape[1]
    for k, ref in enumerate((own, one, two, three)):
        stack[tp ^ k] = ref[...].astype(F32)
    pieces = [stack[m] for m in range(4)]
    plain = jnp.concatenate([p[:block] for p in pieces], axis=0)
    last = [p[block:] for p in pieces]
    turned = jnp.concatenate(
        [p[:, i * ROPE_DIM : (i + 1) * ROPE_DIM] for p in last for i in range(steps)], axis=0
    )
    cache = jnp.concatenate([plain, turned], axis=1).astype(BF16)
    first = steps * ROPE_DIM
    down = jnp.concatenate([p[:, first : first + down_cols] for p in last], axis=1)
    compressed = (down * unit(down)).astype(BF16)
    end_angles = jnp.concatenate([angles[pl.ds(e, 1), :] for e in ends], axis=0)
    seen = lax.broadcasted_iota(jnp.int32, (count, 4 * block), 1) <= column(ends)
    mixed = attend_rows(compressed, cache, seen, end_angles, w_query, w_keys, w_values)
    total[...] = dot(mixed, w_out[...])
    for k, out in enumerate((out0, out1, out2, out3)):
        columns = pl.ds(pl.multiple_of((tp ^ k) * width, 128), width)
        out[...] = total[:, columns].astype(BF16)


def local_two(prompt, block_sizes, w_query_down, w_query, w_latent, w_keys, w_values, w_out):
    section = lax.axis_index("section")
    tokens, share = prompt.shape
    block = tokens // 4
    count = block_sizes.shape[0]
    w_down, w_up, w_lat = w_query_down[0].T, w_query[0], w_latent[0].T
    w_key, w_value, w_final = w_keys[0], w_values[0], w_out[0]
    down_cols, latent_cols = w_down.shape[0], w_lat.shape[0]
    model = 4 * share
    frequency = 10000.0 ** (-2.0 * np.arange(HALF, dtype=np.float32) / ROPE_DIM)
    angles = np.arange(tokens, dtype=np.float32)[:, None] * frequency.astype(np.float32)[None, :]
    angles = jnp.asarray(np.concatenate([np.cos(angles), np.sin(angles)], axis=1), F32)

    def route(array, *ways):
        pairs = [
            (s * 4 + i, way[0] * 4 + (i ^ way[1])) for s, way in enumerate(ways) if way for i in range(4)
        ]
        return lax.ppermute(array, ("section", "tp"), pairs)

    def within(array, k):
        return route(array, (0, k), (1, k))

    def onward(array, k):
        return route(array, (1, k), (0, 0))

    def over_rep(array, k):
        return lax.ppermute(array, "rep", [(i, i ^ k) for i in range(4)])

    sent = call(
        send_kernel,
        [jax.ShapeDtypeStruct((tokens, share), BF16)] * 2,
        [prompt, w_lat],
        [
            pltpu.VMEM((latent_cols, model // 2), BF16),
            pltpu.VMEM((2, tokens, share), BF16),
            pltpu.SemaphoreType.DMA((2,)),
        ],
        left=2,
        space=HBM,
        grant=57,
        flops=2 * 10**10,
    )
    two = route(prompt, (1, 0), (0, 2))
    three = route(sent[0], (0, 3), (1, 1))
    one = route(sent[1], (0, 1), (1, 1))
    parts = call(
        down_kernel,
        jax.ShapeDtypeStruct((tokens + tokens // 3, 256), BF16),
        [prompt, two, three, one, w_down, w_lat],
        flops=2 * 10**10,
    )
    pieces = [parts] + [within(parts, k) for k in (1, 2, 3)]
    near = [over_rep(three, 1), over_rep(one, 1)]

    message = jax.ShapeDtypeStruct((block + count, model), BF16)
    *blocks, first_cache, passed, rest = call(
        layer_kernel,
        [message] * 4
        + [
            jax.ShapeDtypeStruct((block, ROW_WIDTH), BF16),
            jax.ShapeDtypeStruct((2, latent_cols, model // 2 - 384), BF16),
            jax.ShapeDtypeStruct((2, latent_cols, 384), BF16),
        ],
        [block_sizes, *pieces, one, three, w_lat, prompt, angles, w_up, w_key, w_value, w_final],
        [
            pltpu.VMEM((4, *parts.shape), BF16),
            pltpu.VMEM((tokens + count, model), F32),
            pltpu.VMEM((tokens, ROW_WIDTH), BF16),
        ],
        flops=2 * tokens * (w_up.size + w_key.size + w_value.size + w_final.size),
        scalars=1,
        grant=16,
    )
    arrived = [onward(blocks[k], k) for k in (3, 2, 1, 0)]
    passed = route(passed, None, (1, 2))
    near += [passed, over_rep(passed[0], 1), over_rep(passed[1], 1), rest, over_rep(rest, 1)]
    fresh, last_cache, ends_share = call(
        latent_kernel,
        [
            jax.ShapeDtypeStruct((block + count, LATENT), BF16),
            jax.ShapeDtypeStruct((block, ROW_WIDTH), BF16),
            jax.ShapeDtypeStruct((count, share), BF16),
        ],
        [*arrived, angles, w_lat, three, one, *near, w_down],
        [pltpu.VMEM((block + count, model), F32), pltpu.VMEM((4, block, latent_cols), F32)],
        flops=2 * 10**11,
    )
    pieces = [fresh] + [within(fresh, k) for k in (1, 2, 3)]
    first_ends = onward(ends_share, 0)
    outs = call(
        ends_kernel,
        [jax.ShapeDtypeStruct((count, share), BF16)] * 4,
        [block_sizes, *pieces, angles, w_up, w_key, w_value, w_final],
        [
            pltpu.VMEM((4, block + count, LATENT), F32),
            pltpu.VMEM((count, model), F32),
        ],
        flops=2 * tokens * (w_key.size + w_value.size),
        scalars=1,
    )
    total = ends_share.astype(F32) + outs[0].astype(F32)
    for k in (1, 2, 3):
        total = total + within(outs[k], k).astype(F32)
    own_ends = jnp.where(section == 0, first_ends, total.astype(BF16))
    own_cache = jnp.where(section == 0, first_cache, last_cache)
    return (own_cache[None], own_ends[None])


def solution(mesh):
    sizes = [mesh.shape[a] for a in ("section", "tp", "rep")]
    body = local_two if sizes == [2, 4, 4] else local
    in_specs = (
        P("rep", "tp"),
        P("rep"),
        P("section", None, "tp"),
        P("section", None, "tp"),
        P("section", None, "tp"),
        P("section", None, "tp"),
        P("section", None, "tp"),
        P("section", "tp", None),
    )
    out_specs = (P("section", ("rep", "tp"), None), P("section", "rep", "tp"))
    return jax.shard_map(body, mesh=mesh, in_specs=in_specs, out_specs=out_specs, check_vma=False)
```

```python
import jax
import jax.numpy as jnp
import numpy as np
from jax import lax
from jax.experimental import pallas as pl
from jax.experimental.pallas import tpu as pltpu
from jax.sharding import PartitionSpec as P

NOPE_DIM = 128
ROPE_DIM = 32
VALUE_DIM = 128
LATENT = 512
EPSILON = 1e-06
F32 = jnp.float32
BF16 = jnp.bfloat16


def rms_rows(values):
    return values * lax.rsqrt(jnp.mean(values * values, axis=-1, keepdims=True) + EPSILON)


def rotate(values, positions):
    half_width = values.shape[-1] // 2
    frequency = 10000.0 ** (-2.0 * jnp.arange(half_width, dtype=F32) / values.shape[-1])
    angles = positions.astype(F32)[:, None] * frequency[None, :]
    if values.ndim == 3:
        angles = angles[:, None, :]
    cosine = jnp.cos(angles)
    sine_part = jnp.sin(angles)
    first_half = values[..., :half_width]
    second = values[..., half_width:]
    return jnp.concatenate(
        [first_half * cosine - second * sine_part, first_half * sine_part + second * cosine],
        axis=-1,
    )


def dot(a, b):
    return jnp.dot(a, b, preferred_element_type=F32)


def local(prompt, block_sizes, w_query_down, w_query, w_latent, w_keys, w_values, w_out):
    sections = lax.axis_size("section")
    section_id = lax.axis_index("section")
    tp_id = lax.axis_index("tp")
    tp_count = lax.axis_size("tp")
    tokens, share_cols = prompt.shape
    share_rows = tokens // tp_count
    down_weight, query_weight, latent_weight = w_query_down[0], w_query[0], w_latent[0]
    key_weight, value_weight, out_weight = w_keys[0], w_values[0], w_out[0]
    down_cols, latent_cols = down_weight.shape[1], latent_weight.shape[1]
    head_count = query_weight.shape[1] // (NOPE_DIM + ROPE_DIM)
    scale_factor = (NOPE_DIM + ROPE_DIM) ** (-0.5)
    all_positions = jnp.arange(tokens, dtype=jnp.int32)
    end_rows = jnp.cumsum(block_sizes) - 1

    def shift(array, distance, routes):
        pairs = [
            (a * tp_count + i, b * tp_count + (i + distance) % tp_count)
            for a, b in routes
            for i in range(tp_count)
        ]
        return lax.ppermute(array, ("section", "tp"), pairs)

    def gather(array, where, axis):
        routes = [(s, s) for s in where]
        width = array.shape[axis]
        shape = list(array.shape)
        shape[axis] = width * tp_count
        whole = jnp.zeros(shape, array.dtype)
        for k in range(tp_count):
            piece = array if k == 0 else shift(array, k, routes)
            whole = lax.dynamic_update_slice_in_dim(
                whole, piece, lax.rem(tp_id - k + tp_count, tp_count) * width, axis
            )
        return whole

    def keys_and_values(cache):
        plain = cache[:, :LATENT]
        keys = dot(plain, key_weight).astype(BF16).reshape(tokens, head_count, NOPE_DIM)
        values = dot(plain, value_weight).astype(BF16).reshape(tokens, head_count, VALUE_DIM)
        return keys, values

    def attend(compressed, positions, cache):
        keys, values = keys_and_values(cache)
        rows = compressed.shape[0]
        queries = dot(compressed, query_weight).reshape(rows, head_count, NOPE_DIM + ROPE_DIM)
        queries = jnp.concatenate(
            [queries[..., :NOPE_DIM], rotate(queries[..., NOPE_DIM:], positions)], axis=-1
        ).astype(BF16)
        scores = jnp.einsum("ihd,jhd->hij", queries[..., :NOPE_DIM], keys, preferred_element_type=F32)
        scores = scores + jnp.einsum(
            "ihr,jr->hij", queries[..., NOPE_DIM:], cache[:, LATENT:], preferred_element_type=F32
        )
        visible = all_positions[None, :] <= positions[:, None]
        powered = jnp.where(visible[None], jnp.exp(scores * scale_factor), 0.0)
        attention = (powered / jnp.sum(powered, axis=-1, keepdims=True)).astype(BF16)
        mixed = jnp.einsum("hij,jhv->ihv", attention, values, preferred_element_type=F32)
        return dot(mixed.astype(BF16).reshape(rows, head_count * VALUE_DIM), out_weight)

    def layer(hidden, own_share, tick):
        normed = rms_rows(hidden.astype(F32)).astype(BF16)
        parts = jnp.concatenate(
            [dot(normed, down_weight).astype(BF16), dot(normed, latent_weight).astype(BF16)], axis=1
        )
        whole = gather(parts[None], [tick], 0).astype(F32)
        down = jnp.concatenate([whole[m, :, :down_cols] for m in range(tp_count)], axis=1)
        latent = jnp.concatenate([whole[m, :, down_cols:] for m in range(tp_count)], axis=1)
        compressed = rms_rows(down).astype(BF16)
        cache = jnp.concatenate(
            [rms_rows(latent[:, :LATENT]), rotate(latent[:, LATENT:], all_positions)], axis=-1
        ).astype(BF16)
        partial = attend(compressed, all_positions, cache)
        start = tp_id * share_cols
        mine = lax.dynamic_slice_in_dim(partial, start, share_cols, 1) + own_share.astype(F32)
        partial = lax.dynamic_update_slice_in_dim(partial, mine, start, 1).astype(BF16)
        return partial, cache

    def pass_on(partial, tick):
        ends = jnp.take(partial, end_rows, axis=0)
        total = 0.0
        for k in range(tp_count):
            first = lax.rem(tp_id + k, tp_count) * share_rows
            block = lax.dynamic_slice_in_dim(partial, first, share_rows, 0)
            block = jnp.concatenate([block, ends], axis=0)
            total = total + shift(block, k, [(tick, tick + 1)]).astype(F32)
        total = total.astype(BF16)
        return total[:share_rows], total[share_rows:]

    own_cache = jnp.zeros((share_rows, LATENT + ROPE_DIM), BF16)
    own_ends = jnp.zeros((block_sizes.shape[0], share_cols), BF16)
    last = sections - 1
    latent_whole = gather(latent_weight, range(1, sections), 1) if last else latent_weight
    hidden, own_share = gather(prompt, [0], 1), prompt
    for tick in range(last):
        partial, cache = layer(hidden, own_share, tick)
        mine = lax.dynamic_slice_in_dim(cache, tp_id * share_rows, share_rows, 0)
        own_cache = jnp.where(section_id == tick, mine, own_cache)
        rows, ends = pass_on(partial, tick)
        ends_share = lax.dynamic_slice_in_dim(ends, tp_id * share_cols, share_cols, 1)
        own_ends = jnp.where(section_id == tick, shift(ends_share, 0, [(tick + 1, tick)]), own_ends)
        if tick + 1 < last:
            hidden = gather(rows, [tick + 1], 0)
            own_share = lax.dynamic_slice_in_dim(hidden, tp_id * share_cols, share_cols, 1)

    row_positions = tp_id * share_rows + jnp.arange(share_rows, dtype=jnp.int32)
    latent = dot(rms_rows(rows.astype(F32)).astype(BF16), latent_whole)
    fresh = jnp.concatenate(
        [rms_rows(latent[:, :LATENT]), rotate(latent[:, LATENT:], row_positions)], axis=-1
    ).astype(BF16)
    own_cache = jnp.where(section_id == last, fresh, own_cache)
    down = dot(rms_rows(ends.astype(F32)).astype(BF16), down_weight).astype(BF16)
    down = jnp.pad(down, ((0, 0), (0, fresh.shape[1] - down_cols)))
    whole = gather(jnp.concatenate([fresh, down], axis=0)[None], [last], 0)
    cache = whole[:, :share_rows].reshape(tokens, LATENT + ROPE_DIM)
    down = jnp.concatenate([whole[m, share_rows:, :down_cols] for m in range(tp_count)], axis=1)
    compressed = rms_rows(down.astype(F32)).astype(BF16)
    partial = attend(compressed, end_rows, cache).astype(BF16)
    total = ends_share.astype(F32)
    for k in range(tp_count):
        start = lax.rem(tp_id + k, tp_count) * share_cols
        block = lax.dynamic_slice_in_dim(partial, start, share_cols, 1)
        total = total + (shift(block, k, [(last, last)]) if k else block).astype(F32)
    own_ends = jnp.where(section_id == last, total.astype(BF16), own_ends)
    return (own_cache[None], own_ends[None])


ROW_WIDTH = LATENT + ROPE_DIM
HEAD_WIDTH = NOPE_DIM + ROPE_DIM
HALF = ROPE_DIM // 2
SMEM = pl.BlockSpec(memory_space=pltpu.SMEM)
VMEM = pl.BlockSpec(memory_space=pltpu.VMEM)
HBM = pl.BlockSpec(memory_space=pltpu.HBM)


def call(kernel, out_shape, args, scratch=(), flops=0, scalars=0, left=0, space=VMEM, grant=8):
    many = isinstance(out_shape, list)
    moved = sum(a.size * a.dtype.itemsize for a in args)
    return pl.pallas_call(
        kernel,
        out_shape=out_shape,
        in_specs=[SMEM] * scalars + [VMEM] * (len(args) - scalars - left) + [HBM] * left,
        out_specs=[space] * len(out_shape) if many else space,
        scratch_shapes=list(scratch),
        compiler_params=pltpu.CompilerParams(vmem_limit_bytes=grant * 2**20),
        cost_estimate=pl.CostEstimate(flops=flops, bytes_accessed=moved, transcendentals=0),
    )(*args)


def dot_t(a, b):
    return lax.dot_general(a, b, (((1,), (1,)), ((), ())), preferred_element_type=F32)


def unit(values):
    return lax.rsqrt(jnp.mean(values * values, axis=-1, keepdims=True) + EPSILON)


def turn(pair, angles):
    cosine, sine = angles[:, :HALF], angles[:, HALF:]
    a, b = pair[:, :HALF], pair[:, HALF:]
    return jnp.concatenate([a * cosine - b * sine, a * sine + b * cosine], axis=1)


def end_rows(sizes):
    ends = [sizes[0] - 1]
    for i in range(1, sizes.shape[0]):
        ends.append(ends[-1] + sizes[i])
    return ends


def column(scalars):
    rows = lax.broadcasted_iota(jnp.int32, (len(scalars), 1), 0)
    out = jnp.zeros((len(scalars), 1), jnp.int32)
    for i, value in enumerate(scalars):
        out = jnp.where(rows == i, value, out)
    return out


def send_kernel(prompt, w_latent, out, half, packed, sem):
    section, rep = lax.axis_index("section"), lax.axis_index("rep")
    rows, width = out.shape
    cols, long = half.shape

    @pl.when(section == 0)
    def _():
        copy = pltpu.make_async_copy(prompt, packed, sem)
        copy.start()
        copy.wait()

    @pl.when(section != 0)
    def _():
        columns = pl.ds(pl.multiple_of((rep & 1) * long, 128), long)
        copy = pltpu.make_async_copy(w_latent.at[:, columns], half, sem)
        copy.start()
        copy.wait()
        extra = half[:, width : width + 256].astype(F32)
        free = rows - cols
        left = cols - 2 * free
        tail = [extra[2 * free :, :128], extra[2 * free :, 128:], jnp.zeros((free - 2 * left, 128), F32)]
        extra = jnp.concatenate(
            [extra[:free], extra[free : 2 * free], jnp.concatenate(tail, axis=0)], axis=1
        )
        whole = jnp.concatenate([half[:, :width].astype(F32), extra], axis=0)
        packed[...] = whole.astype(BF16)

    copy = pltpu.make_async_copy(packed, out, sem)
    copy.start()
    copy.wait()


def unpack_share(share, cols):
    share = share.astype(F32)
    free = share.shape[0] - cols
    left = cols - 2 * free
    extra, tail = share[cols:, :512], share[cols:, 512:]
    tail = jnp.concatenate([tail[:left], tail[left : 2 * left]], axis=1)
    extra = jnp.concatenate([extra[:, :256], extra[:, 256:], tail], axis=0)
    return jnp.concatenate([share[:cols], extra], axis=1).astype(BF16)


def down_kernel(own, two, three, one, w_down, w_latent, out):
    section, tp, rep = (lax.axis_index(a) for a in ("section", "tp", "rep"))
    tokens, share = own.shape
    cols, model = w_latent.shape
    third = tokens // 3

    @pl.when(section == 0)
    def _():
        squares, down, latent = 0.0, 0.0, 0.0
        for k, ref in enumerate((own, one, two, three)):
            columns = pl.ds(pl.multiple_of((tp ^ k) * share, 128), share)
            piece = ref[...]
            wide = piece.astype(F32)
            squares = squares + jnp.sum(wide * wide, axis=1, keepdims=True)
            down = down + dot_t(piece, w_down[:, columns])
            latent = latent + dot_t(piece, w_latent[:, columns])
        scale = lax.rsqrt(squares / model + EPSILON)
        parts = jnp.concatenate([down * scale, latent * scale], axis=1)
        rest = parts[:, 256:]
        rest = [rest[i * third : (i + 1) * third] for i in range(3)]
        rest.append(jnp.zeros((third, 256 - 3 * rest[0].shape[1]), F32))
        out[...] = jnp.concatenate([parts[:, :256], jnp.concatenate(rest, axis=1)], axis=0).astype(BF16)

    @pl.when(section != 0)
    def _():
        first = ((rep & 1) + 1) * (model // 2) - 384
        mine = w_latent[:, pl.ds(pl.multiple_of(first, 128), 384)].astype(F32)
        rest = mine[:, 256:]
        high = cols // 2 + 4
        lower = jnp.concatenate([rest[high:], jnp.zeros((2 * high - cols, 128), F32)], axis=0)
        rest = jnp.concatenate([rest[:high], lower], axis=1)
        blank = jnp.zeros((out.shape[0] - cols - high, 256), F32)
        out[...] = jnp.concatenate([mine[:, :256], rest, blank], axis=0).astype(BF16)


def unpack_rest(piece, cols):
    piece = piece.astype(F32)
    high = cols // 2 + 4
    rest = piece[cols : cols + high]
    rest = jnp.concatenate([rest[:, :128], rest[: cols - high, 128:]], axis=0)
    return jnp.concatenate([piece[:cols], rest], axis=1).astype(BF16)


def unpack_parts(piece, tokens, width):
    piece = piece.astype(F32)
    rest, size = piece[tokens:], width - 256
    rest = jnp.concatenate([rest[:, i * size : (i + 1) * size] for i in range(3)], axis=0)
    return jnp.concatenate([piece[:tokens], rest], axis=1)


def attend_rows(compressed, cache, seen, angles, w_query, w_keys, w_values):
    plain, turned = cache[:, :LATENT], cache[:, LATENT:]
    keys = dot(plain, w_keys[...]).astype(BF16)
    values = dot(plain, w_values[...]).astype(BF16)
    queries = dot(compressed, w_query[...])
    mixed = []
    for head in range(queries.shape[1] // HEAD_WIDTH):
        query = queries[:, head * HEAD_WIDTH : (head + 1) * HEAD_WIDTH]
        query = jnp.concatenate(
            [query[:, :NOPE_DIM], turn(query[:, NOPE_DIM:], angles)], axis=1
        ).astype(BF16)
        key = jnp.concatenate([keys[:, head * NOPE_DIM : (head + 1) * NOPE_DIM], turned], axis=1)
        scores = dot_t(query, key) * HEAD_WIDTH**-0.5
        powered = jnp.where(seen, jnp.exp(scores), 0.0)
        attention = (powered / jnp.sum(powered, axis=1, keepdims=True)).astype(BF16)
        mixed.append(dot(attention, values[:, head * VALUE_DIM : (head + 1) * VALUE_DIM]))
    return jnp.concatenate(mixed, axis=1).astype(BF16)


def layer_kernel(
    sizes, own, one, two, three, share1, w_latent, prompt, angles,
    w_query, w_keys, w_values, w_out, out0, out1, out2, out3, own_cache, passed, rest, stack, total, cached,
):
    section, tp, rep = (lax.axis_index(a) for a in ("section", "tp", "rep"))
    tokens, width = prompt.shape
    block = tokens // 4
    cols, early = passed.shape[1:]
    down_cols = w_query.shape[0] // 4

    @pl.when(section != 0)
    def _():
        first = (rep & 1) * (early + rest.shape[2])
        passed[0] = w_latent[:, pl.ds(pl.multiple_of(first, 128), early)]
        passed[1] = unpack_share(share1[...], cols)
        for k, ref in enumerate((one, two, three)):
            rest[k] = unpack_rest(ref[...], cols)

    @pl.when(section == 0)
    def _():
        ends = column(end_rows(sizes))
        for k, ref in enumerate((own, one, two, three)):
            stack[tp ^ k] = ref[...]
        pieces = [unpack_parts(stack[m], tokens, down_cols + cols) for m in range(4)]
        down = jnp.concatenate([p[:, :down_cols] for p in pieces], axis=1)
        latent = jnp.concatenate([p[:, down_cols:] for p in pieces], axis=1)
        compressed = (down * unit(down)).astype(BF16)
        plain = latent[:, :LATENT]
        cache = jnp.concatenate(
            [plain * unit(plain), turn(latent[:, LATENT:], angles[...])], axis=1
        ).astype(BF16)
        cached[...] = cache
        own_cache[...] = cached[pl.ds(pl.multiple_of(tp * block, block), block), :]
        seen = lax.broadcasted_iota(jnp.int32, (tokens, tokens), 0) >= lax.broadcasted_iota(
            jnp.int32, (tokens, tokens), 1
        )
        mixed = attend_rows(compressed, cache, seen, angles[...], w_query, w_keys, w_values)
        chosen = lax.broadcasted_iota(jnp.int32, (ends.shape[0], tokens), 1) == ends
        chosen = chosen.astype(BF16)
        rows = jnp.concatenate([mixed, dot(chosen, mixed).astype(BF16)], axis=0)
        total[...] = dot(rows, w_out[...])
        mine = pl.ds(pl.multiple_of(tp * width, 128), width)
        added = jnp.concatenate([prompt[...].astype(F32), dot(chosen, prompt[...])], axis=0)
        total[:, mine] += added
        last = total[tokens:, :]
        for k, out in enumerate((out0, out1, out2, out3)):
            part = total[pl.ds(pl.multiple_of((tp ^ k) * block, block), block), :]
            out[...] = jnp.concatenate([part, last], axis=0).astype(BF16)


def latent_kernel(
    one, two, three, four, angles, w_latent, first1, first2, first3, rest,
    near1, near2, near3, near_rest, w_down, out, own_cache, own_ends, hidden, parts,
):
    tp, rep = lax.axis_index("tp"), lax.axis_index("rep")
    block = angles.shape[0] // 4
    width = own_ends.shape[1]
    model = w_latent.shape[1]
    early = first1.shape[1]
    rows = one[...].astype(F32) + two[...].astype(F32) + three[...].astype(F32) + four[...].astype(F32)
    narrow = rows.astype(BF16)
    rows = narrow.astype(F32)
    hidden[...] = rows
    scale = unit(rows)
    parts[tp] = dot_t(narrow[:block], w_latent[...])
    sums = [0.0, 0.0, 0.0]
    for core, weights in enumerate(
        (
            (first1, first2, first3, rest),
            (near1, near2, near3, near_rest),
        )
    ):
        first = ((rep & 1) ^ core) * (model // 2)
        head = hidden[0:block, pl.ds(pl.multiple_of(first, 128), early)].astype(BF16)
        late = pl.ds(pl.multiple_of(first + early, 128), model // 2 - early)
        tail = hidden[0:block, late].astype(BF16)
        for k in range(3):
            sums[k] += dot_t(head, weights[k][...]) + dot_t(tail, weights[3][k])
    for k, value in enumerate(sums):
        parts[tp ^ (k + 1)] = value
    latent = jnp.concatenate([parts[m] for m in range(4)], axis=1) * scale[:block]
    plain = latent[:, :LATENT]
    plain = plain * unit(plain)
    own_angles = angles[pl.ds(pl.multiple_of(tp * block, block), block), :]
    turned = turn(latent[:, LATENT:], own_angles)
    own_cache[...] = jnp.concatenate([plain, turned], axis=1).astype(BF16)
    down = dot_t(narrow[block:, :], w_down[...]) * scale[block:]
    count = down.shape[0]
    turned = [turned[i * count : (i + 1) * count] for i in range(block // count)]
    last = jnp.concatenate([*turned, down], axis=1)
    last = jnp.concatenate([last, jnp.zeros((count, LATENT - last.shape[1]), F32)], axis=1)
    out[...] = jnp.concatenate([plain, last], axis=0).astype(BF16)
    mine = pl.ds(pl.multiple_of(tp * width, 128), width)
    own_ends[...] = hidden[block:, mine].astype(BF16)


def ends_kernel(
    sizes, own, one, two, three, angles, w_query, w_keys, w_values, w_out,
    out0, out1, out2, out3, stack, total,
):
    tp = lax.axis_index("tp")
    ends = end_rows(sizes)
    count = len(ends)
    block = own.shape[0] - count
    steps = block // count
    down_cols = w_query.shape[0] // 4
    width = out0.shape[1]
    for k, ref in enumerate((own, one, two, three)):
        stack[tp ^ k] = ref[...].astype(F32)
    pieces = [stack[m] for m in range(4)]
    plain = jnp.concatenate([p[:block] for p in pieces], axis=0)
    last = [p[block:] for p in pieces]
    turned = jnp.concatenate(
        [p[:, i * ROPE_DIM : (i + 1) * ROPE_DIM] for p in last for i in range(steps)], axis=0
    )
    cache = jnp.concatenate([plain, turned], axis=1).astype(BF16)
    first = steps * ROPE_DIM
    down = jnp.concatenate([p[:, first : first + down_cols] for p in last], axis=1)
    compressed = (down * unit(down)).astype(BF16)
    end_angles = jnp.concatenate([angles[pl.ds(e, 1), :] for e in ends], axis=0)
    seen = lax.broadcasted_iota(jnp.int32, (count, 4 * block), 1) <= column(ends)
    mixed = attend_rows(compressed, cache, seen, end_angles, w_query, w_keys, w_values)
    total[...] = dot(mixed, w_out[...])
    for k, out in enumerate((out0, out1, out2, out3)):
        columns = pl.ds(pl.multiple_of((tp ^ k) * width, 128), width)
        out[...] = total[:, columns].astype(BF16)


def local_two(prompt, block_sizes, w_query_down, w_query, w_latent, w_keys, w_values, w_out):
    section = lax.axis_index("section")
    tokens, share = prompt.shape
    block = tokens // 4
    count = block_sizes.shape[0]
    w_down, w_up, w_lat = w_query_down[0].T, w_query[0], w_latent[0].T
    w_key, w_value, w_final = w_keys[0], w_values[0], w_out[0]
    down_cols, latent_cols = w_down.shape[0], w_lat.shape[0]
    model = 4 * share
    frequency = 10000.0 ** (-2.0 * np.arange(HALF, dtype=np.float32) / ROPE_DIM)
    angles = np.arange(tokens, dtype=np.float32)[:, None] * frequency.astype(np.float32)[None, :]
    angles = jnp.asarray(np.concatenate([np.cos(angles), np.sin(angles)], axis=1), F32)

    def route(array, *ways):
        pairs = [
            (s * 4 + i, way[0] * 4 + (i ^ way[1])) for s, way in enumerate(ways) if way for i in range(4)
        ]
        return lax.ppermute(array, ("section", "tp"), pairs)

    def within(array, k):
        return route(array, (0, k), (1, k))

    def onward(array, k):
        return route(array, (1, k), (0, 0))

    def over_rep(array, k):
        return lax.ppermute(array, "rep", [(i, i ^ k) for i in range(4)])

    sent = call(
        send_kernel,
        jax.ShapeDtypeStruct((tokens, share), BF16),
        [prompt, w_lat],
        [
            pltpu.VMEM((latent_cols, model // 2), BF16),
            pltpu.VMEM((tokens, share), BF16),
            pltpu.SemaphoreType.DMA,
        ],
        left=2,
        space=HBM,
        grant=57,
        flops=2 * 10**10,
    )
    two = route(prompt, (1, 0), (0, 2))
    three = route(prompt, (0, 3), (1, 1))
    one = route(sent, (0, 1), (1, 1))
    parts = call(
        down_kernel,
        jax.ShapeDtypeStruct((tokens + tokens // 3, 256), BF16),
        [prompt, two, three, one, w_down, w_lat],
        flops=2 * 10**10,
    )
    pieces = [parts] + [within(parts, k) for k in (1, 2, 3)]

    message = jax.ShapeDtypeStruct((block + count, model), BF16)
    *blocks, first_cache, passed, rest = call(
        layer_kernel,
        [message] * 4
        + [
            jax.ShapeDtypeStruct((block, ROW_WIDTH), BF16),
            jax.ShapeDtypeStruct((2, latent_cols, model // 2 - 384), BF16),
            jax.ShapeDtypeStruct((3, latent_cols, 384), BF16),
        ],
        [block_sizes, *pieces, one, w_lat, prompt, angles, w_up, w_key, w_value, w_final],
        [
            pltpu.VMEM((4, *parts.shape), BF16),
            pltpu.VMEM((tokens + count, model), F32),
            pltpu.VMEM((tokens, ROW_WIDTH), BF16),
        ],
        flops=2 * tokens * (w_up.size + w_key.size + w_value.size + w_final.size),
        scalars=1,
        grant=16,
    )
    arrived = [onward(blocks[k], k) for k in (3, 2, 1, 0)]
    relayed = route(passed, None, (1, 2))
    relayed, late, first = lax.optimization_barrier((relayed, rest, passed[1]))
    weights = [first, relayed[0], relayed[1], late]
    weights += [over_rep(w, 1) for w in weights]
    fresh, last_cache, ends_share = call(
        latent_kernel,
        [
            jax.ShapeDtypeStruct((block + count, LATENT), BF16),
            jax.ShapeDtypeStruct((block, ROW_WIDTH), BF16),
            jax.ShapeDtypeStruct((count, share), BF16),
        ],
        [*arrived, angles, w_lat, *weights, w_down],
        [pltpu.VMEM((block + count, model), F32), pltpu.VMEM((4, block, latent_cols), F32)],
        flops=2 * 10**11,
    )
    pieces = [fresh] + [within(fresh, k) for k in (1, 2, 3)]
    first_ends = onward(ends_share, 0)
    outs = call(
        ends_kernel,
        [jax.ShapeDtypeStruct((count, share), BF16)] * 4,
        [block_sizes, *pieces, angles, w_up, w_key, w_value, w_final],
        [
            pltpu.VMEM((4, block + count, LATENT), F32),
            pltpu.VMEM((count, model), F32),
        ],
        flops=2 * tokens * (w_key.size + w_value.size),
        scalars=1,
    )
    total = ends_share.astype(F32) + outs[0].astype(F32)
    for k in (1, 2, 3):
        total = total + within(outs[k], k).astype(F32)
    own_ends = jnp.where(section == 0, first_ends, total.astype(BF16))
    own_cache = jnp.where(section == 0, first_cache, last_cache)
    return (own_cache[None], own_ends[None])


def solution(mesh):
    sizes = [mesh.shape[a] for a in ("section", "tp", "rep")]
    body = local_two if sizes == [2, 4, 4] else local
    in_specs = (
        P("rep", "tp"),
        P("rep"),
        P("section", None, "tp"),
        P("section", None, "tp"),
        P("section", None, "tp"),
        P("section", None, "tp"),
        P("section", None, "tp"),
        P("section", "tp", None),
    )
    out_specs = (P("section", ("rep", "tp"), None), P("section", "rep", "tp"))
    return jax.shard_map(body, mesh=mesh, in_specs=in_specs, out_specs=out_specs, check_vma=False)
```

```python
import jax
import jax.numpy as jnp
import numpy as np
from jax import lax
from jax.experimental import pallas as pl
from jax.experimental.pallas import tpu as pltpu
from jax.sharding import PartitionSpec as P

NOPE_DIM = 128
ROPE_DIM = 32
VALUE_DIM = 128
LATENT = 512
EPSILON = 1e-06
F32 = jnp.float32
BF16 = jnp.bfloat16


def rms_rows(values):
    return values * lax.rsqrt(jnp.mean(values * values, axis=-1, keepdims=True) + EPSILON)


def rotate(values, positions):
    half_width = values.shape[-1] // 2
    frequency = 10000.0 ** (-2.0 * jnp.arange(half_width, dtype=F32) / values.shape[-1])
    angles = positions.astype(F32)[:, None] * frequency[None, :]
    if values.ndim == 3:
        angles = angles[:, None, :]
    cosine = jnp.cos(angles)
    sine_part = jnp.sin(angles)
    first_half = values[..., :half_width]
    second = values[..., half_width:]
    return jnp.concatenate(
        [first_half * cosine - second * sine_part, first_half * sine_part + second * cosine],
        axis=-1,
    )


def dot(a, b):
    return jnp.dot(a, b, preferred_element_type=F32)


def local(prompt, block_sizes, w_query_down, w_query, w_latent, w_keys, w_values, w_out):
    sections = lax.axis_size("section")
    section_id = lax.axis_index("section")
    tp_id = lax.axis_index("tp")
    tp_count = lax.axis_size("tp")
    tokens, share_cols = prompt.shape
    share_rows = tokens // tp_count
    down_weight, query_weight, latent_weight = w_query_down[0], w_query[0], w_latent[0]
    key_weight, value_weight, out_weight = w_keys[0], w_values[0], w_out[0]
    down_cols, latent_cols = down_weight.shape[1], latent_weight.shape[1]
    head_count = query_weight.shape[1] // (NOPE_DIM + ROPE_DIM)
    scale_factor = (NOPE_DIM + ROPE_DIM) ** (-0.5)
    all_positions = jnp.arange(tokens, dtype=jnp.int32)
    end_rows = jnp.cumsum(block_sizes) - 1

    def shift(array, distance, routes):
        pairs = [
            (a * tp_count + i, b * tp_count + (i + distance) % tp_count)
            for a, b in routes
            for i in range(tp_count)
        ]
        return lax.ppermute(array, ("section", "tp"), pairs)

    def gather(array, where, axis):
        routes = [(s, s) for s in where]
        width = array.shape[axis]
        shape = list(array.shape)
        shape[axis] = width * tp_count
        whole = jnp.zeros(shape, array.dtype)
        for k in range(tp_count):
            piece = array if k == 0 else shift(array, k, routes)
            whole = lax.dynamic_update_slice_in_dim(
                whole, piece, lax.rem(tp_id - k + tp_count, tp_count) * width, axis
            )
        return whole

    def keys_and_values(cache):
        plain = cache[:, :LATENT]
        keys = dot(plain, key_weight).astype(BF16).reshape(tokens, head_count, NOPE_DIM)
        values = dot(plain, value_weight).astype(BF16).reshape(tokens, head_count, VALUE_DIM)
        return keys, values

    def attend(compressed, positions, cache):
        keys, values = keys_and_values(cache)
        rows = compressed.shape[0]
        queries = dot(compressed, query_weight).reshape(rows, head_count, NOPE_DIM + ROPE_DIM)
        queries = jnp.concatenate(
            [queries[..., :NOPE_DIM], rotate(queries[..., NOPE_DIM:], positions)], axis=-1
        ).astype(BF16)
        scores = jnp.einsum("ihd,jhd->hij", queries[..., :NOPE_DIM], keys, preferred_element_type=F32)
        scores = scores + jnp.einsum(
            "ihr,jr->hij", queries[..., NOPE_DIM:], cache[:, LATENT:], preferred_element_type=F32
        )
        visible = all_positions[None, :] <= positions[:, None]
        powered = jnp.where(visible[None], jnp.exp(scores * scale_factor), 0.0)
        attention = (powered / jnp.sum(powered, axis=-1, keepdims=True)).astype(BF16)
        mixed = jnp.einsum("hij,jhv->ihv", attention, values, preferred_element_type=F32)
        return dot(mixed.astype(BF16).reshape(rows, head_count * VALUE_DIM), out_weight)

    def layer(hidden, own_share, tick):
        normed = rms_rows(hidden.astype(F32)).astype(BF16)
        parts = jnp.concatenate(
            [dot(normed, down_weight).astype(BF16), dot(normed, latent_weight).astype(BF16)], axis=1
        )
        whole = gather(parts[None], [tick], 0).astype(F32)
        down = jnp.concatenate([whole[m, :, :down_cols] for m in range(tp_count)], axis=1)
        latent = jnp.concatenate([whole[m, :, down_cols:] for m in range(tp_count)], axis=1)
        compressed = rms_rows(down).astype(BF16)
        cache = jnp.concatenate(
            [rms_rows(latent[:, :LATENT]), rotate(latent[:, LATENT:], all_positions)], axis=-1
        ).astype(BF16)
        partial = attend(compressed, all_positions, cache)
        start = tp_id * share_cols
        mine = lax.dynamic_slice_in_dim(partial, start, share_cols, 1) + own_share.astype(F32)
        partial = lax.dynamic_update_slice_in_dim(partial, mine, start, 1).astype(BF16)
        return partial, cache

    def pass_on(partial, tick):
        ends = jnp.take(partial, end_rows, axis=0)
        total = 0.0
        for k in range(tp_count):
            first = lax.rem(tp_id + k, tp_count) * share_rows
            block = lax.dynamic_slice_in_dim(partial, first, share_rows, 0)
            block = jnp.concatenate([block, ends], axis=0)
            total = total + shift(block, k, [(tick, tick + 1)]).astype(F32)
        total = total.astype(BF16)
        return total[:share_rows], total[share_rows:]

    own_cache = jnp.zeros((share_rows, LATENT + ROPE_DIM), BF16)
    own_ends = jnp.zeros((block_sizes.shape[0], share_cols), BF16)
    last = sections - 1
    latent_whole = gather(latent_weight, range(1, sections), 1) if last else latent_weight
    hidden, own_share = gather(prompt, [0], 1), prompt
    for tick in range(last):
        partial, cache = layer(hidden, own_share, tick)
        mine = lax.dynamic_slice_in_dim(cache, tp_id * share_rows, share_rows, 0)
        own_cache = jnp.where(section_id == tick, mine, own_cache)
        rows, ends = pass_on(partial, tick)
        ends_share = lax.dynamic_slice_in_dim(ends, tp_id * share_cols, share_cols, 1)
        own_ends = jnp.where(section_id == tick, shift(ends_share, 0, [(tick + 1, tick)]), own_ends)
        if tick + 1 < last:
            hidden = gather(rows, [tick + 1], 0)
            own_share = lax.dynamic_slice_in_dim(hidden, tp_id * share_cols, share_cols, 1)

    row_positions = tp_id * share_rows + jnp.arange(share_rows, dtype=jnp.int32)
    latent = dot(rms_rows(rows.astype(F32)).astype(BF16), latent_whole)
    fresh = jnp.concatenate(
        [rms_rows(latent[:, :LATENT]), rotate(latent[:, LATENT:], row_positions)], axis=-1
    ).astype(BF16)
    own_cache = jnp.where(section_id == last, fresh, own_cache)
    down = dot(rms_rows(ends.astype(F32)).astype(BF16), down_weight).astype(BF16)
    down = jnp.pad(down, ((0, 0), (0, fresh.shape[1] - down_cols)))
    whole = gather(jnp.concatenate([fresh, down], axis=0)[None], [last], 0)
    cache = whole[:, :share_rows].reshape(tokens, LATENT + ROPE_DIM)
    down = jnp.concatenate([whole[m, share_rows:, :down_cols] for m in range(tp_count)], axis=1)
    compressed = rms_rows(down.astype(F32)).astype(BF16)
    partial = attend(compressed, end_rows, cache).astype(BF16)
    total = ends_share.astype(F32)
    for k in range(tp_count):
        start = lax.rem(tp_id + k, tp_count) * share_cols
        block = lax.dynamic_slice_in_dim(partial, start, share_cols, 1)
        total = total + (shift(block, k, [(last, last)]) if k else block).astype(F32)
    own_ends = jnp.where(section_id == last, total.astype(BF16), own_ends)
    return (own_cache[None], own_ends[None])


ROW_WIDTH = LATENT + ROPE_DIM
HEAD_WIDTH = NOPE_DIM + ROPE_DIM
HALF = ROPE_DIM // 2
SMEM = pl.BlockSpec(memory_space=pltpu.SMEM)
VMEM = pl.BlockSpec(memory_space=pltpu.VMEM)
HBM = pl.BlockSpec(memory_space=pltpu.HBM)


def call(kernel, out_shape, args, scratch=(), flops=0, scalars=0, left=0, space=VMEM, grant=8):
    many = isinstance(out_shape, list)
    moved = sum(a.size * a.dtype.itemsize for a in args)
    return pl.pallas_call(
        kernel,
        out_shape=out_shape,
        in_specs=[SMEM] * scalars + [VMEM] * (len(args) - scalars - left) + [HBM] * left,
        out_specs=[space] * len(out_shape) if many else space,
        scratch_shapes=list(scratch),
        compiler_params=pltpu.CompilerParams(vmem_limit_bytes=grant * 2**20),
        cost_estimate=pl.CostEstimate(flops=flops, bytes_accessed=moved, transcendentals=0),
    )(*args)


def dot_t(a, b):
    return lax.dot_general(a, b, (((1,), (1,)), ((), ())), preferred_element_type=F32)


def unit(values):
    return lax.rsqrt(jnp.mean(values * values, axis=-1, keepdims=True) + EPSILON)


def turn(pair, angles):
    cosine, sine = angles[:, :HALF], angles[:, HALF:]
    a, b = pair[:, :HALF], pair[:, HALF:]
    return jnp.concatenate([a * cosine - b * sine, a * sine + b * cosine], axis=1)


def end_rows(sizes):
    ends = [sizes[0] - 1]
    for i in range(1, sizes.shape[0]):
        ends.append(ends[-1] + sizes[i])
    return ends


def column(scalars):
    rows = lax.broadcasted_iota(jnp.int32, (len(scalars), 1), 0)
    out = jnp.zeros((len(scalars), 1), jnp.int32)
    for i, value in enumerate(scalars):
        out = jnp.where(rows == i, value, out)
    return out


def send_kernel(prompt, w_latent, out, half, packed, sem):
    section, rep = lax.axis_index("section"), lax.axis_index("rep")
    rows, width = out.shape
    cols, long = half.shape

    @pl.when(section == 0)
    def _():
        copy = pltpu.make_async_copy(prompt, packed, sem)
        copy.start()
        copy.wait()

    @pl.when(section != 0)
    def _():
        columns = pl.ds(pl.multiple_of((rep & 1) * long, 128), long)
        copy = pltpu.make_async_copy(w_latent.at[:, columns], half, sem)
        copy.start()
        copy.wait()
        extra = half[:, width : width + 256].astype(F32)
        free = rows - cols
        left = cols - 2 * free
        tail = [extra[2 * free :, :128], extra[2 * free :, 128:], jnp.zeros((free - 2 * left, 128), F32)]
        extra = jnp.concatenate(
            [extra[:free], extra[free : 2 * free], jnp.concatenate(tail, axis=0)], axis=1
        )
        whole = jnp.concatenate([half[:, :width].astype(F32), extra], axis=0)
        packed[...] = whole.astype(BF16)

    copy = pltpu.make_async_copy(packed, out, sem)
    copy.start()
    copy.wait()


def unpack_share(share, cols):
    share = share.astype(F32)
    free = share.shape[0] - cols
    left = cols - 2 * free
    extra, tail = share[cols:, :512], share[cols:, 512:]
    tail = jnp.concatenate([tail[:left], tail[left : 2 * left]], axis=1)
    extra = jnp.concatenate([extra[:, :256], extra[:, 256:], tail], axis=0)
    return jnp.concatenate([share[:cols], extra], axis=1).astype(BF16)


def down_kernel(own, three, two, one, w_down, w_latent, out):
    section, tp, rep = (lax.axis_index(a) for a in ("section", "tp", "rep"))
    tokens, share = own.shape
    cols, model = w_latent.shape
    third = tokens // 3

    @pl.when(section == 0)
    def _():
        squares, down, latent = 0.0, 0.0, 0.0
        for k, ref in enumerate((own, one, two, three)):
            columns = pl.ds(pl.multiple_of((tp ^ k) * share, 128), share)
            piece = ref[...]
            wide = piece.astype(F32)
            squares = squares + jnp.sum(wide * wide, axis=1, keepdims=True)
            down = down + dot_t(piece, w_down[:, columns])
            latent = latent + dot_t(piece, w_latent[:, columns])
        scale = lax.rsqrt(squares / model + EPSILON)
        parts = jnp.concatenate([down * scale, latent * scale], axis=1)
        rest = parts[:, 256:]
        rest = [rest[i * third : (i + 1) * third] for i in range(3)]
        rest.append(jnp.zeros((third, 256 - 3 * rest[0].shape[1]), F32))
        out[...] = jnp.concatenate([parts[:, :256], jnp.concatenate(rest, axis=1)], axis=0).astype(BF16)

    @pl.when(section != 0)
    def _():
        first = ((rep & 1) + 1) * (model // 2) - 384
        mine = w_latent[:, pl.ds(pl.multiple_of(first, 128), 384)].astype(F32)
        rest = mine[:, 256:]
        high = cols // 2 + 4
        lower = jnp.concatenate([rest[high:], jnp.zeros((2 * high - cols, 128), F32)], axis=0)
        rest = jnp.concatenate([rest[:high], lower], axis=1)
        blank = jnp.zeros((out.shape[0] - cols - high, 256), F32)
        out[...] = jnp.concatenate([mine[:, :256], rest, blank], axis=0).astype(BF16)


def unpack_rest(piece, cols):
    piece = piece.astype(F32)
    high = cols // 2 + 4
    rest = piece[cols : cols + high]
    rest = jnp.concatenate([rest[:, :128], rest[: cols - high, 128:]], axis=0)
    return jnp.concatenate([piece[:cols], rest], axis=1).astype(BF16)


def unpack_parts(piece, tokens, width):
    piece = piece.astype(F32)
    rest, size = piece[tokens:], width - 256
    rest = jnp.concatenate([rest[:, i * size : (i + 1) * size] for i in range(3)], axis=0)
    return jnp.concatenate([piece[:tokens], rest], axis=1)


def attend_rows(compressed, cache, seen, angles, w_query, w_keys, w_values):
    plain, turned = cache[:, :LATENT], cache[:, LATENT:]
    keys = dot(plain, w_keys[...]).astype(BF16)
    values = dot(plain, w_values[...]).astype(BF16)
    queries = dot(compressed, w_query[...])
    mixed = []
    for head in range(queries.shape[1] // HEAD_WIDTH):
        query = queries[:, head * HEAD_WIDTH : (head + 1) * HEAD_WIDTH]
        query = jnp.concatenate(
            [query[:, :NOPE_DIM], turn(query[:, NOPE_DIM:], angles)], axis=1
        ).astype(BF16)
        key = jnp.concatenate([keys[:, head * NOPE_DIM : (head + 1) * NOPE_DIM], turned], axis=1)
        scores = dot_t(query, key) * HEAD_WIDTH**-0.5
        powered = jnp.where(seen, jnp.exp(scores), 0.0)
        attention = (powered / jnp.sum(powered, axis=1, keepdims=True)).astype(BF16)
        mixed.append(dot(attention, values[:, head * VALUE_DIM : (head + 1) * VALUE_DIM]))
    return jnp.concatenate(mixed, axis=1).astype(BF16)


def layer_kernel(
    sizes, own, one, two, three, share1, w_latent, prompt, angles,
    w_query, w_keys, w_values, w_out, out0, out1, out2, out3, own_cache, passed, rest, stack, total, cached,
):
    section, tp, rep = (lax.axis_index(a) for a in ("section", "tp", "rep"))
    tokens, width = prompt.shape
    block = tokens // 4
    cols, early = passed.shape[1:]
    down_cols = w_query.shape[0] // 4

    @pl.when(section != 0)
    def _():
        first = (rep & 1) * (early + rest.shape[2])
        passed[0] = w_latent[:, pl.ds(pl.multiple_of(first, 128), early)]
        passed[1] = unpack_share(share1[...], cols)
        for k, ref in enumerate((one, two, three)):
            rest[k] = unpack_rest(ref[...], cols)

    @pl.when(section == 0)
    def _():
        ends = column(end_rows(sizes))
        for k, ref in enumerate((own, one, two, three)):
            stack[tp ^ k] = ref[...]
        pieces = [unpack_parts(stack[m], tokens, down_cols + cols) for m in range(4)]
        down = jnp.concatenate([p[:, :down_cols] for p in pieces], axis=1)
        latent = jnp.concatenate([p[:, down_cols:] for p in pieces], axis=1)
        compressed = (down * unit(down)).astype(BF16)
        plain = latent[:, :LATENT]
        cache = jnp.concatenate(
            [plain * unit(plain), turn(latent[:, LATENT:], angles[...])], axis=1
        ).astype(BF16)
        cached[...] = cache
        own_cache[...] = cached[pl.ds(pl.multiple_of(tp * block, block), block), :]
        seen = lax.broadcasted_iota(jnp.int32, (tokens, tokens), 0) >= lax.broadcasted_iota(
            jnp.int32, (tokens, tokens), 1
        )
        mixed = attend_rows(compressed, cache, seen, angles[...], w_query, w_keys, w_values)
        chosen = lax.broadcasted_iota(jnp.int32, (ends.shape[0], tokens), 1) == ends
        chosen = chosen.astype(BF16)
        rows = jnp.concatenate([mixed, dot(chosen, mixed).astype(BF16)], axis=0)
        total[...] = dot(rows, w_out[...])
        mine = pl.ds(pl.multiple_of(tp * width, 128), width)
        added = jnp.concatenate([prompt[...].astype(F32), dot(chosen, prompt[...])], axis=0)
        total[:, mine] += added
        last = total[tokens:, :]
        for k, out in enumerate((out0, out1, out2, out3)):
            part = total[pl.ds(pl.multiple_of((tp ^ k) * block, block), block), :]
            out[...] = jnp.concatenate([part, last], axis=0).astype(BF16)


def latent_kernel(
    one, two, three, four, angles, w_latent, first1, first2, first3, rest,
    near1, near2, near3, near_rest, w_down, out, own_cache, own_ends, hidden, parts,
):
    tp, rep = lax.axis_index("tp"), lax.axis_index("rep")
    block = angles.shape[0] // 4
    width = own_ends.shape[1]
    model = w_latent.shape[1]
    early = first1.shape[1]
    rows = one[...].astype(F32) + two[...].astype(F32) + three[...].astype(F32) + four[...].astype(F32)
    narrow = rows.astype(BF16)
    rows = narrow.astype(F32)
    hidden[...] = rows
    scale = unit(rows)
    parts[tp] = dot_t(narrow[:block], w_latent[...])
    sums = [0.0, 0.0, 0.0]
    for core, weights in enumerate(
        (
            (first1, first2, first3, rest),
            (near1, near2, near3, near_rest),
        )
    ):
        first = ((rep & 1) ^ core) * (model // 2)
        head = hidden[0:block, pl.ds(pl.multiple_of(first, 128), early)].astype(BF16)
        late = pl.ds(pl.multiple_of(first + early, 128), model // 2 - early)
        tail = hidden[0:block, late].astype(BF16)
        for k in range(3):
            sums[k] += dot_t(head, weights[k][...]) + dot_t(tail, weights[3][k])
    for k, value in enumerate(sums):
        parts[tp ^ (k + 1)] = value
    latent = jnp.concatenate([parts[m] for m in range(4)], axis=1) * scale[:block]
    plain = latent[:, :LATENT]
    plain = plain * unit(plain)
    own_angles = angles[pl.ds(pl.multiple_of(tp * block, block), block), :]
    turned = turn(latent[:, LATENT:], own_angles)
    own_cache[...] = jnp.concatenate([plain, turned], axis=1).astype(BF16)
    down = dot_t(narrow[block:, :], w_down[...]) * scale[block:]
    count = down.shape[0]
    turned = [turned[i * count : (i + 1) * count] for i in range(block // count)]
    last = jnp.concatenate([*turned, down], axis=1)
    last = jnp.concatenate([last, jnp.zeros((count, LATENT - last.shape[1]), F32)], axis=1)
    out[...] = jnp.concatenate([plain, last], axis=0).astype(BF16)
    mine = pl.ds(pl.multiple_of(tp * width, 128), width)
    own_ends[...] = hidden[block:, mine].astype(BF16)


def ends_kernel(
    sizes, own, one, two, three, angles, w_query, w_keys, w_values, w_out,
    out0, out1, out2, out3, stack, total,
):
    tp = lax.axis_index("tp")
    ends = end_rows(sizes)
    count = len(ends)
    block = own.shape[0] - count
    steps = block // count
    down_cols = w_query.shape[0] // 4
    width = out0.shape[1]
    for k, ref in enumerate((own, one, two, three)):
        stack[tp ^ k] = ref[...].astype(F32)
    pieces = [stack[m] for m in range(4)]
    plain = jnp.concatenate([p[:block] for p in pieces], axis=0)
    last = [p[block:] for p in pieces]
    turned = jnp.concatenate(
        [p[:, i * ROPE_DIM : (i + 1) * ROPE_DIM] for p in last for i in range(steps)], axis=0
    )
    cache = jnp.concatenate([plain, turned], axis=1).astype(BF16)
    first = steps * ROPE_DIM
    down = jnp.concatenate([p[:, first : first + down_cols] for p in last], axis=1)
    compressed = (down * unit(down)).astype(BF16)
    end_angles = jnp.concatenate([angles[pl.ds(e, 1), :] for e in ends], axis=0)
    seen = lax.broadcasted_iota(jnp.int32, (count, 4 * block), 1) <= column(ends)
    mixed = attend_rows(compressed, cache, seen, end_angles, w_query, w_keys, w_values)
    total[...] = dot(mixed, w_out[...])
    for k, out in enumerate((out0, out1, out2, out3)):
        columns = pl.ds(pl.multiple_of((tp ^ k) * width, 128), width)
        out[...] = total[:, columns].astype(BF16)


def local_two(prompt, block_sizes, w_query_down, w_query, w_latent, w_keys, w_values, w_out):
    section = lax.axis_index("section")
    tokens, share = prompt.shape
    block = tokens // 4
    count = block_sizes.shape[0]
    w_down, w_up, w_lat = w_query_down[0].T, w_query[0], w_latent[0].T
    w_key, w_value, w_final = w_keys[0], w_values[0], w_out[0]
    down_cols, latent_cols = w_down.shape[0], w_lat.shape[0]
    model = 4 * share
    frequency = 10000.0 ** (-2.0 * np.arange(HALF, dtype=np.float32) / ROPE_DIM)
    angles = np.arange(tokens, dtype=np.float32)[:, None] * frequency.astype(np.float32)[None, :]
    angles = jnp.asarray(np.concatenate([np.cos(angles), np.sin(angles)], axis=1), F32)

    def route(array, *ways):
        pairs = [
            (s * 4 + i, way[0] * 4 + (i ^ way[1])) for s, way in enumerate(ways) if way for i in range(4)
        ]
        return lax.ppermute(array, ("section", "tp"), pairs)

    def within(array, k):
        return route(array, (0, k), (1, k))

    def onward(array, k):
        return route(array, (1, k), (0, 0))

    def over_rep(array, k):
        return lax.ppermute(array, "rep", [(i, i ^ k) for i in range(4)])

    sent = call(
        send_kernel,
        jax.ShapeDtypeStruct((tokens, share), BF16),
        [prompt, w_lat],
        [
            pltpu.VMEM((latent_cols, model // 2), BF16),
            pltpu.VMEM((tokens, share), BF16),
            pltpu.SemaphoreType.DMA,
        ],
        left=2,
        space=HBM,
        grant=57,
        flops=2 * 10**10,
    )
    two = route(prompt, (1, 0), (0, 2))
    three = route(prompt, (0, 3), (1, 1))
    one = route(sent, (0, 1), (1, 1))
    parts = call(
        down_kernel,
        jax.ShapeDtypeStruct((tokens + tokens // 3, 256), BF16),
        [prompt, three, two, one, w_down, w_lat],
        flops=2 * 10**10,
    )
    pieces = [parts] + [within(parts, k) for k in (1, 2, 3)]

    message = jax.ShapeDtypeStruct((block + count, model), BF16)
    *blocks, first_cache, passed, rest = call(
        layer_kernel,
        [message] * 4
        + [
            jax.ShapeDtypeStruct((block, ROW_WIDTH), BF16),
            jax.ShapeDtypeStruct((2, latent_cols, model // 2 - 384), BF16),
            jax.ShapeDtypeStruct((3, latent_cols, 384), BF16),
        ],
        [block_sizes, *pieces, one, w_lat, prompt, angles, w_up, w_key, w_value, w_final],
        [
            pltpu.VMEM((4, *parts.shape), BF16),
            pltpu.VMEM((tokens + count, model), F32),
            pltpu.VMEM((tokens, ROW_WIDTH), BF16),
        ],
        flops=2 * tokens * (w_up.size + w_key.size + w_value.size + w_final.size),
        scalars=1,
        grant=16,
    )
    arrived = [onward(blocks[k], k) for k in (3, 2, 1, 0)]
    relayed = route(passed, None, (1, 2))
    relayed, late, first = lax.optimization_barrier((relayed, rest, passed[1]))
    weights = [first, relayed[0], relayed[1], late]
    weights += [over_rep(w, 1) for w in weights]
    fresh, last_cache, ends_share = call(
        latent_kernel,
        [
            jax.ShapeDtypeStruct((block + count, LATENT), BF16),
            jax.ShapeDtypeStruct((block, ROW_WIDTH), BF16),
            jax.ShapeDtypeStruct((count, share), BF16),
        ],
        [*arrived, angles, w_lat, *weights, w_down],
        [pltpu.VMEM((block + count, model), F32), pltpu.VMEM((4, block, latent_cols), F32)],
        flops=2 * 10**11,
    )
    pieces = [fresh] + [within(fresh, k) for k in (1, 2, 3)]
    first_ends = onward(ends_share, 0)
    outs = call(
        ends_kernel,
        [jax.ShapeDtypeStruct((count, share), BF16)] * 4,
        [block_sizes, *pieces, angles, w_up, w_key, w_value, w_final],
        [
            pltpu.VMEM((4, block + count, LATENT), F32),
            pltpu.VMEM((count, model), F32),
        ],
        flops=2 * tokens * (w_key.size + w_value.size),
        scalars=1,
    )
    total = ends_share.astype(F32) + outs[0].astype(F32)
    for k in (1, 2, 3):
        total = total + within(outs[k], k).astype(F32)
    own_ends = jnp.where(section == 0, first_ends, total.astype(BF16))
    own_cache = jnp.where(section == 0, first_cache, last_cache)
    return (own_cache[None], own_ends[None])


def solution(mesh):
    sizes = [mesh.shape[a] for a in ("section", "tp", "rep")]
    body = local_two if sizes == [2, 4, 4] else local
    in_specs = (
        P("rep", "tp"),
        P("rep"),
        P("section", None, "tp"),
        P("section", None, "tp"),
        P("section", None, "tp"),
        P("section", None, "tp"),
        P("section", None, "tp"),
        P("section", "tp", None),
    )
    out_specs = (P("section", ("rep", "tp"), None), P("section", "rep", "tp"))
    return jax.shard_map(body, mesh=mesh, in_specs=in_specs, out_specs=out_specs, check_vma=False)
```

```python
import jax
import jax.numpy as jnp
import numpy as np
from jax import lax
from jax.experimental import pallas as pl
from jax.experimental.pallas import tpu as pltpu
from jax.sharding import PartitionSpec as P

NOPE_DIM = 128
ROPE_DIM = 32
VALUE_DIM = 128
LATENT = 512
EPSILON = 1e-06
F32 = jnp.float32
BF16 = jnp.bfloat16


def rms_rows(values):
    return values * lax.rsqrt(jnp.mean(values * values, axis=-1, keepdims=True) + EPSILON)


def rotate(values, positions):
    half_width = values.shape[-1] // 2
    frequency = 10000.0 ** (-2.0 * jnp.arange(half_width, dtype=F32) / values.shape[-1])
    angles = positions.astype(F32)[:, None] * frequency[None, :]
    if values.ndim == 3:
        angles = angles[:, None, :]
    cosine = jnp.cos(angles)
    sine_part = jnp.sin(angles)
    first_half = values[..., :half_width]
    second = values[..., half_width:]
    return jnp.concatenate(
        [first_half * cosine - second * sine_part, first_half * sine_part + second * cosine],
        axis=-1,
    )


def dot(a, b):
    return jnp.dot(a, b, preferred_element_type=F32)


def local(prompt, block_sizes, w_query_down, w_query, w_latent, w_keys, w_values, w_out):
    sections = lax.axis_size("section")
    section_id = lax.axis_index("section")
    tp_id = lax.axis_index("tp")
    tp_count = lax.axis_size("tp")
    tokens, share_cols = prompt.shape
    share_rows = tokens // tp_count
    down_weight, query_weight, latent_weight = w_query_down[0], w_query[0], w_latent[0]
    key_weight, value_weight, out_weight = w_keys[0], w_values[0], w_out[0]
    down_cols, latent_cols = down_weight.shape[1], latent_weight.shape[1]
    head_count = query_weight.shape[1] // (NOPE_DIM + ROPE_DIM)
    scale_factor = (NOPE_DIM + ROPE_DIM) ** (-0.5)
    all_positions = jnp.arange(tokens, dtype=jnp.int32)
    end_rows = jnp.cumsum(block_sizes) - 1

    def shift(array, distance, routes):
        pairs = [
            (a * tp_count + i, b * tp_count + (i + distance) % tp_count)
            for a, b in routes
            for i in range(tp_count)
        ]
        return lax.ppermute(array, ("section", "tp"), pairs)

    def gather(array, where, axis):
        routes = [(s, s) for s in where]
        width = array.shape[axis]
        shape = list(array.shape)
        shape[axis] = width * tp_count
        whole = jnp.zeros(shape, array.dtype)
        for k in range(tp_count):
            piece = array if k == 0 else shift(array, k, routes)
            whole = lax.dynamic_update_slice_in_dim(
                whole, piece, lax.rem(tp_id - k + tp_count, tp_count) * width, axis
            )
        return whole

    def keys_and_values(cache):
        plain = cache[:, :LATENT]
        keys = dot(plain, key_weight).astype(BF16).reshape(tokens, head_count, NOPE_DIM)
        values = dot(plain, value_weight).astype(BF16).reshape(tokens, head_count, VALUE_DIM)
        return keys, values

    def attend(compressed, positions, cache):
        keys, values = keys_and_values(cache)
        rows = compressed.shape[0]
        queries = dot(compressed, query_weight).reshape(rows, head_count, NOPE_DIM + ROPE_DIM)
        queries = jnp.concatenate(
            [queries[..., :NOPE_DIM], rotate(queries[..., NOPE_DIM:], positions)], axis=-1
        ).astype(BF16)
        scores = jnp.einsum("ihd,jhd->hij", queries[..., :NOPE_DIM], keys, preferred_element_type=F32)
        scores = scores + jnp.einsum(
            "ihr,jr->hij", queries[..., NOPE_DIM:], cache[:, LATENT:], preferred_element_type=F32
        )
        visible = all_positions[None, :] <= positions[:, None]
        powered = jnp.where(visible[None], jnp.exp(scores * scale_factor), 0.0)
        attention = (powered / jnp.sum(powered, axis=-1, keepdims=True)).astype(BF16)
        mixed = jnp.einsum("hij,jhv->ihv", attention, values, preferred_element_type=F32)
        return dot(mixed.astype(BF16).reshape(rows, head_count * VALUE_DIM), out_weight)

    def layer(hidden, own_share, tick):
        normed = rms_rows(hidden.astype(F32)).astype(BF16)
        parts = jnp.concatenate(
            [dot(normed, down_weight).astype(BF16), dot(normed, latent_weight).astype(BF16)], axis=1
        )
        whole = gather(parts[None], [tick], 0).astype(F32)
        down = jnp.concatenate([whole[m, :, :down_cols] for m in range(tp_count)], axis=1)
        latent = jnp.concatenate([whole[m, :, down_cols:] for m in range(tp_count)], axis=1)
        compressed = rms_rows(down).astype(BF16)
        cache = jnp.concatenate(
            [rms_rows(latent[:, :LATENT]), rotate(latent[:, LATENT:], all_positions)], axis=-1
        ).astype(BF16)
        partial = attend(compressed, all_positions, cache)
        start = tp_id * share_cols
        mine = lax.dynamic_slice_in_dim(partial, start, share_cols, 1) + own_share.astype(F32)
        partial = lax.dynamic_update_slice_in_dim(partial, mine, start, 1).astype(BF16)
        return partial, cache

    def pass_on(partial, tick):
        ends = jnp.take(partial, end_rows, axis=0)
        total = 0.0
        for k in range(tp_count):
            first = lax.rem(tp_id + k, tp_count) * share_rows
            block = lax.dynamic_slice_in_dim(partial, first, share_rows, 0)
            block = jnp.concatenate([block, ends], axis=0)
            total = total + shift(block, k, [(tick, tick + 1)]).astype(F32)
        total = total.astype(BF16)
        return total[:share_rows], total[share_rows:]

    own_cache = jnp.zeros((share_rows, LATENT + ROPE_DIM), BF16)
    own_ends = jnp.zeros((block_sizes.shape[0], share_cols), BF16)
    last = sections - 1
    latent_whole = gather(latent_weight, range(1, sections), 1) if last else latent_weight
    hidden, own_share = gather(prompt, [0], 1), prompt
    for tick in range(last):
        partial, cache = layer(hidden, own_share, tick)
        mine = lax.dynamic_slice_in_dim(cache, tp_id * share_rows, share_rows, 0)
        own_cache = jnp.where(section_id == tick, mine, own_cache)
        rows, ends = pass_on(partial, tick)
        ends_share = lax.dynamic_slice_in_dim(ends, tp_id * share_cols, share_cols, 1)
        own_ends = jnp.where(section_id == tick, shift(ends_share, 0, [(tick + 1, tick)]), own_ends)
        if tick + 1 < last:
            hidden = gather(rows, [tick + 1], 0)
            own_share = lax.dynamic_slice_in_dim(hidden, tp_id * share_cols, share_cols, 1)

    row_positions = tp_id * share_rows + jnp.arange(share_rows, dtype=jnp.int32)
    latent = dot(rms_rows(rows.astype(F32)).astype(BF16), latent_whole)
    fresh = jnp.concatenate(
        [rms_rows(latent[:, :LATENT]), rotate(latent[:, LATENT:], row_positions)], axis=-1
    ).astype(BF16)
    own_cache = jnp.where(section_id == last, fresh, own_cache)
    down = dot(rms_rows(ends.astype(F32)).astype(BF16), down_weight).astype(BF16)
    down = jnp.pad(down, ((0, 0), (0, fresh.shape[1] - down_cols)))
    whole = gather(jnp.concatenate([fresh, down], axis=0)[None], [last], 0)
    cache = whole[:, :share_rows].reshape(tokens, LATENT + ROPE_DIM)
    down = jnp.concatenate([whole[m, share_rows:, :down_cols] for m in range(tp_count)], axis=1)
    compressed = rms_rows(down.astype(F32)).astype(BF16)
    partial = attend(compressed, end_rows, cache).astype(BF16)
    total = ends_share.astype(F32)
    for k in range(tp_count):
        start = lax.rem(tp_id + k, tp_count) * share_cols
        block = lax.dynamic_slice_in_dim(partial, start, share_cols, 1)
        total = total + (shift(block, k, [(last, last)]) if k else block).astype(F32)
    own_ends = jnp.where(section_id == last, total.astype(BF16), own_ends)
    return (own_cache[None], own_ends[None])


ROW_WIDTH = LATENT + ROPE_DIM
HEAD_WIDTH = NOPE_DIM + ROPE_DIM
HALF = ROPE_DIM // 2
SMEM = pl.BlockSpec(memory_space=pltpu.SMEM)
VMEM = pl.BlockSpec(memory_space=pltpu.VMEM)
HBM = pl.BlockSpec(memory_space=pltpu.HBM)


def call(kernel, out_shape, args, scratch=(), flops=0, scalars=0, left=0, space=VMEM, grant=8):
    many = isinstance(out_shape, list)
    moved = sum(a.size * a.dtype.itemsize for a in args)
    return pl.pallas_call(
        kernel,
        out_shape=out_shape,
        in_specs=[SMEM] * scalars + [VMEM] * (len(args) - scalars - left) + [HBM] * left,
        out_specs=[space] * len(out_shape) if many else space,
        scratch_shapes=list(scratch),
        compiler_params=pltpu.CompilerParams(vmem_limit_bytes=grant * 2**20),
        cost_estimate=pl.CostEstimate(flops=flops, bytes_accessed=moved, transcendentals=0),
    )(*args)


def dot_t(a, b):
    return lax.dot_general(a, b, (((1,), (1,)), ((), ())), preferred_element_type=F32)


def unit(values):
    return lax.rsqrt(jnp.mean(values * values, axis=-1, keepdims=True) + EPSILON)


def turn(pair, angles):
    cosine, sine = angles[:, :HALF], angles[:, HALF:]
    a, b = pair[:, :HALF], pair[:, HALF:]
    return jnp.concatenate([a * cosine - b * sine, a * sine + b * cosine], axis=1)


def end_rows(sizes):
    ends = [sizes[0] - 1]
    for i in range(1, sizes.shape[0]):
        ends.append(ends[-1] + sizes[i])
    return ends


def column(scalars):
    rows = lax.broadcasted_iota(jnp.int32, (len(scalars), 1), 0)
    out = jnp.zeros((len(scalars), 1), jnp.int32)
    for i, value in enumerate(scalars):
        out = jnp.where(rows == i, value, out)
    return out


def send_kernel(prompt, w_latent, out, half, packed, sem):
    section, rep = lax.axis_index("section"), lax.axis_index("rep")
    rows, width = out.shape
    cols, long = half.shape

    @pl.when(section == 0)
    def _():
        copy = pltpu.make_async_copy(prompt, packed, sem)
        copy.start()
        copy.wait()

    @pl.when(section != 0)
    def _():
        columns = pl.ds(pl.multiple_of((rep & 1) * long, 128), long)
        copy = pltpu.make_async_copy(w_latent.at[:, columns], half, sem)
        copy.start()
        copy.wait()
        extra = half[:, width : width + 256].astype(F32)
        free = rows - cols
        left = cols - 2 * free
        tail = [extra[2 * free :, :128], extra[2 * free :, 128:], jnp.zeros((free - 2 * left, 128), F32)]
        extra = jnp.concatenate(
            [extra[:free], extra[free : 2 * free], jnp.concatenate(tail, axis=0)], axis=1
        )
        whole = jnp.concatenate([half[:, :width].astype(F32), extra], axis=0)
        packed[...] = whole.astype(BF16)

    copy = pltpu.make_async_copy(packed, out, sem)
    copy.start()
    copy.wait()


def unpack_share(share, cols):
    share = share.astype(F32)
    free = share.shape[0] - cols
    left = cols - 2 * free
    extra, tail = share[cols:, :512], share[cols:, 512:]
    tail = jnp.concatenate([tail[:left], tail[left : 2 * left]], axis=1)
    extra = jnp.concatenate([extra[:, :256], extra[:, 256:], tail], axis=0)
    return jnp.concatenate([share[:cols], extra], axis=1).astype(BF16)


def down_kernel(own, three, two, one, w_down, w_latent, out):
    section, tp, rep = (lax.axis_index(a) for a in ("section", "tp", "rep"))
    tokens, share = own.shape
    cols, model = w_latent.shape
    third = tokens // 3

    @pl.when(section == 0)
    def _():
        squares, down, latent = 0.0, 0.0, 0.0
        for k, ref in enumerate((own, one, two, three)):
            columns = pl.ds(pl.multiple_of((tp ^ k) * share, 128), share)
            piece = ref[...]
            wide = piece.astype(F32)
            squares = squares + jnp.sum(wide * wide, axis=1, keepdims=True)
            down = down + dot_t(piece, w_down[:, columns])
            latent = latent + dot_t(piece, w_latent[:, columns])
        scale = lax.rsqrt(squares / model + EPSILON)
        parts = jnp.concatenate([down * scale, latent * scale], axis=1)
        rest = parts[:, 256:]
        rest = [rest[i * third : (i + 1) * third] for i in range(3)]
        rest.append(jnp.zeros((third, 256 - 3 * rest[0].shape[1]), F32))
        out[...] = jnp.concatenate([parts[:, :256], jnp.concatenate(rest, axis=1)], axis=0).astype(BF16)

    @pl.when(section != 0)
    def _():
        first = ((rep & 1) + 1) * (model // 2) - 384
        mine = w_latent[:, pl.ds(pl.multiple_of(first, 128), 384)].astype(F32)
        rest = mine[:, 256:]
        high = cols // 2 + 4
        lower = jnp.concatenate([rest[high:], jnp.zeros((2 * high - cols, 128), F32)], axis=0)
        rest = jnp.concatenate([rest[:high], lower], axis=1)
        blank = jnp.zeros((out.shape[0] - cols - high, 256), F32)
        out[...] = jnp.concatenate([mine[:, :256], rest, blank], axis=0).astype(BF16)


def unpack_rest(piece, cols):
    piece = piece.astype(F32)
    high = cols // 2 + 4
    rest = piece[cols : cols + high]
    rest = jnp.concatenate([rest[:, :128], rest[: cols - high, 128:]], axis=0)
    return jnp.concatenate([piece[:cols], rest], axis=1).astype(BF16)


def unpack_parts(piece, tokens, width):
    piece = piece.astype(F32)
    rest, size = piece[tokens:], width - 256
    rest = jnp.concatenate([rest[:, i * size : (i + 1) * size] for i in range(3)], axis=0)
    return jnp.concatenate([piece[:tokens], rest], axis=1)


def attend_rows(compressed, cache, seen, angles, w_query, w_keys, w_values):
    plain, turned = cache[:, :LATENT], cache[:, LATENT:]
    keys = dot(plain, w_keys[...]).astype(BF16)
    values = dot(plain, w_values[...]).astype(BF16)
    queries = dot(compressed, w_query[...])
    mixed = []
    for head in range(queries.shape[1] // HEAD_WIDTH):
        query = queries[:, head * HEAD_WIDTH : (head + 1) * HEAD_WIDTH]
        query = jnp.concatenate(
            [query[:, :NOPE_DIM], turn(query[:, NOPE_DIM:], angles)], axis=1
        ).astype(BF16)
        key = jnp.concatenate([keys[:, head * NOPE_DIM : (head + 1) * NOPE_DIM], turned], axis=1)
        scores = dot_t(query, key) * HEAD_WIDTH**-0.5
        powered = jnp.where(seen, jnp.exp(scores), 0.0)
        attention = (powered / jnp.sum(powered, axis=1, keepdims=True)).astype(BF16)
        mixed.append(dot(attention, values[:, head * VALUE_DIM : (head + 1) * VALUE_DIM]))
    return jnp.concatenate(mixed, axis=1).astype(BF16)


def layer_kernel(
    sizes, own, one, two, three, share1, w_latent, prompt, angles,
    w_query, w_keys, w_values, w_out, out0, out1, out2, out3, own_cache, passed, rest, stack, total, cached,
):
    section, tp, rep = (lax.axis_index(a) for a in ("section", "tp", "rep"))
    tokens, width = prompt.shape
    block = tokens // 4
    cols, early = passed.shape[1:]
    down_cols = w_query.shape[0] // 4

    @pl.when(section != 0)
    def _():
        first = (rep & 1) * (early + rest.shape[2])
        passed[0] = w_latent[:, pl.ds(pl.multiple_of(first, 128), early)]
        passed[1] = unpack_share(share1[...], cols)
        for k, ref in enumerate((one, two, three)):
            rest[k] = unpack_rest(ref[...], cols)

    @pl.when(section == 0)
    def _():
        ends = column(end_rows(sizes))
        for k, ref in enumerate((own, one, two, three)):
            stack[tp ^ k] = ref[...]
        pieces = [unpack_parts(stack[m], tokens, down_cols + cols) for m in range(4)]
        down = jnp.concatenate([p[:, :down_cols] for p in pieces], axis=1)
        latent = jnp.concatenate([p[:, down_cols:] for p in pieces], axis=1)
        compressed = (down * unit(down)).astype(BF16)
        plain = latent[:, :LATENT]
        cache = jnp.concatenate(
            [plain * unit(plain), turn(latent[:, LATENT:], angles[...])], axis=1
        ).astype(BF16)
        cached[...] = cache
        own_cache[...] = cached[pl.ds(pl.multiple_of(tp * block, block), block), :]
        seen = lax.broadcasted_iota(jnp.int32, (tokens, tokens), 0) >= lax.broadcasted_iota(
            jnp.int32, (tokens, tokens), 1
        )
        mixed = attend_rows(compressed, cache, seen, angles[...], w_query, w_keys, w_values)
        chosen = lax.broadcasted_iota(jnp.int32, (ends.shape[0], tokens), 1) == ends
        chosen = chosen.astype(BF16)
        rows = jnp.concatenate([mixed, dot(chosen, mixed).astype(BF16)], axis=0)
        total[...] = dot(rows, w_out[...])
        mine = pl.ds(pl.multiple_of(tp * width, 128), width)
        added = jnp.concatenate([prompt[...].astype(F32), dot(chosen, prompt[...])], axis=0)
        total[:, mine] += added
        last = total[tokens:, :]
        for k, out in enumerate((out0, out1, out2, out3)):
            part = total[pl.ds(pl.multiple_of((tp ^ k) * block, block), block), :]
            out[...] = jnp.concatenate([part, last], axis=0).astype(BF16)


def latent_kernel(
    one, two, three, four, angles, w_latent, first1, first2, first3, rest,
    near1, near2, near3, near_rest, w_down, out, own_cache, own_ends, hidden, parts,
):
    tp, rep = lax.axis_index("tp"), lax.axis_index("rep")
    block = angles.shape[0] // 4
    width = own_ends.shape[1]
    model = w_latent.shape[1]
    early = first1.shape[1]
    rows = one[...].astype(F32) + two[...].astype(F32) + three[...].astype(F32) + four[...].astype(F32)
    narrow = rows.astype(BF16)
    rows = narrow.astype(F32)
    hidden[...] = rows
    scale = unit(rows)
    parts[tp] = dot_t(narrow[:block], w_latent[...])
    sums = [0.0, 0.0, 0.0]
    for core, weights in enumerate(
        (
            (first1, first2, first3, rest),
            (near1, near2, near3, near_rest),
        )
    ):
        first = ((rep & 1) ^ core) * (model // 2)
        head = hidden[0:block, pl.ds(pl.multiple_of(first, 128), early)].astype(BF16)
        late = pl.ds(pl.multiple_of(first + early, 128), model // 2 - early)
        tail = hidden[0:block, late].astype(BF16)
        for k in range(3):
            sums[k] += dot_t(head, weights[k][...]) + dot_t(tail, weights[3][k])
    for k, value in enumerate(sums):
        parts[tp ^ (k + 1)] = value
    latent = jnp.concatenate([parts[m] for m in range(4)], axis=1) * scale[:block]
    plain = latent[:, :LATENT]
    plain = plain * unit(plain)
    own_angles = angles[pl.ds(pl.multiple_of(tp * block, block), block), :]
    turned = turn(latent[:, LATENT:], own_angles)
    own_cache[...] = jnp.concatenate([plain, turned], axis=1).astype(BF16)
    down = dot_t(narrow[block:, :], w_down[...]) * scale[block:]
    count = down.shape[0]
    turned = [turned[i * count : (i + 1) * count] for i in range(block // count)]
    last = jnp.concatenate([*turned, down], axis=1)
    last = jnp.concatenate([last, jnp.zeros((count, LATENT - last.shape[1]), F32)], axis=1)
    out[...] = jnp.concatenate([plain, last], axis=0).astype(BF16)
    mine = pl.ds(pl.multiple_of(tp * width, 128), width)
    own_ends[...] = hidden[block:, mine].astype(BF16)


def ends_kernel(
    sizes, own, three, two, one, angles, w_query, w_keys, w_values, out, stack
):
    tp = lax.axis_index("tp")
    ends = end_rows(sizes)
    count = len(ends)
    block = own.shape[0] - count
    steps = block // count
    down_cols = w_query.shape[0] // 4
    for k, ref in enumerate((own, one, two, three)):
        stack[tp ^ k] = ref[...].astype(F32)
    pieces = [stack[m] for m in range(4)]
    plain = jnp.concatenate([p[:block] for p in pieces], axis=0)
    last = [p[block:] for p in pieces]
    turned = jnp.concatenate(
        [p[:, i * ROPE_DIM : (i + 1) * ROPE_DIM] for p in last for i in range(steps)], axis=0
    )
    cache = jnp.concatenate([plain, turned], axis=1).astype(BF16)
    first = steps * ROPE_DIM
    down = jnp.concatenate([p[:, first : first + down_cols] for p in last], axis=1)
    compressed = (down * unit(down)).astype(BF16)
    end_angles = jnp.concatenate([angles[pl.ds(e, 1), :] for e in ends], axis=0)
    seen = lax.broadcasted_iota(jnp.int32, (count, 4 * block), 1) <= column(ends)
    out[...] = attend_rows(compressed, cache, seen, end_angles, w_query, w_keys, w_values)


def final_kernel(mixed, w_out, out0, out1, out2, out3, total):
    tp = lax.axis_index("tp")
    width = out0.shape[1]
    total[...] = dot(mixed[...], w_out[...])
    for k, out in enumerate((out0, out1, out2, out3)):
        columns = pl.ds(pl.multiple_of((tp ^ k) * width, 128), width)
        out[...] = total[:, columns].astype(BF16)


def local_two(prompt, block_sizes, w_query_down, w_query, w_latent, w_keys, w_values, w_out):
    section = lax.axis_index("section")
    tokens, share = prompt.shape
    block = tokens // 4
    count = block_sizes.shape[0]
    w_down, w_up, w_lat = w_query_down[0].T, w_query[0], w_latent[0].T
    w_key, w_value, w_final = w_keys[0], w_values[0], w_out[0]
    down_cols, latent_cols = w_down.shape[0], w_lat.shape[0]
    model = 4 * share
    frequency = 10000.0 ** (-2.0 * np.arange(HALF, dtype=np.float32) / ROPE_DIM)
    angles = np.arange(tokens, dtype=np.float32)[:, None] * frequency.astype(np.float32)[None, :]
    angles = jnp.asarray(np.concatenate([np.cos(angles), np.sin(angles)], axis=1), F32)

    def route(array, *ways):
        pairs = [
            (s * 4 + i, way[0] * 4 + (i ^ way[1])) for s, way in enumerate(ways) if way for i in range(4)
        ]
        return lax.ppermute(array, ("section", "tp"), pairs)

    def within(array, k):
        return route(array, (0, k), (1, k))

    def onward(array, k):
        return route(array, (1, k), (0, 0))

    def over_rep(array, k):
        return lax.ppermute(array, "rep", [(i, i ^ k) for i in range(4)])

    sent = call(
        send_kernel,
        jax.ShapeDtypeStruct((tokens, share), BF16),
        [prompt, w_lat],
        [
            pltpu.VMEM((latent_cols, model // 2), BF16),
            pltpu.VMEM((tokens, share), BF16),
            pltpu.SemaphoreType.DMA,
        ],
        left=2,
        space=HBM,
        grant=57,
        flops=2 * 10**10,
    )
    two = route(prompt, (1, 0), (0, 2))
    three = route(prompt, (0, 3), (1, 1))
    one = route(sent, (0, 1), (1, 1))
    parts = call(
        down_kernel,
        jax.ShapeDtypeStruct((tokens + tokens // 3, 256), BF16),
        [prompt, three, two, one, w_down, w_lat],
        flops=2 * 10**10,
    )
    pieces = [parts] + [within(parts, k) for k in (1, 2, 3)]

    message = jax.ShapeDtypeStruct((block + count, model), BF16)
    *blocks, first_cache, passed, rest = call(
        layer_kernel,
        [message] * 4
        + [
            jax.ShapeDtypeStruct((block, ROW_WIDTH), BF16),
            jax.ShapeDtypeStruct((2, latent_cols, model // 2 - 384), BF16),
            jax.ShapeDtypeStruct((3, latent_cols, 384), BF16),
        ],
        [block_sizes, *pieces, one, w_lat, prompt, angles, w_up, w_key, w_value, w_final],
        [
            pltpu.VMEM((4, *parts.shape), BF16),
            pltpu.VMEM((tokens + count, model), F32),
            pltpu.VMEM((tokens, ROW_WIDTH), BF16),
        ],
        flops=2 * tokens * (w_up.size + w_key.size + w_value.size + w_final.size),
        scalars=1,
        grant=16,
    )
    arrived = [onward(blocks[k], k) for k in (2, 1, 3, 0)]
    relayed = route(passed, None, (1, 2))
    relayed, late, first = lax.optimization_barrier((relayed, rest, passed[1]))
    weights = [first, relayed[0], relayed[1], late]
    weights += [over_rep(w, 1) for w in weights]
    fresh, last_cache, ends_share = call(
        latent_kernel,
        [
            jax.ShapeDtypeStruct((block + count, LATENT), BF16),
            jax.ShapeDtypeStruct((block, ROW_WIDTH), BF16),
            jax.ShapeDtypeStruct((count, share), BF16),
        ],
        [*arrived, angles, w_lat, *weights, w_down],
        [pltpu.VMEM((block + count, model), F32), pltpu.VMEM((4, block, latent_cols), F32)],
        flops=2 * 10**11,
    )
    pieces = [fresh] + [within(fresh, k) for k in (3, 2, 1)]
    first_ends = onward(ends_share, 0)
    mixed = call(
        ends_kernel,
        jax.ShapeDtypeStruct((count, w_final.shape[0]), BF16),
        [block_sizes, *pieces, angles, w_up, w_key, w_value],
        [pltpu.VMEM((4, block + count, LATENT), F32)],
        flops=2 * 10**10,
        scalars=1,
    )
    outs = call(
        final_kernel,
        [jax.ShapeDtypeStruct((count, share), BF16)] * 4,
        [mixed, w_final],
        [pltpu.VMEM((count, model), F32)],
        flops=10**8,
    )
    total = ends_share.astype(F32) + outs[0].astype(F32)
    for k in (1, 2, 3):
        total = total + within(outs[k], k).astype(F32)
    own_ends = jnp.where(section == 0, first_ends, total.astype(BF16))
    own_cache = jnp.where(section == 0, first_cache, last_cache)
    return (own_cache[None], own_ends[None])


def solution(mesh):
    sizes = [mesh.shape[a] for a in ("section", "tp", "rep")]
    body = local_two if sizes == [2, 4, 4] else local
    in_specs = (
        P("rep", "tp"),
        P("rep"),
        P("section", None, "tp"),
        P("section", None, "tp"),
        P("section", None, "tp"),
        P("section", None, "tp"),
        P("section", None, "tp"),
        P("section", "tp", None),
    )
    out_specs = (P("section", ("rep", "tp"), None), P("section", "rep", "tp"))
    return jax.shard_map(body, mesh=mesh, in_specs=in_specs, out_specs=out_specs, check_vma=False)
```

```python
import jax
import jax.numpy as jnp
import numpy as np
from jax import lax
from jax.experimental import pallas as pl
from jax.experimental.pallas import tpu as pltpu
from jax.sharding import PartitionSpec as P

NOPE_DIM = 128
ROPE_DIM = 32
VALUE_DIM = 128
LATENT = 512
EPSILON = 1e-06
F32 = jnp.float32
BF16 = jnp.bfloat16


def rms_rows(values):
    return values * lax.rsqrt(jnp.mean(values * values, axis=-1, keepdims=True) + EPSILON)


def rotate(values, positions):
    half_width = values.shape[-1] // 2
    frequency = 10000.0 ** (-2.0 * jnp.arange(half_width, dtype=F32) / values.shape[-1])
    angles = positions.astype(F32)[:, None] * frequency[None, :]
    if values.ndim == 3:
        angles = angles[:, None, :]
    cosine = jnp.cos(angles)
    sine_part = jnp.sin(angles)
    first_half = values[..., :half_width]
    second = values[..., half_width:]
    return jnp.concatenate(
        [first_half * cosine - second * sine_part, first_half * sine_part + second * cosine],
        axis=-1,
    )


def dot(a, b):
    return jnp.dot(a, b, preferred_element_type=F32)


def local(prompt, block_sizes, w_query_down, w_query, w_latent, w_keys, w_values, w_out):
    sections = lax.axis_size("section")
    section_id = lax.axis_index("section")
    tp_id = lax.axis_index("tp")
    tp_count = lax.axis_size("tp")
    tokens, share_cols = prompt.shape
    share_rows = tokens // tp_count
    down_weight, query_weight, latent_weight = w_query_down[0], w_query[0], w_latent[0]
    key_weight, value_weight, out_weight = w_keys[0], w_values[0], w_out[0]
    down_cols, latent_cols = down_weight.shape[1], latent_weight.shape[1]
    head_count = query_weight.shape[1] // (NOPE_DIM + ROPE_DIM)
    scale_factor = (NOPE_DIM + ROPE_DIM) ** (-0.5)
    all_positions = jnp.arange(tokens, dtype=jnp.int32)
    end_rows = jnp.cumsum(block_sizes) - 1

    def shift(array, distance, routes):
        pairs = [
            (a * tp_count + i, b * tp_count + (i + distance) % tp_count)
            for a, b in routes
            for i in range(tp_count)
        ]
        return lax.ppermute(array, ("section", "tp"), pairs)

    def gather(array, where, axis):
        routes = [(s, s) for s in where]
        width = array.shape[axis]
        shape = list(array.shape)
        shape[axis] = width * tp_count
        whole = jnp.zeros(shape, array.dtype)
        for k in range(tp_count):
            piece = array if k == 0 else shift(array, k, routes)
            whole = lax.dynamic_update_slice_in_dim(
                whole, piece, lax.rem(tp_id - k + tp_count, tp_count) * width, axis
            )
        return whole

    def keys_and_values(cache):
        plain = cache[:, :LATENT]
        keys = dot(plain, key_weight).astype(BF16).reshape(tokens, head_count, NOPE_DIM)
        values = dot(plain, value_weight).astype(BF16).reshape(tokens, head_count, VALUE_DIM)
        return keys, values

    def attend(compressed, positions, cache):
        keys, values = keys_and_values(cache)
        rows = compressed.shape[0]
        queries = dot(compressed, query_weight).reshape(rows, head_count, NOPE_DIM + ROPE_DIM)
        queries = jnp.concatenate(
            [queries[..., :NOPE_DIM], rotate(queries[..., NOPE_DIM:], positions)], axis=-1
        ).astype(BF16)
        scores = jnp.einsum("ihd,jhd->hij", queries[..., :NOPE_DIM], keys, preferred_element_type=F32)
        scores = scores + jnp.einsum(
            "ihr,jr->hij", queries[..., NOPE_DIM:], cache[:, LATENT:], preferred_element_type=F32
        )
        visible = all_positions[None, :] <= positions[:, None]
        powered = jnp.where(visible[None], jnp.exp(scores * scale_factor), 0.0)
        attention = (powered / jnp.sum(powered, axis=-1, keepdims=True)).astype(BF16)
        mixed = jnp.einsum("hij,jhv->ihv", attention, values, preferred_element_type=F32)
        return dot(mixed.astype(BF16).reshape(rows, head_count * VALUE_DIM), out_weight)

    def layer(hidden, own_share, tick):
        normed = rms_rows(hidden.astype(F32)).astype(BF16)
        parts = jnp.concatenate(
            [dot(normed, down_weight).astype(BF16), dot(normed, latent_weight).astype(BF16)], axis=1
        )
        whole = gather(parts[None], [tick], 0).astype(F32)
        down = jnp.concatenate([whole[m, :, :down_cols] for m in range(tp_count)], axis=1)
        latent = jnp.concatenate([whole[m, :, down_cols:] for m in range(tp_count)], axis=1)
        compressed = rms_rows(down).astype(BF16)
        cache = jnp.concatenate(
            [rms_rows(latent[:, :LATENT]), rotate(latent[:, LATENT:], all_positions)], axis=-1
        ).astype(BF16)
        partial = attend(compressed, all_positions, cache)
        start = tp_id * share_cols
        mine = lax.dynamic_slice_in_dim(partial, start, share_cols, 1) + own_share.astype(F32)
        partial = lax.dynamic_update_slice_in_dim(partial, mine, start, 1).astype(BF16)
        return partial, cache

    def pass_on(partial, tick):
        ends = jnp.take(partial, end_rows, axis=0)
        total = 0.0
        for k in range(tp_count):
            first = lax.rem(tp_id + k, tp_count) * share_rows
            block = lax.dynamic_slice_in_dim(partial, first, share_rows, 0)
            block = jnp.concatenate([block, ends], axis=0)
            total = total + shift(block, k, [(tick, tick + 1)]).astype(F32)
        total = total.astype(BF16)
        return total[:share_rows], total[share_rows:]

    own_cache = jnp.zeros((share_rows, LATENT + ROPE_DIM), BF16)
    own_ends = jnp.zeros((block_sizes.shape[0], share_cols), BF16)
    last = sections - 1
    latent_whole = gather(latent_weight, range(1, sections), 1) if last else latent_weight
    hidden, own_share = gather(prompt, [0], 1), prompt
    for tick in range(last):
        partial, cache = layer(hidden, own_share, tick)
        mine = lax.dynamic_slice_in_dim(cache, tp_id * share_rows, share_rows, 0)
        own_cache = jnp.where(section_id == tick, mine, own_cache)
        rows, ends = pass_on(partial, tick)
        ends_share = lax.dynamic_slice_in_dim(ends, tp_id * share_cols, share_cols, 1)
        own_ends = jnp.where(section_id == tick, shift(ends_share, 0, [(tick + 1, tick)]), own_ends)
        if tick + 1 < last:
            hidden = gather(rows, [tick + 1], 0)
            own_share = lax.dynamic_slice_in_dim(hidden, tp_id * share_cols, share_cols, 1)

    row_positions = tp_id * share_rows + jnp.arange(share_rows, dtype=jnp.int32)
    latent = dot(rms_rows(rows.astype(F32)).astype(BF16), latent_whole)
    fresh = jnp.concatenate(
        [rms_rows(latent[:, :LATENT]), rotate(latent[:, LATENT:], row_positions)], axis=-1
    ).astype(BF16)
    own_cache = jnp.where(section_id == last, fresh, own_cache)
    down = dot(rms_rows(ends.astype(F32)).astype(BF16), down_weight).astype(BF16)
    down = jnp.pad(down, ((0, 0), (0, fresh.shape[1] - down_cols)))
    whole = gather(jnp.concatenate([fresh, down], axis=0)[None], [last], 0)
    cache = whole[:, :share_rows].reshape(tokens, LATENT + ROPE_DIM)
    down = jnp.concatenate([whole[m, share_rows:, :down_cols] for m in range(tp_count)], axis=1)
    compressed = rms_rows(down.astype(F32)).astype(BF16)
    partial = attend(compressed, end_rows, cache).astype(BF16)
    total = ends_share.astype(F32)
    for k in range(tp_count):
        start = lax.rem(tp_id + k, tp_count) * share_cols
        block = lax.dynamic_slice_in_dim(partial, start, share_cols, 1)
        total = total + (shift(block, k, [(last, last)]) if k else block).astype(F32)
    own_ends = jnp.where(section_id == last, total.astype(BF16), own_ends)
    return (own_cache[None], own_ends[None])


ROW_WIDTH = LATENT + ROPE_DIM
HEAD_WIDTH = NOPE_DIM + ROPE_DIM
HALF = ROPE_DIM // 2
SMEM = pl.BlockSpec(memory_space=pltpu.SMEM)
VMEM = pl.BlockSpec(memory_space=pltpu.VMEM)


def call(kernel, out_shape, args, scratch=(), flops=0, scalars=0, grant=8):
    many = isinstance(out_shape, list)
    moved = sum(a.size * a.dtype.itemsize for a in args)
    return pl.pallas_call(
        kernel,
        out_shape=out_shape,
        in_specs=[SMEM] * scalars + [VMEM] * (len(args) - scalars),
        out_specs=[VMEM] * len(out_shape) if many else VMEM,
        scratch_shapes=list(scratch),
        compiler_params=pltpu.CompilerParams(vmem_limit_bytes=grant * 2**20),
        cost_estimate=pl.CostEstimate(flops=flops, bytes_accessed=moved, transcendentals=0),
    )(*args)


def dot_t(a, b):
    return lax.dot_general(a, b, (((1,), (1,)), ((), ())), preferred_element_type=F32)


def unit(values):
    return lax.rsqrt(jnp.mean(values * values, axis=-1, keepdims=True) + EPSILON)


def turn(pair, angles):
    cosine, sine = angles[:, :HALF], angles[:, HALF:]
    a, b = pair[:, :HALF], pair[:, HALF:]
    return jnp.concatenate([a * cosine - b * sine, a * sine + b * cosine], axis=1)


def end_rows(sizes):
    ends = [sizes[0] - 1]
    for i in range(1, sizes.shape[0]):
        ends.append(ends[-1] + sizes[i])
    return ends


def column(scalars):
    rows = lax.broadcasted_iota(jnp.int32, (len(scalars), 1), 0)
    out = jnp.zeros((len(scalars), 1), jnp.int32)
    for i, value in enumerate(scalars):
        out = jnp.where(rows == i, value, out)
    return out


def send_kernel(prompt, w_latent, out):
    section, rep = lax.axis_index("section"), lax.axis_index("rep")
    rows, width = out.shape
    cols, model = w_latent.shape

    @pl.when(section == 0)
    def _():
        out[...] = prompt[...]

    @pl.when(section != 0)
    def _():
        first = (rep & 1) * (model // 2)
        half = w_latent[:, pl.ds(pl.multiple_of(first, 128), width + 256)].astype(F32)
        extra = half[:, width:]
        free = rows - cols
        left = cols - 2 * free
        tail = [extra[2 * free :, :128], extra[2 * free :, 128:], jnp.zeros((free - 2 * left, 128), F32)]
        extra = jnp.concatenate(
            [extra[:free], extra[free : 2 * free], jnp.concatenate(tail, axis=0)], axis=1
        )
        out[...] = jnp.concatenate([half[:, :width], extra], axis=0).astype(BF16)


def unpack_share(share, cols):
    share = share.astype(F32)
    free = share.shape[0] - cols
    left = cols - 2 * free
    extra, tail = share[cols:, :512], share[cols:, 512:]
    tail = jnp.concatenate([tail[:left], tail[left : 2 * left]], axis=1)
    extra = jnp.concatenate([extra[:, :256], extra[:, 256:], tail], axis=0)
    return jnp.concatenate([share[:cols], extra], axis=1).astype(BF16)


def down_kernel(own, three, two, one, w_down, w_latent, out):
    section, tp, rep = (lax.axis_index(a) for a in ("section", "tp", "rep"))
    tokens, share = own.shape
    cols, model = w_latent.shape
    third = tokens // 3

    @pl.when(section == 0)
    def _():
        squares, down, latent = 0.0, 0.0, 0.0
        for k, ref in enumerate((own, one, two, three)):
            columns = pl.ds(pl.multiple_of((tp ^ k) * share, 128), share)
            piece = ref[...]
            wide = piece.astype(F32)
            squares = squares + jnp.sum(wide * wide, axis=1, keepdims=True)
            down = down + dot_t(piece, w_down[:, columns])
            latent = latent + dot_t(piece, w_latent[:, columns])
        scale = lax.rsqrt(squares / model + EPSILON)
        parts = jnp.concatenate([down * scale, latent * scale], axis=1)
        rest = parts[:, 256:]
        rest = [rest[i * third : (i + 1) * third] for i in range(3)]
        rest.append(jnp.zeros((third, 256 - 3 * rest[0].shape[1]), F32))
        out[...] = jnp.concatenate([parts[:, :256], jnp.concatenate(rest, axis=1)], axis=0).astype(BF16)

    @pl.when(section != 0)
    def _():
        first = ((rep & 1) + 1) * (model // 2) - 384
        mine = w_latent[:, pl.ds(pl.multiple_of(first, 128), 384)].astype(F32)
        rest = mine[:, 256:]
        high = cols // 2 + 4
        lower = jnp.concatenate([rest[high:], jnp.zeros((2 * high - cols, 128), F32)], axis=0)
        rest = jnp.concatenate([rest[:high], lower], axis=1)
        blank = jnp.zeros((out.shape[0] - cols - high, 256), F32)
        out[...] = jnp.concatenate([mine[:, :256], rest, blank], axis=0).astype(BF16)


def unpack_rest(piece, cols):
    piece = piece.astype(F32)
    high = cols // 2 + 4
    rest = piece[cols : cols + high]
    rest = jnp.concatenate([rest[:, :128], rest[: cols - high, 128:]], axis=0)
    return jnp.concatenate([piece[:cols], rest], axis=1).astype(BF16)


def unpack_parts(piece, tokens, width):
    piece = piece.astype(F32)
    rest, size = piece[tokens:], width - 256
    rest = jnp.concatenate([rest[:, i * size : (i + 1) * size] for i in range(3)], axis=0)
    return jnp.concatenate([piece[:tokens], rest], axis=1)


def attend_rows(compressed, cache, seen, angles, w_query, w_keys, w_values):
    plain, turned = cache[:, :LATENT], cache[:, LATENT:]
    keys = dot(plain, w_keys[...]).astype(BF16)
    values = dot(plain, w_values[...]).astype(BF16)
    queries = dot(compressed, w_query[...])
    mixed = []
    for head in range(queries.shape[1] // HEAD_WIDTH):
        query = queries[:, head * HEAD_WIDTH : (head + 1) * HEAD_WIDTH]
        query = jnp.concatenate(
            [query[:, :NOPE_DIM], turn(query[:, NOPE_DIM:], angles)], axis=1
        ).astype(BF16)
        key = jnp.concatenate([keys[:, head * NOPE_DIM : (head + 1) * NOPE_DIM], turned], axis=1)
        scores = dot_t(query, key) * HEAD_WIDTH**-0.5
        powered = jnp.where(seen, jnp.exp(scores), 0.0)
        attention = (powered / jnp.sum(powered, axis=1, keepdims=True)).astype(BF16)
        mixed.append(dot(attention, values[:, head * VALUE_DIM : (head + 1) * VALUE_DIM]))
    return jnp.concatenate(mixed, axis=1).astype(BF16)


def layer_kernel(
    sizes, own, one, two, three, share1, w_latent, prompt, angles,
    w_query, w_keys, w_values, w_out, out0, out1, out2, out3, own_cache, passed, rest, stack, total, cached,
):
    section, tp, rep = (lax.axis_index(a) for a in ("section", "tp", "rep"))
    tokens, width = prompt.shape
    block = tokens // 4
    cols, early = passed.shape[1:]
    down_cols = w_query.shape[0] // 4

    @pl.when(section != 0)
    def _():
        first = (rep & 1) * (early + rest.shape[2])
        passed[0] = w_latent[:, pl.ds(pl.multiple_of(first, 128), early)]
        passed[1] = unpack_share(share1[...], cols)
        for k, ref in enumerate((one, two, three)):
            rest[k] = unpack_rest(ref[...], cols)

    @pl.when(section == 0)
    def _():
        ends = column(end_rows(sizes))
        for k, ref in enumerate((own, one, two, three)):
            stack[tp ^ k] = ref[...]
        pieces = [unpack_parts(stack[m], tokens, down_cols + cols) for m in range(4)]
        down = jnp.concatenate([p[:, :down_cols] for p in pieces], axis=1)
        latent = jnp.concatenate([p[:, down_cols:] for p in pieces], axis=1)
        compressed = (down * unit(down)).astype(BF16)
        plain = latent[:, :LATENT]
        cache = jnp.concatenate(
            [plain * unit(plain), turn(latent[:, LATENT:], angles[...])], axis=1
        ).astype(BF16)
        cached[...] = cache
        own_cache[...] = cached[pl.ds(pl.multiple_of(tp * block, block), block), :]
        seen = lax.broadcasted_iota(jnp.int32, (tokens, tokens), 0) >= lax.broadcasted_iota(
            jnp.int32, (tokens, tokens), 1
        )
        mixed = attend_rows(compressed, cache, seen, angles[...], w_query, w_keys, w_values)
        chosen = lax.broadcasted_iota(jnp.int32, (ends.shape[0], tokens), 1) == ends
        chosen = chosen.astype(BF16)
        rows = jnp.concatenate([mixed, dot(chosen, mixed).astype(BF16)], axis=0)
        total[...] = dot(rows, w_out[...])
        mine = pl.ds(pl.multiple_of(tp * width, 128), width)
        added = jnp.concatenate([prompt[...].astype(F32), dot(chosen, prompt[...])], axis=0)
        total[:, mine] += added
        last = total[tokens:, :]
        for k, out in enumerate((out0, out1, out2, out3)):
            part = total[pl.ds(pl.multiple_of((tp ^ k) * block, block), block), :]
            out[...] = jnp.concatenate([part, last], axis=0).astype(BF16)


def latent_kernel(
    one, two, three, four, angles, w_latent, first1, first2, first3, rest,
    near1, near2, near3, near_rest, w_down, out, own_cache, own_ends, hidden, parts,
):
    tp, rep = lax.axis_index("tp"), lax.axis_index("rep")
    block = angles.shape[0] // 4
    width = own_ends.shape[1]
    model = w_latent.shape[1]
    early = first1.shape[1]
    rows = one[...].astype(F32) + two[...].astype(F32) + three[...].astype(F32) + four[...].astype(F32)
    narrow = rows.astype(BF16)
    rows = narrow.astype(F32)
    hidden[...] = rows
    scale = unit(rows)
    parts[tp] = dot_t(narrow[:block], w_latent[...])
    sums = [0.0, 0.0, 0.0]
    for core, weights in enumerate(
        (
            (first1, first2, first3, rest),
            (near1, near2, near3, near_rest),
        )
    ):
        first = ((rep & 1) ^ core) * (model // 2)
        head = hidden[0:block, pl.ds(pl.multiple_of(first, 128), early)].astype(BF16)
        late = pl.ds(pl.multiple_of(first + early, 128), model // 2 - early)
        tail = hidden[0:block, late].astype(BF16)
        for k in range(3):
            sums[k] += dot_t(head, weights[k][...]) + dot_t(tail, weights[3][k])
    for k, value in enumerate(sums):
        parts[tp ^ (k + 1)] = value
    latent = jnp.concatenate([parts[m] for m in range(4)], axis=1) * scale[:block]
    plain = latent[:, :LATENT]
    plain = plain * unit(plain)
    own_angles = angles[pl.ds(pl.multiple_of(tp * block, block), block), :]
    turned = turn(latent[:, LATENT:], own_angles)
    own_cache[...] = jnp.concatenate([plain, turned], axis=1).astype(BF16)
    down = dot_t(narrow[block:, :], w_down[...]) * scale[block:]
    count = down.shape[0]
    turned = [turned[i * count : (i + 1) * count] for i in range(block // count)]
    last = jnp.concatenate([*turned, down], axis=1)
    last = jnp.concatenate([last, jnp.zeros((count, LATENT - last.shape[1]), F32)], axis=1)
    out[...] = jnp.concatenate([plain, last], axis=0).astype(BF16)
    mine = pl.ds(pl.multiple_of(tp * width, 128), width)
    own_ends[...] = hidden[block:, mine].astype(BF16)


def ends_kernel(
    sizes, own, three, two, one, angles, w_query, w_keys, w_values, out, stack
):
    tp = lax.axis_index("tp")
    ends = end_rows(sizes)
    count = len(ends)
    block = own.shape[0] - count
    steps = block // count
    down_cols = w_query.shape[0] // 4
    for k, ref in enumerate((own, one, two, three)):
        stack[tp ^ k] = ref[...].astype(F32)
    pieces = [stack[m] for m in range(4)]
    plain = jnp.concatenate([p[:block] for p in pieces], axis=0)
    last = [p[block:] for p in pieces]
    turned = jnp.concatenate(
        [p[:, i * ROPE_DIM : (i + 1) * ROPE_DIM] for p in last for i in range(steps)], axis=0
    )
    cache = jnp.concatenate([plain, turned], axis=1).astype(BF16)
    first = steps * ROPE_DIM
    down = jnp.concatenate([p[:, first : first + down_cols] for p in last], axis=1)
    compressed = (down * unit(down)).astype(BF16)
    end_angles = jnp.concatenate([angles[pl.ds(e, 1), :] for e in ends], axis=0)
    seen = lax.broadcasted_iota(jnp.int32, (count, 4 * block), 1) <= column(ends)
    out[...] = attend_rows(compressed, cache, seen, end_angles, w_query, w_keys, w_values)


def final_kernel(mixed, w_out, out0, out1, out2, out3, total):
    tp = lax.axis_index("tp")
    width = out0.shape[1]
    total[...] = dot(mixed[...], w_out[...])
    for k, out in enumerate((out0, out1, out2, out3)):
        columns = pl.ds(pl.multiple_of((tp ^ k) * width, 128), width)
        out[...] = total[:, columns].astype(BF16)


def local_two(prompt, block_sizes, w_query_down, w_query, w_latent, w_keys, w_values, w_out):
    section = lax.axis_index("section")
    tokens, share = prompt.shape
    block = tokens // 4
    count = block_sizes.shape[0]
    w_down, w_up, w_lat = w_query_down[0].T, w_query[0], w_latent[0].T
    w_key, w_value, w_final = w_keys[0], w_values[0], w_out[0]
    down_cols, latent_cols = w_down.shape[0], w_lat.shape[0]
    model = 4 * share
    frequency = 10000.0 ** (-2.0 * np.arange(HALF, dtype=np.float32) / ROPE_DIM)
    angles = np.arange(tokens, dtype=np.float32)[:, None] * frequency.astype(np.float32)[None, :]
    angles = jnp.asarray(np.concatenate([np.cos(angles), np.sin(angles)], axis=1), F32)

    def route(array, *ways):
        pairs = []
        for s, way in enumerate(ways):
            if way:
                to, k, r = (*way, 0)[:3]
                pairs += [
                    ((s * 4 + i) * 4 + j, (to * 4 + (i ^ k)) * 4 + (j ^ r)) for i in range(4) for j in range(4)
                ]
        return lax.ppermute(array, ("section", "tp", "rep"), pairs)

    def within(array, k):
        return route(array, (0, k), (1, k))

    def onward(array, k):
        return route(array, (1, k), (0, 0))

    def over_rep(array, k):
        return lax.ppermute(array, "rep", [(i, i ^ k) for i in range(4)])

    sent = call(
        send_kernel,
        jax.ShapeDtypeStruct((tokens, share), BF16),
        [prompt, w_lat],
        grant=8,
        flops=2 * 10**10,
    )
    two = route(prompt, (1, 0), (0, 2))
    three = route(prompt, (0, 3), (1, 0, 1))
    one = route(sent, (0, 1), (1, 1))
    parts = call(
        down_kernel,
        jax.ShapeDtypeStruct((tokens + tokens // 3, 256), BF16),
        [prompt, three, two, one, w_down, w_lat],
        flops=2 * 10**10,
    )
    pieces = [parts] + [within(parts, k) for k in (1, 2, 3)]

    message = jax.ShapeDtypeStruct((block + count, model), BF16)
    *blocks, first_cache, passed, rest = call(
        layer_kernel,
        [message] * 4
        + [
            jax.ShapeDtypeStruct((block, ROW_WIDTH), BF16),
            jax.ShapeDtypeStruct((2, latent_cols, model // 2 - 384), BF16),
            jax.ShapeDtypeStruct((3, latent_cols, 384), BF16),
        ],
        [block_sizes, *pieces, one, w_lat, prompt, angles, w_up, w_key, w_value, w_final],
        [
            pltpu.VMEM((4, *parts.shape), BF16),
            pltpu.VMEM((tokens + count, model), F32),
            pltpu.VMEM((tokens, ROW_WIDTH), BF16),
        ],
        flops=2 * tokens * (w_up.size + w_key.size + w_value.size + w_final.size),
        scalars=1,
        grant=16,
    )
    arrived = [onward(blocks[k], k) for k in (2, 1, 3, 0)]
    relayed = route(passed, None, (1, 2))
    relayed, late, first = lax.optimization_barrier((relayed, rest, passed[1]))
    weights = [first, relayed[0], relayed[1], late]
    weights += [over_rep(w, 1) for w in weights]
    fresh, last_cache, ends_share = call(
        latent_kernel,
        [
            jax.ShapeDtypeStruct((block + count, LATENT), BF16),
            jax.ShapeDtypeStruct((block, ROW_WIDTH), BF16),
            jax.ShapeDtypeStruct((count, share), BF16),
        ],
        [*arrived, angles, w_lat, *weights, w_down],
        [pltpu.VMEM((block + count, model), F32), pltpu.VMEM((4, block, latent_cols), F32)],
        flops=2 * 10**11,
    )
    pieces = [fresh] + [within(fresh, k) for k in (3, 2, 1)]
    first_ends = onward(ends_share, 0)
    mixed = call(
        ends_kernel,
        jax.ShapeDtypeStruct((count, w_final.shape[0]), BF16),
        [block_sizes, *pieces, angles, w_up, w_key, w_value],
        [pltpu.VMEM((4, block + count, LATENT), F32)],
        flops=2 * 10**10,
        scalars=1,
    )
    outs = call(
        final_kernel,
        [jax.ShapeDtypeStruct((count, share), BF16)] * 4,
        [mixed, w_final],
        [pltpu.VMEM((count, model), F32)],
        flops=10**8,
    )
    total = ends_share.astype(F32) + outs[0].astype(F32)
    for k in (1, 2, 3):
        total = total + within(outs[k], k).astype(F32)
    own_ends = jnp.where(section == 0, first_ends, total.astype(BF16))
    own_cache = jnp.where(section == 0, first_cache, last_cache)
    return (own_cache[None], own_ends[None])


def solution(mesh):
    sizes = [mesh.shape[a] for a in ("section", "tp", "rep")]
    body = local_two if sizes == [2, 4, 4] else local
    in_specs = (
        P("rep", "tp"),
        P("rep"),
        P("section", None, "tp"),
        P("section", None, "tp"),
        P("section", None, "tp"),
        P("section", None, "tp"),
        P("section", None, "tp"),
        P("section", "tp", None),
    )
    out_specs = (P("section", ("rep", "tp"), None), P("section", "rep", "tp"))
    return jax.shard_map(body, mesh=mesh, in_specs=in_specs, out_specs=out_specs, check_vma=False)
```

```python
import jax
import jax.numpy as jnp
import numpy as np
from jax import lax
from jax.experimental import pallas as pl
from jax.experimental.pallas import tpu as pltpu
from jax.sharding import PartitionSpec as P

NOPE_DIM = 128
ROPE_DIM = 32
VALUE_DIM = 128
LATENT = 512
EPSILON = 1e-06
F32 = jnp.float32
BF16 = jnp.bfloat16


def rms_rows(values):
    return values * lax.rsqrt(jnp.mean(values * values, axis=-1, keepdims=True) + EPSILON)


def rotate(values, positions):
    half_width = values.shape[-1] // 2
    frequency = 10000.0 ** (-2.0 * jnp.arange(half_width, dtype=F32) / values.shape[-1])
    angles = positions.astype(F32)[:, None] * frequency[None, :]
    if values.ndim == 3:
        angles = angles[:, None, :]
    cosine = jnp.cos(angles)
    sine_part = jnp.sin(angles)
    first_half = values[..., :half_width]
    second = values[..., half_width:]
    return jnp.concatenate(
        [first_half * cosine - second * sine_part, first_half * sine_part + second * cosine],
        axis=-1,
    )


def dot(a, b):
    return jnp.dot(a, b, preferred_element_type=F32)


def local(prompt, block_sizes, w_query_down, w_query, w_latent, w_keys, w_values, w_out):
    sections = lax.axis_size("section")
    section_id = lax.axis_index("section")
    tp_id = lax.axis_index("tp")
    tp_count = lax.axis_size("tp")
    tokens, share_cols = prompt.shape
    share_rows = tokens // tp_count
    down_weight, query_weight, latent_weight = w_query_down[0], w_query[0], w_latent[0]
    key_weight, value_weight, out_weight = w_keys[0], w_values[0], w_out[0]
    down_cols, latent_cols = down_weight.shape[1], latent_weight.shape[1]
    head_count = query_weight.shape[1] // (NOPE_DIM + ROPE_DIM)
    scale_factor = (NOPE_DIM + ROPE_DIM) ** (-0.5)
    all_positions = jnp.arange(tokens, dtype=jnp.int32)
    end_rows = jnp.cumsum(block_sizes) - 1

    def shift(array, distance, routes):
        pairs = [
            (a * tp_count + i, b * tp_count + (i + distance) % tp_count)
            for a, b in routes
            for i in range(tp_count)
        ]
        return lax.ppermute(array, ("section", "tp"), pairs)

    def gather(array, where, axis):
        routes = [(s, s) for s in where]
        width = array.shape[axis]
        shape = list(array.shape)
        shape[axis] = width * tp_count
        whole = jnp.zeros(shape, array.dtype)
        for k in range(tp_count):
            piece = array if k == 0 else shift(array, k, routes)
            whole = lax.dynamic_update_slice_in_dim(
                whole, piece, lax.rem(tp_id - k + tp_count, tp_count) * width, axis
            )
        return whole

    def keys_and_values(cache):
        plain = cache[:, :LATENT]
        keys = dot(plain, key_weight).astype(BF16).reshape(tokens, head_count, NOPE_DIM)
        values = dot(plain, value_weight).astype(BF16).reshape(tokens, head_count, VALUE_DIM)
        return keys, values

    def attend(compressed, positions, cache):
        keys, values = keys_and_values(cache)
        rows = compressed.shape[0]
        queries = dot(compressed, query_weight).reshape(rows, head_count, NOPE_DIM + ROPE_DIM)
        queries = jnp.concatenate(
            [queries[..., :NOPE_DIM], rotate(queries[..., NOPE_DIM:], positions)], axis=-1
        ).astype(BF16)
        scores = jnp.einsum("ihd,jhd->hij", queries[..., :NOPE_DIM], keys, preferred_element_type=F32)
        scores = scores + jnp.einsum(
            "ihr,jr->hij", queries[..., NOPE_DIM:], cache[:, LATENT:], preferred_element_type=F32
        )
        visible = all_positions[None, :] <= positions[:, None]
        powered = jnp.where(visible[None], jnp.exp(scores * scale_factor), 0.0)
        attention = (powered / jnp.sum(powered, axis=-1, keepdims=True)).astype(BF16)
        mixed = jnp.einsum("hij,jhv->ihv", attention, values, preferred_element_type=F32)
        return dot(mixed.astype(BF16).reshape(rows, head_count * VALUE_DIM), out_weight)

    def layer(hidden, own_share, tick):
        normed = rms_rows(hidden.astype(F32)).astype(BF16)
        parts = jnp.concatenate(
            [dot(normed, down_weight).astype(BF16), dot(normed, latent_weight).astype(BF16)], axis=1
        )
        whole = gather(parts[None], [tick], 0).astype(F32)
        down = jnp.concatenate([whole[m, :, :down_cols] for m in range(tp_count)], axis=1)
        latent = jnp.concatenate([whole[m, :, down_cols:] for m in range(tp_count)], axis=1)
        compressed = rms_rows(down).astype(BF16)
        cache = jnp.concatenate(
            [rms_rows(latent[:, :LATENT]), rotate(latent[:, LATENT:], all_positions)], axis=-1
        ).astype(BF16)
        partial = attend(compressed, all_positions, cache)
        start = tp_id * share_cols
        mine = lax.dynamic_slice_in_dim(partial, start, share_cols, 1) + own_share.astype(F32)
        partial = lax.dynamic_update_slice_in_dim(partial, mine, start, 1).astype(BF16)
        return partial, cache

    def pass_on(partial, tick):
        ends = jnp.take(partial, end_rows, axis=0)
        total = 0.0
        for k in range(tp_count):
            first = lax.rem(tp_id + k, tp_count) * share_rows
            block = lax.dynamic_slice_in_dim(partial, first, share_rows, 0)
            block = jnp.concatenate([block, ends], axis=0)
            total = total + shift(block, k, [(tick, tick + 1)]).astype(F32)
        total = total.astype(BF16)
        return total[:share_rows], total[share_rows:]

    own_cache = jnp.zeros((share_rows, LATENT + ROPE_DIM), BF16)
    own_ends = jnp.zeros((block_sizes.shape[0], share_cols), BF16)
    last = sections - 1
    latent_whole = gather(latent_weight, range(1, sections), 1) if last else latent_weight
    hidden, own_share = gather(prompt, [0], 1), prompt
    for tick in range(last):
        partial, cache = layer(hidden, own_share, tick)
        mine = lax.dynamic_slice_in_dim(cache, tp_id * share_rows, share_rows, 0)
        own_cache = jnp.where(section_id == tick, mine, own_cache)
        rows, ends = pass_on(partial, tick)
        ends_share = lax.dynamic_slice_in_dim(ends, tp_id * share_cols, share_cols, 1)
        own_ends = jnp.where(section_id == tick, shift(ends_share, 0, [(tick + 1, tick)]), own_ends)
        if tick + 1 < last:
            hidden = gather(rows, [tick + 1], 0)
            own_share = lax.dynamic_slice_in_dim(hidden, tp_id * share_cols, share_cols, 1)

    row_positions = tp_id * share_rows + jnp.arange(share_rows, dtype=jnp.int32)
    latent = dot(rms_rows(rows.astype(F32)).astype(BF16), latent_whole)
    fresh = jnp.concatenate(
        [rms_rows(latent[:, :LATENT]), rotate(latent[:, LATENT:], row_positions)], axis=-1
    ).astype(BF16)
    own_cache = jnp.where(section_id == last, fresh, own_cache)
    down = dot(rms_rows(ends.astype(F32)).astype(BF16), down_weight).astype(BF16)
    down = jnp.pad(down, ((0, 0), (0, fresh.shape[1] - down_cols)))
    whole = gather(jnp.concatenate([fresh, down], axis=0)[None], [last], 0)
    cache = whole[:, :share_rows].reshape(tokens, LATENT + ROPE_DIM)
    down = jnp.concatenate([whole[m, share_rows:, :down_cols] for m in range(tp_count)], axis=1)
    compressed = rms_rows(down.astype(F32)).astype(BF16)
    partial = attend(compressed, end_rows, cache).astype(BF16)
    total = ends_share.astype(F32)
    for k in range(tp_count):
        start = lax.rem(tp_id + k, tp_count) * share_cols
        block = lax.dynamic_slice_in_dim(partial, start, share_cols, 1)
        total = total + (shift(block, k, [(last, last)]) if k else block).astype(F32)
    own_ends = jnp.where(section_id == last, total.astype(BF16), own_ends)
    return (own_cache[None], own_ends[None])


ROW_WIDTH = LATENT + ROPE_DIM
HEAD_WIDTH = NOPE_DIM + ROPE_DIM
HALF = ROPE_DIM // 2
SMEM = pl.BlockSpec(memory_space=pltpu.SMEM)
VMEM = pl.BlockSpec(memory_space=pltpu.VMEM)


def call(kernel, out_shape, args, scratch=(), flops=0, scalars=0, grant=8):
    many = isinstance(out_shape, list)
    moved = sum(a.size * a.dtype.itemsize for a in args)
    return pl.pallas_call(
        kernel,
        out_shape=out_shape,
        in_specs=[SMEM] * scalars + [VMEM] * (len(args) - scalars),
        out_specs=[VMEM] * len(out_shape) if many else VMEM,
        scratch_shapes=list(scratch),
        compiler_params=pltpu.CompilerParams(vmem_limit_bytes=grant * 2**20),
        cost_estimate=pl.CostEstimate(flops=flops, bytes_accessed=moved, transcendentals=0),
    )(*args)


def dot_t(a, b):
    return lax.dot_general(a, b, (((1,), (1,)), ((), ())), preferred_element_type=F32)


def unit(values):
    return lax.rsqrt(jnp.mean(values * values, axis=-1, keepdims=True) + EPSILON)


def turn(pair, angles):
    cosine, sine = angles[:, :HALF], angles[:, HALF:]
    a, b = pair[:, :HALF], pair[:, HALF:]
    return jnp.concatenate([a * cosine - b * sine, a * sine + b * cosine], axis=1)


def end_rows(sizes):
    ends = [sizes[0] - 1]
    for i in range(1, sizes.shape[0]):
        ends.append(ends[-1] + sizes[i])
    return ends


def column(scalars):
    rows = lax.broadcasted_iota(jnp.int32, (len(scalars), 1), 0)
    out = jnp.zeros((len(scalars), 1), jnp.int32)
    for i, value in enumerate(scalars):
        out = jnp.where(rows == i, value, out)
    return out


def send_kernel(prompt, w_latent, out):
    section, rep = lax.axis_index("section"), lax.axis_index("rep")
    rows, width = out.shape
    cols, model = w_latent.shape

    @pl.when(section == 0)
    def _():
        out[...] = prompt[...]

    @pl.when(section != 0)
    def _():
        first = (rep & 1) * (model // 2)
        half = w_latent[:, pl.ds(pl.multiple_of(first, 128), width + 256)].astype(F32)
        extra = half[:, width:]
        free = rows - cols
        left = cols - 2 * free
        tail = [extra[2 * free :, :128], extra[2 * free :, 128:], jnp.zeros((free - 2 * left, 128), F32)]
        extra = jnp.concatenate(
            [extra[:free], extra[free : 2 * free], jnp.concatenate(tail, axis=0)], axis=1
        )
        out[...] = jnp.concatenate([half[:, :width], extra], axis=0).astype(BF16)


def unpack_share(share, cols):
    share = share.astype(F32)
    free = share.shape[0] - cols
    left = cols - 2 * free
    extra, tail = share[cols:, :512], share[cols:, 512:]
    tail = jnp.concatenate([tail[:left], tail[left : 2 * left]], axis=1)
    extra = jnp.concatenate([extra[:, :256], extra[:, 256:], tail], axis=0)
    return jnp.concatenate([share[:cols], extra], axis=1).astype(BF16)


def down_kernel(own, three, two, one, w_down, w_latent, out):
    section, tp, rep = (lax.axis_index(a) for a in ("section", "tp", "rep"))
    tokens, share = own.shape
    cols, model = w_latent.shape
    third = tokens // 3

    @pl.when(section == 0)
    def _():
        squares, down, latent = 0.0, 0.0, 0.0
        for k, ref in enumerate((own, one, two, three)):
            columns = pl.ds(pl.multiple_of((tp ^ k) * share, 128), share)
            piece = ref[...]
            wide = piece.astype(F32)
            squares = squares + jnp.sum(wide * wide, axis=1, keepdims=True)
            down = down + dot_t(piece, w_down[:, columns])
            latent = latent + dot_t(piece, w_latent[:, columns])
        scale = lax.rsqrt(squares / model + EPSILON)
        parts = jnp.concatenate([down * scale, latent * scale], axis=1)
        rest = parts[:, 256:]
        rest = [rest[i * third : (i + 1) * third] for i in range(3)]
        rest.append(jnp.zeros((third, 256 - 3 * rest[0].shape[1]), F32))
        out[...] = jnp.concatenate([parts[:, :256], jnp.concatenate(rest, axis=1)], axis=0).astype(BF16)

    @pl.when(section != 0)
    def _():
        first = ((rep & 1) + 1) * (model // 2) - 384
        mine = w_latent[:, pl.ds(pl.multiple_of(first, 128), 384)].astype(F32)
        rest = mine[:, 256:]
        high = cols // 2 + 4
        lower = jnp.concatenate([rest[high:], jnp.zeros((2 * high - cols, 128), F32)], axis=0)
        rest = jnp.concatenate([rest[:high], lower], axis=1)
        blank = jnp.zeros((out.shape[0] - cols - high, 256), F32)
        out[...] = jnp.concatenate([mine[:, :256], rest, blank], axis=0).astype(BF16)


def unpack_rest(piece, cols):
    piece = piece.astype(F32)
    high = cols // 2 + 4
    rest = piece[cols : cols + high]
    rest = jnp.concatenate([rest[:, :128], rest[: cols - high, 128:]], axis=0)
    return jnp.concatenate([piece[:cols], rest], axis=1).astype(BF16)


def unpack_parts(piece, tokens, width):
    piece = piece.astype(F32)
    rest, size = piece[tokens:], width - 256
    rest = jnp.concatenate([rest[:, i * size : (i + 1) * size] for i in range(3)], axis=0)
    return jnp.concatenate([piece[:tokens], rest], axis=1)


def attend_rows(compressed, cache, seen, angles, w_query, w_keys, w_values):
    plain, turned = cache[:, :LATENT], cache[:, LATENT:]
    keys = dot(plain, w_keys[...]).astype(BF16)
    values = dot(plain, w_values[...]).astype(BF16)
    queries = dot(compressed, w_query[...])
    mixed = []
    for head in range(queries.shape[1] // HEAD_WIDTH):
        query = queries[:, head * HEAD_WIDTH : (head + 1) * HEAD_WIDTH]
        query = jnp.concatenate(
            [query[:, :NOPE_DIM], turn(query[:, NOPE_DIM:], angles)], axis=1
        ).astype(BF16)
        key = jnp.concatenate([keys[:, head * NOPE_DIM : (head + 1) * NOPE_DIM], turned], axis=1)
        scores = dot_t(query, key) * HEAD_WIDTH**-0.5
        powered = jnp.where(seen, jnp.exp(scores), 0.0)
        attention = (powered / jnp.sum(powered, axis=1, keepdims=True)).astype(BF16)
        mixed.append(dot(attention, values[:, head * VALUE_DIM : (head + 1) * VALUE_DIM]))
    return jnp.concatenate(mixed, axis=1).astype(BF16)


def layer_kernel(
    sizes, own, two, one, three, share1, w_latent, prompt, angles,
    w_query, w_keys, w_values, w_out, out0, out1, out2, out3, own_cache, passed, rest, stack, total, cached,
):
    section, tp, rep = (lax.axis_index(a) for a in ("section", "tp", "rep"))
    tokens, width = prompt.shape
    block = tokens // 4
    cols, early = passed.shape[1:]
    down_cols = w_query.shape[0] // 4

    @pl.when(section != 0)
    def _():
        first = (rep & 1) * (early + rest.shape[2])
        passed[0] = w_latent[:, pl.ds(pl.multiple_of(first, 128), early)]
        passed[1] = unpack_share(share1[...], cols)
        for k, ref in enumerate((one, two, three)):
            rest[k] = unpack_rest(ref[...], cols)

    @pl.when(section == 0)
    def _():
        ends = column(end_rows(sizes))
        for k, ref in enumerate((own, one, two, three)):
            stack[tp ^ k] = ref[...]
        pieces = [unpack_parts(stack[m], tokens, down_cols + cols) for m in range(4)]
        down = jnp.concatenate([p[:, :down_cols] for p in pieces], axis=1)
        latent = jnp.concatenate([p[:, down_cols:] for p in pieces], axis=1)
        compressed = (down * unit(down)).astype(BF16)
        plain = latent[:, :LATENT]
        cache = jnp.concatenate(
            [plain * unit(plain), turn(latent[:, LATENT:], angles[...])], axis=1
        ).astype(BF16)
        cached[...] = cache
        own_cache[...] = cached[pl.ds(pl.multiple_of(tp * block, block), block), :]
        seen = lax.broadcasted_iota(jnp.int32, (tokens, tokens), 0) >= lax.broadcasted_iota(
            jnp.int32, (tokens, tokens), 1
        )
        mixed = attend_rows(compressed, cache, seen, angles[...], w_query, w_keys, w_values)
        chosen = lax.broadcasted_iota(jnp.int32, (ends.shape[0], tokens), 1) == ends
        chosen = chosen.astype(BF16)
        rows = jnp.concatenate([mixed, dot(chosen, mixed).astype(BF16)], axis=0)
        total[...] = dot(rows, w_out[...])
        mine = pl.ds(pl.multiple_of(tp * width, 128), width)
        added = jnp.concatenate([prompt[...].astype(F32), dot(chosen, prompt[...])], axis=0)
        total[:, mine] += added
        last = total[tokens:, :]
        for k, out in enumerate((out0, out1, out2, out3)):
            part = total[pl.ds(pl.multiple_of((tp ^ k) * block, block), block), :]
            out[...] = jnp.concatenate([part, last], axis=0).astype(BF16)


def latent_kernel(
    one, two, three, four, angles, w_latent, first1, first2, first3, rest,
    near1, near2, near3, near_rest, w_down, out, own_cache, own_ends, hidden, parts,
):
    tp, rep = lax.axis_index("tp"), lax.axis_index("rep")
    block = angles.shape[0] // 4
    width = own_ends.shape[1]
    model = w_latent.shape[1]
    early = first1.shape[1]
    rows = one[...].astype(F32) + two[...].astype(F32) + three[...].astype(F32) + four[...].astype(F32)
    narrow = rows.astype(BF16)
    rows = narrow.astype(F32)
    hidden[...] = rows
    scale = unit(rows)
    parts[tp] = dot_t(narrow[:block], w_latent[...])
    sums = [0.0, 0.0, 0.0]
    for core, weights in enumerate(
        (
            (first1, first2, first3, rest),
            (near1, near2, near3, near_rest),
        )
    ):
        first = ((rep & 1) ^ core) * (model // 2)
        head = hidden[0:block, pl.ds(pl.multiple_of(first, 128), early)].astype(BF16)
        late = pl.ds(pl.multiple_of(first + early, 128), model // 2 - early)
        tail = hidden[0:block, late].astype(BF16)
        for k in range(3):
            sums[k] += dot_t(head, weights[k][...]) + dot_t(tail, weights[3][k])
    for k, value in enumerate(sums):
        parts[tp ^ (k + 1)] = value
    latent = jnp.concatenate([parts[m] for m in range(4)], axis=1) * scale[:block]
    plain = latent[:, :LATENT]
    plain = plain * unit(plain)
    own_angles = angles[pl.ds(pl.multiple_of(tp * block, block), block), :]
    turned = turn(latent[:, LATENT:], own_angles)
    own_cache[...] = jnp.concatenate([plain, turned], axis=1).astype(BF16)
    down = dot_t(narrow[block:, :], w_down[...]) * scale[block:]
    count = down.shape[0]
    turned = [turned[i * count : (i + 1) * count] for i in range(block // count)]
    last = jnp.concatenate([*turned, down], axis=1)
    last = jnp.concatenate([last, jnp.zeros((count, LATENT - last.shape[1]), F32)], axis=1)
    out[...] = jnp.concatenate([plain, last], axis=0).astype(BF16)
    mine = pl.ds(pl.multiple_of(tp * width, 128), width)
    own_ends[...] = hidden[block:, mine].astype(BF16)


def ends_kernel(
    sizes, own, three, two, one, angles, w_query, w_keys, w_values, out, stack
):
    tp = lax.axis_index("tp")
    ends = end_rows(sizes)
    count = len(ends)
    block = own.shape[0] - count
    steps = block // count
    down_cols = w_query.shape[0] // 4
    for k, ref in enumerate((own, one, two, three)):
        stack[tp ^ k] = ref[...].astype(F32)
    pieces = [stack[m] for m in range(4)]
    plain = jnp.concatenate([p[:block] for p in pieces], axis=0)
    last = [p[block:] for p in pieces]
    turned = jnp.concatenate(
        [p[:, i * ROPE_DIM : (i + 1) * ROPE_DIM] for p in last for i in range(steps)], axis=0
    )
    cache = jnp.concatenate([plain, turned], axis=1).astype(BF16)
    first = steps * ROPE_DIM
    down = jnp.concatenate([p[:, first : first + down_cols] for p in last], axis=1)
    compressed = (down * unit(down)).astype(BF16)
    end_angles = jnp.concatenate([angles[pl.ds(e, 1), :] for e in ends], axis=0)
    seen = lax.broadcasted_iota(jnp.int32, (count, 4 * block), 1) <= column(ends)
    out[...] = attend_rows(compressed, cache, seen, end_angles, w_query, w_keys, w_values)


def final_kernel(mixed, w_out, out0, out1, out2, out3, total):
    tp = lax.axis_index("tp")
    width = out0.shape[1]
    total[...] = dot(mixed[...], w_out[...])
    for k, out in enumerate((out0, out1, out2, out3)):
        columns = pl.ds(pl.multiple_of((tp ^ k) * width, 128), width)
        out[...] = total[:, columns].astype(BF16)


def local_two(prompt, block_sizes, w_query_down, w_query, w_latent, w_keys, w_values, w_out):
    section = lax.axis_index("section")
    tokens, share = prompt.shape
    block = tokens // 4
    count = block_sizes.shape[0]
    w_down, w_up, w_lat = w_query_down[0].T, w_query[0], w_latent[0].T
    w_key, w_value, w_final = w_keys[0], w_values[0], w_out[0]
    down_cols, latent_cols = w_down.shape[0], w_lat.shape[0]
    model = 4 * share
    frequency = 10000.0 ** (-2.0 * np.arange(HALF, dtype=np.float32) / ROPE_DIM)
    angles = np.arange(tokens, dtype=np.float32)[:, None] * frequency.astype(np.float32)[None, :]
    angles = jnp.asarray(np.concatenate([np.cos(angles), np.sin(angles)], axis=1), F32)

    def route(array, *ways):
        pairs = []
        for s, way in enumerate(ways):
            if way:
                to, k, r = (*way, 0)[:3]
                pairs += [
                    ((s * 4 + i) * 4 + j, (to * 4 + (i ^ k)) * 4 + (j ^ r)) for i in range(4) for j in range(4)
                ]
        return lax.ppermute(array, ("section", "tp", "rep"), pairs)

    def within(array, k):
        return route(array, (0, k), (1, k))

    def onward(array, k):
        return route(array, (1, k), (0, 0))

    def over_rep(array, k):
        return lax.ppermute(array, "rep", [(i, i ^ k) for i in range(4)])

    sent = call(
        send_kernel,
        jax.ShapeDtypeStruct((tokens, share), BF16),
        [prompt, w_lat],
        grant=8,
        flops=2 * 10**10,
    )
    two = route(prompt, (0, 2), (1, 0, 1))
    three = route(prompt, (1, 0), (0, 3))
    one = route(sent, (0, 1), (1, 1))
    parts = call(
        down_kernel,
        jax.ShapeDtypeStruct((tokens + tokens // 3, 256), BF16),
        [prompt, three, two, one, w_down, w_lat],
        flops=2 * 10**10,
    )
    pieces = [parts] + [within(parts, k) for k in (1, 2, 3)]

    message = jax.ShapeDtypeStruct((block + count, model), BF16)
    *blocks, first_cache, passed, rest = call(
        layer_kernel,
        [message] * 4
        + [
            jax.ShapeDtypeStruct((block, ROW_WIDTH), BF16),
            jax.ShapeDtypeStruct((2, latent_cols, model // 2 - 384), BF16),
            jax.ShapeDtypeStruct((3, latent_cols, 384), BF16),
        ],
        [block_sizes, pieces[0], pieces[2], pieces[1], pieces[3], one, w_lat, prompt, angles, w_up, w_key, w_value, w_final],
        [
            pltpu.VMEM((4, *parts.shape), BF16),
            pltpu.VMEM((tokens + count, model), F32),
            pltpu.VMEM((tokens, ROW_WIDTH), BF16),
        ],
        flops=2 * tokens * (w_up.size + w_key.size + w_value.size + w_final.size),
        scalars=1,
        grant=16,
    )
    arrived = [onward(blocks[k], k) for k in (2, 1, 3, 0)]
    relayed = route(passed, None, (1, 2))
    relayed, late, first = lax.optimization_barrier((relayed, rest, passed[1]))
    weights = [first, relayed[0], relayed[1], late]
    weights += [over_rep(w, 1) for w in weights]
    fresh, last_cache, ends_share = call(
        latent_kernel,
        [
            jax.ShapeDtypeStruct((block + count, LATENT), BF16),
            jax.ShapeDtypeStruct((block, ROW_WIDTH), BF16),
            jax.ShapeDtypeStruct((count, share), BF16),
        ],
        [*arrived, angles, w_lat, *weights, w_down],
        [pltpu.VMEM((block + count, model), F32), pltpu.VMEM((4, block, latent_cols), F32)],
        flops=2 * 10**11,
    )
    pieces = [fresh] + [within(fresh, k) for k in (3, 2, 1)]
    first_ends = onward(ends_share, 0)
    mixed = call(
        ends_kernel,
        jax.ShapeDtypeStruct((count, w_final.shape[0]), BF16),
        [block_sizes, *pieces, angles, w_up, w_key, w_value],
        [pltpu.VMEM((4, block + count, LATENT), F32)],
        flops=2 * 10**10,
        scalars=1,
    )
    outs = call(
        final_kernel,
        [jax.ShapeDtypeStruct((count, share), BF16)] * 4,
        [mixed, w_final],
        [pltpu.VMEM((count, model), F32)],
        flops=10**8,
    )
    total = ends_share.astype(F32) + outs[0].astype(F32)
    for k in (1, 2, 3):
        total = total + within(outs[k], k).astype(F32)
    own_ends = jnp.where(section == 0, first_ends, total.astype(BF16))
    own_cache = jnp.where(section == 0, first_cache, last_cache)
    return (own_cache[None], own_ends[None])


def solution(mesh):
    sizes = [mesh.shape[a] for a in ("section", "tp", "rep")]
    body = local_two if sizes == [2, 4, 4] else local
    in_specs = (
        P("rep", "tp"),
        P("rep"),
        P("section", None, "tp"),
        P("section", None, "tp"),
        P("section", None, "tp"),
        P("section", None, "tp"),
        P("section", None, "tp"),
        P("section", "tp", None),
    )
    out_specs = (P("section", ("rep", "tp"), None), P("section", "rep", "tp"))
    return jax.shard_map(body, mesh=mesh, in_specs=in_specs, out_specs=out_specs, check_vma=False)
```

```python
import jax
import jax.numpy as jnp
import numpy as np
from jax import lax
from jax.experimental import pallas as pl
from jax.experimental.pallas import tpu as pltpu
from jax.sharding import PartitionSpec as P

NOPE_DIM = 128
ROPE_DIM = 32
VALUE_DIM = 128
LATENT = 512
EPSILON = 1e-06
F32 = jnp.float32
BF16 = jnp.bfloat16


def rms_rows(values):
    return values * lax.rsqrt(jnp.mean(values * values, axis=-1, keepdims=True) + EPSILON)


def rotate(values, positions):
    half_width = values.shape[-1] // 2
    frequency = 10000.0 ** (-2.0 * jnp.arange(half_width, dtype=F32) / values.shape[-1])
    angles = positions.astype(F32)[:, None] * frequency[None, :]
    if values.ndim == 3:
        angles = angles[:, None, :]
    cosine = jnp.cos(angles)
    sine_part = jnp.sin(angles)
    first_half = values[..., :half_width]
    second = values[..., half_width:]
    return jnp.concatenate(
        [first_half * cosine - second * sine_part, first_half * sine_part + second * cosine],
        axis=-1,
    )


def dot(a, b):
    return jnp.dot(a, b, preferred_element_type=F32)


def local(prompt, block_sizes, w_query_down, w_query, w_latent, w_keys, w_values, w_out):
    sections = lax.axis_size("section")
    section_id = lax.axis_index("section")
    tp_id = lax.axis_index("tp")
    tp_count = lax.axis_size("tp")
    tokens, share_cols = prompt.shape
    share_rows = tokens // tp_count
    down_weight, query_weight, latent_weight = w_query_down[0], w_query[0], w_latent[0]
    key_weight, value_weight, out_weight = w_keys[0], w_values[0], w_out[0]
    down_cols, latent_cols = down_weight.shape[1], latent_weight.shape[1]
    head_count = query_weight.shape[1] // (NOPE_DIM + ROPE_DIM)
    scale_factor = (NOPE_DIM + ROPE_DIM) ** (-0.5)
    all_positions = jnp.arange(tokens, dtype=jnp.int32)
    end_rows = jnp.cumsum(block_sizes) - 1

    def shift(array, distance, routes):
        pairs = [
            (a * tp_count + i, b * tp_count + (i + distance) % tp_count)
            for a, b in routes
            for i in range(tp_count)
        ]
        return lax.ppermute(array, ("section", "tp"), pairs)

    def gather(array, where, axis):
        routes = [(s, s) for s in where]
        width = array.shape[axis]
        shape = list(array.shape)
        shape[axis] = width * tp_count
        whole = jnp.zeros(shape, array.dtype)
        for k in range(tp_count):
            piece = array if k == 0 else shift(array, k, routes)
            whole = lax.dynamic_update_slice_in_dim(
                whole, piece, lax.rem(tp_id - k + tp_count, tp_count) * width, axis
            )
        return whole

    def keys_and_values(cache):
        plain = cache[:, :LATENT]
        keys = dot(plain, key_weight).astype(BF16).reshape(tokens, head_count, NOPE_DIM)
        values = dot(plain, value_weight).astype(BF16).reshape(tokens, head_count, VALUE_DIM)
        return keys, values

    def attend(compressed, positions, cache):
        keys, values = keys_and_values(cache)
        rows = compressed.shape[0]
        queries = dot(compressed, query_weight).reshape(rows, head_count, NOPE_DIM + ROPE_DIM)
        queries = jnp.concatenate(
            [queries[..., :NOPE_DIM], rotate(queries[..., NOPE_DIM:], positions)], axis=-1
        ).astype(BF16)
        scores = jnp.einsum("ihd,jhd->hij", queries[..., :NOPE_DIM], keys, preferred_element_type=F32)
        scores = scores + jnp.einsum(
            "ihr,jr->hij", queries[..., NOPE_DIM:], cache[:, LATENT:], preferred_element_type=F32
        )
        visible = all_positions[None, :] <= positions[:, None]
        powered = jnp.where(visible[None], jnp.exp(scores * scale_factor), 0.0)
        attention = (powered / jnp.sum(powered, axis=-1, keepdims=True)).astype(BF16)
        mixed = jnp.einsum("hij,jhv->ihv", attention, values, preferred_element_type=F32)
        return dot(mixed.astype(BF16).reshape(rows, head_count * VALUE_DIM), out_weight)

    def layer(hidden, own_share, tick):
        normed = rms_rows(hidden.astype(F32)).astype(BF16)
        parts = jnp.concatenate(
            [dot(normed, down_weight).astype(BF16), dot(normed, latent_weight).astype(BF16)], axis=1
        )
        whole = gather(parts[None], [tick], 0).astype(F32)
        down = jnp.concatenate([whole[m, :, :down_cols] for m in range(tp_count)], axis=1)
        latent = jnp.concatenate([whole[m, :, down_cols:] for m in range(tp_count)], axis=1)
        compressed = rms_rows(down).astype(BF16)
        cache = jnp.concatenate(
            [rms_rows(latent[:, :LATENT]), rotate(latent[:, LATENT:], all_positions)], axis=-1
        ).astype(BF16)
        partial = attend(compressed, all_positions, cache)
        start = tp_id * share_cols
        mine = lax.dynamic_slice_in_dim(partial, start, share_cols, 1) + own_share.astype(F32)
        partial = lax.dynamic_update_slice_in_dim(partial, mine, start, 1).astype(BF16)
        return partial, cache

    def pass_on(partial, tick):
        ends = jnp.take(partial, end_rows, axis=0)
        total = 0.0
        for k in range(tp_count):
            first = lax.rem(tp_id + k, tp_count) * share_rows
            block = lax.dynamic_slice_in_dim(partial, first, share_rows, 0)
            block = jnp.concatenate([block, ends], axis=0)
            total = total + shift(block, k, [(tick, tick + 1)]).astype(F32)
        total = total.astype(BF16)
        return total[:share_rows], total[share_rows:]

    own_cache = jnp.zeros((share_rows, LATENT + ROPE_DIM), BF16)
    own_ends = jnp.zeros((block_sizes.shape[0], share_cols), BF16)
    last = sections - 1
    latent_whole = gather(latent_weight, range(1, sections), 1) if last else latent_weight
    hidden, own_share = gather(prompt, [0], 1), prompt
    for tick in range(last):
        partial, cache = layer(hidden, own_share, tick)
        mine = lax.dynamic_slice_in_dim(cache, tp_id * share_rows, share_rows, 0)
        own_cache = jnp.where(section_id == tick, mine, own_cache)
        rows, ends = pass_on(partial, tick)
        ends_share = lax.dynamic_slice_in_dim(ends, tp_id * share_cols, share_cols, 1)
        own_ends = jnp.where(section_id == tick, shift(ends_share, 0, [(tick + 1, tick)]), own_ends)
        if tick + 1 < last:
            hidden = gather(rows, [tick + 1], 0)
            own_share = lax.dynamic_slice_in_dim(hidden, tp_id * share_cols, share_cols, 1)

    row_positions = tp_id * share_rows + jnp.arange(share_rows, dtype=jnp.int32)
    latent = dot(rms_rows(rows.astype(F32)).astype(BF16), latent_whole)
    fresh = jnp.concatenate(
        [rms_rows(latent[:, :LATENT]), rotate(latent[:, LATENT:], row_positions)], axis=-1
    ).astype(BF16)
    own_cache = jnp.where(section_id == last, fresh, own_cache)
    down = dot(rms_rows(ends.astype(F32)).astype(BF16), down_weight).astype(BF16)
    down = jnp.pad(down, ((0, 0), (0, fresh.shape[1] - down_cols)))
    whole = gather(jnp.concatenate([fresh, down], axis=0)[None], [last], 0)
    cache = whole[:, :share_rows].reshape(tokens, LATENT + ROPE_DIM)
    down = jnp.concatenate([whole[m, share_rows:, :down_cols] for m in range(tp_count)], axis=1)
    compressed = rms_rows(down.astype(F32)).astype(BF16)
    partial = attend(compressed, end_rows, cache).astype(BF16)
    total = ends_share.astype(F32)
    for k in range(tp_count):
        start = lax.rem(tp_id + k, tp_count) * share_cols
        block = lax.dynamic_slice_in_dim(partial, start, share_cols, 1)
        total = total + (shift(block, k, [(last, last)]) if k else block).astype(F32)
    own_ends = jnp.where(section_id == last, total.astype(BF16), own_ends)
    return (own_cache[None], own_ends[None])


ROW_WIDTH = LATENT + ROPE_DIM
HEAD_WIDTH = NOPE_DIM + ROPE_DIM
HALF = ROPE_DIM // 2
SMEM = pl.BlockSpec(memory_space=pltpu.SMEM)
VMEM = pl.BlockSpec(memory_space=pltpu.VMEM)


def call(kernel, out_shape, args, scratch=(), flops=0, scalars=0, grant=8):
    many = isinstance(out_shape, list)
    moved = sum(a.size * a.dtype.itemsize for a in args)
    return pl.pallas_call(
        kernel,
        out_shape=out_shape,
        in_specs=[SMEM] * scalars + [VMEM] * (len(args) - scalars),
        out_specs=[VMEM] * len(out_shape) if many else VMEM,
        scratch_shapes=list(scratch),
        compiler_params=pltpu.CompilerParams(vmem_limit_bytes=grant * 2**20),
        cost_estimate=pl.CostEstimate(flops=flops, bytes_accessed=moved, transcendentals=0),
    )(*args)


def dot_t(a, b):
    return lax.dot_general(a, b, (((1,), (1,)), ((), ())), preferred_element_type=F32)


def unit(values):
    return lax.rsqrt(jnp.mean(values * values, axis=-1, keepdims=True) + EPSILON)


def turn(pair, angles):
    cosine, sine = angles[:, :HALF], angles[:, HALF:]
    a, b = pair[:, :HALF], pair[:, HALF:]
    return jnp.concatenate([a * cosine - b * sine, a * sine + b * cosine], axis=1)


def end_rows(sizes):
    ends = [sizes[0] - 1]
    for i in range(1, sizes.shape[0]):
        ends.append(ends[-1] + sizes[i])
    return ends


def column(scalars):
    rows = lax.broadcasted_iota(jnp.int32, (len(scalars), 1), 0)
    out = jnp.zeros((len(scalars), 1), jnp.int32)
    for i, value in enumerate(scalars):
        out = jnp.where(rows == i, value, out)
    return out


def send_kernel(prompt, w_latent, out):
    section, rep = lax.axis_index("section"), lax.axis_index("rep")
    rows, width = out.shape
    cols, model = w_latent.shape

    @pl.when(section == 0)
    def _():
        out[...] = prompt[...]

    @pl.when(section != 0)
    def _():
        first = (rep & 1) * (model // 2)
        half = w_latent[:, pl.ds(pl.multiple_of(first, 128), width + 256)].astype(F32)
        extra = half[:, width:]
        free = rows - cols
        left = cols - 2 * free
        tail = [extra[2 * free :, :128], extra[2 * free :, 128:], jnp.zeros((free - 2 * left, 128), F32)]
        extra = jnp.concatenate(
            [extra[:free], extra[free : 2 * free], jnp.concatenate(tail, axis=0)], axis=1
        )
        out[...] = jnp.concatenate([half[:, :width], extra], axis=0).astype(BF16)


def unpack_share(share, cols):
    share = share.astype(F32)
    free = share.shape[0] - cols
    left = cols - 2 * free
    extra, tail = share[cols:, :512], share[cols:, 512:]
    tail = jnp.concatenate([tail[:left], tail[left : 2 * left]], axis=1)
    extra = jnp.concatenate([extra[:, :256], extra[:, 256:], tail], axis=0)
    return jnp.concatenate([share[:cols], extra], axis=1).astype(BF16)


def down_kernel(own, three, two, one, w_down, w_latent, out):
    section, tp, rep = (lax.axis_index(a) for a in ("section", "tp", "rep"))
    tokens, share = own.shape
    cols, model = w_latent.shape
    third = tokens // 3

    @pl.when(section == 0)
    def _():
        squares, down, latent = 0.0, 0.0, 0.0
        for k, ref in enumerate((own, one, two, three)):
            columns = pl.ds(pl.multiple_of((tp ^ k) * share, 128), share)
            piece = ref[...]
            wide = piece.astype(F32)
            squares = squares + jnp.sum(wide * wide, axis=1, keepdims=True)
            down = down + dot_t(piece, w_down[:, columns])
            latent = latent + dot_t(piece, w_latent[:, columns])
        scale = lax.rsqrt(squares / model + EPSILON)
        parts = jnp.concatenate([down * scale, latent * scale], axis=1)
        rest = parts[:, 256:]
        rest = [rest[i * third : (i + 1) * third] for i in range(3)]
        rest.append(jnp.zeros((third, 256 - 3 * rest[0].shape[1]), F32))
        out[...] = jnp.concatenate([parts[:, :256], jnp.concatenate(rest, axis=1)], axis=0).astype(BF16)

    @pl.when(section != 0)
    def _():
        first = ((rep & 1) + 1) * (model // 2) - 384
        mine = w_latent[:, pl.ds(pl.multiple_of(first, 128), 384)].astype(F32)
        rest = mine[:, 256:]
        high = cols // 2 + 4
        lower = jnp.concatenate([rest[high:], jnp.zeros((2 * high - cols, 128), F32)], axis=0)
        rest = jnp.concatenate([rest[:high], lower], axis=1)
        blank = jnp.zeros((out.shape[0] - cols - high, 256), F32)
        out[...] = jnp.concatenate([mine[:, :256], rest, blank], axis=0).astype(BF16)


def unpack_rest(piece, cols):
    piece = piece.astype(F32)
    high = cols // 2 + 4
    rest = piece[cols : cols + high]
    rest = jnp.concatenate([rest[:, :128], rest[: cols - high, 128:]], axis=0)
    return jnp.concatenate([piece[:cols], rest], axis=1).astype(BF16)


def unpack_parts(piece, tokens, width):
    piece = piece.astype(F32)
    rest, size = piece[tokens:], width - 256
    rest = jnp.concatenate([rest[:, i * size : (i + 1) * size] for i in range(3)], axis=0)
    return jnp.concatenate([piece[:tokens], rest], axis=1)


def attend_rows(compressed, cache, seen, angles, w_query, w_keys, w_values):
    plain, turned = cache[:, :LATENT], cache[:, LATENT:]
    keys = dot(plain, w_keys[...]).astype(BF16)
    values = dot(plain, w_values[...]).astype(BF16)
    queries = dot(compressed, w_query[...])
    mixed = []
    for head in range(queries.shape[1] // HEAD_WIDTH):
        query = queries[:, head * HEAD_WIDTH : (head + 1) * HEAD_WIDTH]
        query = jnp.concatenate(
            [query[:, :NOPE_DIM], turn(query[:, NOPE_DIM:], angles)], axis=1
        ).astype(BF16)
        key = jnp.concatenate([keys[:, head * NOPE_DIM : (head + 1) * NOPE_DIM], turned], axis=1)
        scores = dot_t(query, key) * HEAD_WIDTH**-0.5
        powered = jnp.where(seen, jnp.exp(scores), 0.0)
        attention = (powered / jnp.sum(powered, axis=1, keepdims=True)).astype(BF16)
        mixed.append(dot(attention, values[:, head * VALUE_DIM : (head + 1) * VALUE_DIM]))
    return jnp.concatenate(mixed, axis=1).astype(BF16)


def layer_kernel(
    sizes, own, two, one, three, share1, w_latent, prompt, angles,
    w_query, w_keys, w_values, w_out, out0, out1, out2, out3, own_cache, passed, rest, stack, total, cached,
):
    section, tp, rep = (lax.axis_index(a) for a in ("section", "tp", "rep"))
    tokens, width = prompt.shape
    block = tokens // 4
    cols, late = rest.shape[1:]
    down_cols = w_query.shape[0] // 4

    @pl.when(section != 0)
    def _():
        long = passed.shape[1] - share1.shape[1] - 256
        first = (rep & 1) * long
        passed[:, :long] = w_latent[:, pl.ds(pl.multiple_of(first, 128), long)]
        passed[:, long:] = unpack_share(share1[...], cols)
        rest[0] = unpack_rest(one[...], cols)
        rest[1] = unpack_rest(three[...], cols)

    @pl.when(section == 0)
    def _():
        ends = column(end_rows(sizes))
        for k, ref in enumerate((own, one, two, three)):
            stack[tp ^ k] = ref[...]
        pieces = [unpack_parts(stack[m], tokens, down_cols + cols) for m in range(4)]
        down = jnp.concatenate([p[:, :down_cols] for p in pieces], axis=1)
        latent = jnp.concatenate([p[:, down_cols:] for p in pieces], axis=1)
        compressed = (down * unit(down)).astype(BF16)
        plain = latent[:, :LATENT]
        cache = jnp.concatenate(
            [plain * unit(plain), turn(latent[:, LATENT:], angles[...])], axis=1
        ).astype(BF16)
        cached[...] = cache
        own_cache[...] = cached[pl.ds(pl.multiple_of(tp * block, block), block), :]
        seen = lax.broadcasted_iota(jnp.int32, (tokens, tokens), 0) >= lax.broadcasted_iota(
            jnp.int32, (tokens, tokens), 1
        )
        mixed = attend_rows(compressed, cache, seen, angles[...], w_query, w_keys, w_values)
        chosen = lax.broadcasted_iota(jnp.int32, (ends.shape[0], tokens), 1) == ends
        chosen = chosen.astype(BF16)
        rows = jnp.concatenate([mixed, dot(chosen, mixed).astype(BF16)], axis=0)
        total[...] = dot(rows, w_out[...])
        mine = pl.ds(pl.multiple_of(tp * width, 128), width)
        added = jnp.concatenate([prompt[...].astype(F32), dot(chosen, prompt[...])], axis=0)
        total[:, mine] += added
        last = total[tokens:, :]
        for k, out in enumerate((out0, out1, out2, out3)):
            part = total[pl.ds(pl.multiple_of((tp ^ k) * block, block), block), :]
            out[...] = jnp.concatenate([part, last], axis=0).astype(BF16)


def latent_kernel(
    one, two, three, four, angles, w_latent, first1, first2, first3, rest,
    near1, near2, near3, near_rest, w_down, out, own_cache, own_ends, hidden, parts,
):
    tp, rep = lax.axis_index("tp"), lax.axis_index("rep")
    block = angles.shape[0] // 4
    width = own_ends.shape[1]
    model = w_latent.shape[1]
    early = first1.shape[1]
    rows = one[...].astype(F32) + two[...].astype(F32) + three[...].astype(F32) + four[...].astype(F32)
    narrow = rows.astype(BF16)
    rows = narrow.astype(F32)
    hidden[...] = rows
    scale = unit(rows)
    parts[tp] = dot_t(narrow[:block], w_latent[...])
    sums = [0.0, 0.0, 0.0]
    for core, weights in enumerate(
        (
            (first1, first2, first3, rest),
            (near1, near2, near3, near_rest),
        )
    ):
        first = ((rep & 1) ^ core) * (model // 2)
        head = hidden[0:block, pl.ds(pl.multiple_of(first, 128), early)].astype(BF16)
        late = pl.ds(pl.multiple_of(first + early, 128), model // 2 - early)
        tail = hidden[0:block, late].astype(BF16)
        for k in range(3):
            sums[k] += dot_t(head, weights[k][...]) + dot_t(tail, weights[3][k])
    for k, value in enumerate(sums):
        parts[tp ^ (k + 1)] = value
    latent = jnp.concatenate([parts[m] for m in range(4)], axis=1) * scale[:block]
    plain = latent[:, :LATENT]
    plain = plain * unit(plain)
    own_angles = angles[pl.ds(pl.multiple_of(tp * block, block), block), :]
    turned = turn(latent[:, LATENT:], own_angles)
    own_cache[...] = jnp.concatenate([plain, turned], axis=1).astype(BF16)
    down = dot_t(narrow[block:, :], w_down[...]) * scale[block:]
    count = down.shape[0]
    turned = [turned[i * count : (i + 1) * count] for i in range(block // count)]
    last = jnp.concatenate([*turned, down], axis=1)
    last = jnp.concatenate([last, jnp.zeros((count, LATENT - last.shape[1]), F32)], axis=1)
    out[...] = jnp.concatenate([plain, last], axis=0).astype(BF16)
    mine = pl.ds(pl.multiple_of(tp * width, 128), width)
    own_ends[...] = hidden[block:, mine].astype(BF16)


def ends_kernel(
    sizes, own, three, two, one, angles, w_query, w_keys, w_values, out, stack
):
    tp = lax.axis_index("tp")
    ends = end_rows(sizes)
    count = len(ends)
    block = own.shape[0] - count
    steps = block // count
    down_cols = w_query.shape[0] // 4
    for k, ref in enumerate((own, one, two, three)):
        stack[tp ^ k] = ref[...].astype(F32)
    pieces = [stack[m] for m in range(4)]
    plain = jnp.concatenate([p[:block] for p in pieces], axis=0)
    last = [p[block:] for p in pieces]
    turned = jnp.concatenate(
        [p[:, i * ROPE_DIM : (i + 1) * ROPE_DIM] for p in last for i in range(steps)], axis=0
    )
    cache = jnp.concatenate([plain, turned], axis=1).astype(BF16)
    first = steps * ROPE_DIM
    down = jnp.concatenate([p[:, first : first + down_cols] for p in last], axis=1)
    compressed = (down * unit(down)).astype(BF16)
    end_angles = jnp.concatenate([angles[pl.ds(e, 1), :] for e in ends], axis=0)
    seen = lax.broadcasted_iota(jnp.int32, (count, 4 * block), 1) <= column(ends)
    out[...] = attend_rows(compressed, cache, seen, end_angles, w_query, w_keys, w_values)


def final_kernel(mixed, w_out, out0, out1, out2, out3, total):
    tp = lax.axis_index("tp")
    width = out0.shape[1]
    total[...] = dot(mixed[...], w_out[...])
    for k, out in enumerate((out0, out1, out2, out3)):
        columns = pl.ds(pl.multiple_of((tp ^ k) * width, 128), width)
        out[...] = total[:, columns].astype(BF16)


def local_two(prompt, block_sizes, w_query_down, w_query, w_latent, w_keys, w_values, w_out):
    section = lax.axis_index("section")
    tokens, share = prompt.shape
    block = tokens // 4
    count = block_sizes.shape[0]
    w_down, w_up, w_lat = w_query_down[0].T, w_query[0], w_latent[0].T
    w_key, w_value, w_final = w_keys[0], w_values[0], w_out[0]
    down_cols, latent_cols = w_down.shape[0], w_lat.shape[0]
    model = 4 * share
    frequency = 10000.0 ** (-2.0 * np.arange(HALF, dtype=np.float32) / ROPE_DIM)
    angles = np.arange(tokens, dtype=np.float32)[:, None] * frequency.astype(np.float32)[None, :]
    angles = jnp.asarray(np.concatenate([np.cos(angles), np.sin(angles)], axis=1), F32)

    def route(array, *ways):
        pairs = []
        for s, way in enumerate(ways):
            if way:
                to, k, r = (*way, 0)[:3]
                pairs += [
                    ((s * 4 + i) * 4 + j, (to * 4 + (i ^ k)) * 4 + (j ^ r)) for i in range(4) for j in range(4)
                ]
        return lax.ppermute(array, ("section", "tp", "rep"), pairs)

    def within(array, k):
        return route(array, (0, k), (1, k))

    def onward(array, k, back=True):
        return route(array, (1, k), (0, 0) if back else None)

    def over_rep(array, k):
        return lax.ppermute(array, "rep", [(i, i ^ k) for i in range(4)])

    sent = call(
        send_kernel,
        jax.ShapeDtypeStruct((tokens, share), BF16),
        [prompt, w_lat],
        grant=57,
        flops=2 * 10**10,
    )
    two = route(prompt, (0, 2), (1, 0, 1))
    three = route(prompt, (1, 0), (0, 3))
    one = route(sent, (0, 1), (1, 1))
    parts = call(
        down_kernel,
        jax.ShapeDtypeStruct((tokens + tokens // 3, 256), BF16),
        [prompt, three, two, one, w_down, w_lat],
        flops=2 * 10**10,
    )
    pieces = [parts, within(parts, 1), route(parts, (0, 2), (1, 0, 1)), within(parts, 3)]

    message = jax.ShapeDtypeStruct((block + count, model), BF16)
    *blocks, first_cache, passed, rest = call(
        layer_kernel,
        [message] * 4
        + [
            jax.ShapeDtypeStruct((block, ROW_WIDTH), BF16),
            jax.ShapeDtypeStruct((latent_cols, model - 384), BF16),
            jax.ShapeDtypeStruct((2, latent_cols, 384), BF16),
        ],
        [block_sizes, pieces[0], pieces[2], pieces[1], pieces[3], one, w_lat, prompt, angles, w_up, w_key, w_value, w_final],
        [
            pltpu.VMEM((4, *parts.shape), BF16),
            pltpu.VMEM((tokens + count, model), F32),
            pltpu.VMEM((tokens, ROW_WIDTH), BF16),
        ],
        flops=2 * tokens * (w_up.size + w_key.size + w_value.size + w_final.size),
        scalars=1,
        grant=16,
    )
    arrived = [onward(blocks[k], k, k in (1, 2)) for k in (2, 1, 3, 0)]
    relayed = route(passed, None, (1, 2))
    relayed, rest, beside = lax.optimization_barrier((relayed, rest, passed[:, model // 2 :]))
    early = model // 2 - 384
    late = jnp.stack([rest[0], relayed[:, early : model // 2], rest[1]])
    weights = [beside, relayed[:, :early], relayed[:, model // 2 :], late]
    weights += [over_rep(w, 1) for w in weights]
    fresh, last_cache, ends_share = call(
        latent_kernel,
        [
            jax.ShapeDtypeStruct((block + count, LATENT), BF16),
            jax.ShapeDtypeStruct((block, ROW_WIDTH), BF16),
            jax.ShapeDtypeStruct((count, share), BF16),
        ],
        [*arrived, angles, w_lat, *weights, w_down],
        [pltpu.VMEM((block + count, model), F32), pltpu.VMEM((4, block, latent_cols), F32)],
        flops=2 * 10**11,
    )
    pieces = [fresh] + [within(fresh, k) for k in (3, 2, 1)]
    first_ends = onward(ends_share, 0)
    mixed = call(
        ends_kernel,
        jax.ShapeDtypeStruct((count, w_final.shape[0]), BF16),
        [block_sizes, *pieces, angles, w_up, w_key, w_value],
        [pltpu.VMEM((4, block + count, LATENT), F32)],
        flops=2 * 10**10,
        scalars=1,
    )
    outs = call(
        final_kernel,
        [jax.ShapeDtypeStruct((count, share), BF16)] * 4,
        [mixed, w_final],
        [pltpu.VMEM((count, model), F32)],
        flops=10**8,
    )
    total = ends_share.astype(F32) + outs[0].astype(F32)
    for k in (1, 2, 3):
        total = total + within(outs[k], k).astype(F32)
    own_ends = jnp.where(section == 0, first_ends, total.astype(BF16))
    own_cache = jnp.where(section == 0, first_cache, last_cache)
    return (own_cache[None], own_ends[None])


def solution(mesh):
    sizes = [mesh.shape[a] for a in ("section", "tp", "rep")]
    body = local_two if sizes == [2, 4, 4] else local
    in_specs = (
        P("rep", "tp"),
        P("rep"),
        P("section", None, "tp"),
        P("section", None, "tp"),
        P("section", None, "tp"),
        P("section", None, "tp"),
        P("section", None, "tp"),
        P("section", "tp", None),
    )
    out_specs = (P("section", ("rep", "tp"), None), P("section", "rep", "tp"))
    return jax.shard_map(body, mesh=mesh, in_specs=in_specs, out_specs=out_specs, check_vma=False)
```
